512 devices in a mesh: dp: 4 (over z_hi), outer: 16 (over z_lo, y), inner: 8 (over x, core).
Axes of the slice: x: 4, y: 8, z: 8 (z_hi: 4, z_lo: 2; z = z_hi * 2 + z_lo), core: 2. Of those that a mesh axis runs over, the one named last changes fastest.
Arguments:
- queries: bfloat16 [4, 24576, 1024], P('dp', ('outer', 'inner')), may hold values from -6 to 6
- inputs: bfloat16 [4, 24576, 1024], P('dp', ('outer', 'inner')), may hold values from -24 to 24
- kv_weight: bfloat16 [1024, 512], replicated, may hold values from -0.1875 to 0.1875
- grad_out: bfloat16 [4, 24576, 1024], P('dp', ('outer', 'inner')), may hold values from -6 to 6
- segment_ids: int32 [4, 24576], P('dp', ('outer', 'inner')), may hold values from 0 to 63, never falling along the last dimension, each value on 1 to 768 neighbouring positions
Outputs:
- grad_queries: bfloat16 [4, 24576, 1024], P('dp', ('outer', 'inner'))
- grad_inputs: bfloat16 [4, 24576, 1024], P('dp', ('outer', 'inner'))
- grad_weight: float32 [1024, 512], P(('outer', 'inner'))
The draws below stay inside these ranges and needn't reach their ends.
Inputs may be any that keep to these rules, and one draw needn't show every extreme that they name: `segment_ids`: along each replica's row the volume numbers never fall; every volume has 1 to 768 tokens, and some volume has exactly 768.
All inputs are finite; a program needn't handle non-finite values.
Results may differ from the reference program's by a relative error of at most 0.011.
Values may be sent and summed in bfloat16 or wider, within the bound.
A program may use at most 64 MiB of HBM per device.

```python
import math
import jax
import jax.numpy as jnp
import numpy as np
from jax import lax

D = 1024
HEADS = 8
KV_HEADS = 2
HEAD = 128
REACH = 4
TOK_DEV = 192
TOKENS = 24576
LMAX = 768
VOLUMES = 64
REPLICAS = 4
N_DP = 4


def with_spikes(values, stream_key, source, target, parts, factor):
    def block_of(axis_at):
        return (jnp.arange(values.shape[axis_at]) // (values.shape[axis_at] // parts)).reshape((-1,) + (1,) * (values.ndim - 1 - axis_at))

    one_side = jax.random.permutation(stream_key, parts)[block_of(target)]
    far = (block_of(target) + parts // 2) % parts
    return jnp.where((block_of(source) == one_side) | (block_of(source) == far), factor * values, values)


def steps_of(key, dims, split, smallest, top_value):
    gain = 1.0
    for axis_at, blocks in split:
        steps = jax.random.uniform(jax.random.fold_in(jax.random.fold_in(key, 6), axis_at), (blocks,), jnp.float32, smallest / len(split), top_value / len(split))
        gain = gain * jnp.repeat(jnp.exp(steps), dims[axis_at] // blocks).reshape((-1,) + (1,) * (len(dims) - 1 - axis_at))
    return gain


def length_profile(count, total, limit, lean):
    loads = [(1 << 20) // math.isqrt(grade ** lean) + 1 for grade in range(2, count + 1)]
    surplus, counts = total - limit - (count - 1), [1] * (count - 1)
    while surplus > 0:
        candidates = [i for i in range(count - 1) if counts[i] < limit]
        pool, budget = sum([loads[i] for i in candidates]), surplus
        for i in candidates:
            addition = min(limit - counts[i], max(1, budget * loads[i] // pool), surplus)
            counts[i] = counts[i] + addition
            surplus = surplus - addition
    return np.array([limit] + counts)


def ragged_sizes(key, number_of, total, bound, skew):
    if number_of == 2:
        one = jax.random.randint(key, (), max(1, total - bound), min(bound, total - 1) + 1)
        return jnp.stack([one, total - one])
    sizes = jnp.asarray(length_profile(number_of, total, bound, skew), jnp.int32)
    twos = (number_of - 1) // 2
    source_of, sink = sizes[1:1 + 2 * twos:2], sizes[2:2 + 2 * twos:2]
    room = jnp.minimum(source_of - 1, bound - sink)
    passed = jax.random.randint(jax.random.fold_in(key, 1), (twos,), 0, 1 << 20) % (room + 1)
    sizes = sizes.at[1:1 + 2 * twos:2].set(source_of - passed).at[2:2 + 2 * twos:2].set(sink + passed)
    return sizes[jax.random.permutation(jax.random.fold_in(key, 2), number_of)]


def gaussian(rng, shape, deviation, bound, cuts=(), kind=jnp.bfloat16):
    level = steps_of(rng, shape, cuts, -0.22, 0.18) if cuts else 1.0
    values = jax.random.normal(rng, shape, jnp.float32) * deviation * level
    return jnp.minimum(jnp.maximum(values, -bound), bound).astype(kind)


def heavy_noise(own_key, shape, width, limit, pieces, heavy, held_as=jnp.bfloat16):
    result = width * jax.random.normal(own_key, shape, jnp.float32)
    if pieces:
        result = result * steps_of(own_key, shape, pieces, -0.22, 0.18)
    return jnp.clip(with_spikes(result, jax.random.fold_in(own_key, 3), *heavy), -limit, limit).astype(held_as)


def setup_inputs(seed: int = 0) -> dict:
    streams_of = jax.random.split(jax.random.key(seed), 6)
    return {
        "queries": gaussian(streams_of[0], (REPLICAS, TOKENS, HEADS * HEAD), 1.0, 6.0, ((0, 4), (1, 128))),
        "inputs": heavy_noise(streams_of[1], (REPLICAS, TOKENS, D), 1.0, 24.0, ((0, 4), (1, 128)), (1, 2, 128, 5.5)),
        "kv_weight": gaussian(streams_of[2], (D, 2 * KV_HEADS * HEAD), D ** -0.5, 0.1875),
        "grad_out": gaussian(streams_of[3], (REPLICAS, TOKENS, HEADS * HEAD), 1.0, 6.0, ((0, 4), (1, 128))),
        "segment_ids": jax.vmap(lambda own: jnp.searchsorted(jnp.cumsum(ragged_sizes(own, VOLUMES, TOKENS, LMAX, 0)), jnp.arange(TOKENS), side="right"))(jax.random.split(streams_of[4], REPLICAS)).reshape((REPLICAS, TOKENS)).astype(jnp.int32),
    }


def attend(query_rows, upstream, window, volume_here, volume_window):
    factor = HEAD ** -0.5
    per_group = HEADS // KV_HEADS
    query_count = query_rows.shape[0]
    allowed = volume_here[:, None] == volume_window[None, :]
    allowed = jnp.repeat(allowed, per_group, axis=0)
    grad_query_parts = []
    key_parts = []
    value_parts = []
    for group in range(KV_HEADS):
        lo_col = group * per_group * HEAD
        hi_col = (group + 1) * per_group * HEAD
        query_group = query_rows[:, lo_col:hi_col].reshape(query_count * per_group, HEAD)
        upstream_group = upstream[:, lo_col:hi_col].reshape(query_count * per_group, HEAD)
        keys = window[:, group * HEAD:(group + 1) * HEAD]
        values = window[:, (KV_HEADS + group) * HEAD:(KV_HEADS + group + 1) * HEAD]
        scores = jnp.dot(query_group, keys.T, preferred_element_type=jnp.float32) * factor
        scores = jnp.where(allowed, scores, -1e30)
        peak = jnp.max(scores, axis=1, keepdims=True)
        log_total = peak + jnp.log(jnp.sum(jnp.exp(scores - peak), axis=1, keepdims=True))
        probs = jnp.exp(scores - log_total)
        probs_low = probs.astype(jnp.bfloat16)
        output = jnp.dot(probs_low, values, preferred_element_type=jnp.float32)
        dot_term = jnp.sum(upstream_group.astype(jnp.float32) * output, axis=1, keepdims=True)
        grad_probs = jnp.dot(upstream_group, values.T, preferred_element_type=jnp.float32)
        grad_scores = (probs * (grad_probs - dot_term) * factor).astype(jnp.bfloat16)
        grad_query = jnp.dot(grad_scores, keys, preferred_element_type=jnp.float32)
        grad_query_parts.append(grad_query.reshape(query_count, per_group * HEAD))
        key_parts.append(jnp.dot(grad_scores.T, query_group, preferred_element_type=jnp.float32))
        value_parts.append(jnp.dot(probs_low.T, upstream_group, preferred_element_type=jnp.float32))
    return jnp.concatenate(grad_query_parts, axis=1), jnp.concatenate(key_parts + value_parts, axis=1)


def reference(queries, inputs, kv_weight, grad_out, segment_ids):
    margin = REACH * TOK_DEV
    block_count = TOKENS // TOK_DEV
    window_len = (2 * REACH + 1) * TOK_DEV
    kv_cols = 2 * KV_HEADS * HEAD
    grad_query_all = []
    grad_input_all = []
    grad_weight = jnp.zeros((D, kv_cols), jnp.float32)
    for replica in range(N_DP):
        key_value = jnp.dot(inputs[replica], kv_weight, preferred_element_type=jnp.float32).astype(jnp.bfloat16)
        volumes = (segment_ids[replica] + 1).astype(jnp.int32)
        padded_kv = jnp.pad(key_value, ((margin, margin), (0, 0)))
        padded_volumes = jnp.pad(volumes, (margin, margin))
        query_all = queries[replica]
        upstream_all = grad_out[replica]

        def visit_block(accumulated, block):
            start = (block * TOK_DEV).astype(jnp.int32)
            query_rows = lax.dynamic_slice_in_dim(query_all, start, TOK_DEV, 0)
            upstream = lax.dynamic_slice_in_dim(upstream_all, start, TOK_DEV, 0)
            volume_here = lax.dynamic_slice_in_dim(volumes, start, TOK_DEV, 0)
            window = lax.dynamic_slice_in_dim(padded_kv, start, window_len, 0)
            volume_window = lax.dynamic_slice_in_dim(padded_volumes, start, window_len, 0)
            grad_query, grad_window = attend(query_rows, upstream, window, volume_here, volume_window)
            parcel = lax.optimization_barrier(grad_window.astype(jnp.bfloat16)).astype(jnp.float32)
            current = lax.dynamic_slice_in_dim(accumulated, start, window_len, 0)
            accumulated = lax.dynamic_update_slice_in_dim(accumulated, current + parcel, start, 0)
            return accumulated, grad_query.astype(jnp.bfloat16)

        start_acc = jnp.zeros((TOKENS + 2 * margin, kv_cols), jnp.float32)
        accumulated, grad_queries = lax.scan(visit_block, start_acc, jnp.arange(block_count, dtype=jnp.int32))
        grad_kv = accumulated[margin:margin + TOKENS].astype(jnp.bfloat16)
        grad_query_all.append(grad_queries.reshape(TOKENS, HEADS * HEAD))
        grad_input_all.append(jnp.dot(grad_kv, kv_weight.T, preferred_element_type=jnp.float32).astype(jnp.bfloat16))
        grad_weight = grad_weight + jnp.dot(inputs[replica].T, grad_kv, preferred_element_type=jnp.float32)
    return jnp.stack(grad_query_all), jnp.stack(grad_input_all), grad_weight
```

```python
import functools

import jax
import jax.numpy as jnp
from jax import lax
from jax.experimental import pallas as pl
from jax.experimental.pallas import tpu as pltpu
from jax.sharding import PartitionSpec as P

MESH = pl.DeviceIdType.MESH

HEADS = 8
KV_HEADS = 2
HEAD = 128
REACH = 4


def shifted(value, axis, steps):
    count = lax.axis_size(axis)
    leading, last = (max(0, -steps), min(count, count - steps))
    return lax.ppermute(value, axis, [(source, source + steps) for source in range(leading, last)])


def contract(left, right, left_dim, right_dim):
    return lax.dot_general(
        left, right, (((left_dim,), (right_dim,)), ((), ())), preferred_element_type=jnp.float32
    )


def attend(query_rows, upstream, window, volume_here, volume_window):
    factor = HEAD ** (-0.5)
    per_group = HEADS // KV_HEADS
    query_count = query_rows.shape[0]
    allowed = volume_here[:, None] == volume_window[None, :]
    allowed = jnp.repeat(allowed, per_group, axis=0)
    grad_query_parts = []
    key_parts = []
    value_parts = []
    for group in range(KV_HEADS):
        lo_col = group * per_group * HEAD
        hi_col = (group + 1) * per_group * HEAD
        query_group = query_rows[:, lo_col:hi_col].reshape(query_count * per_group, HEAD)
        upstream_group = upstream[:, lo_col:hi_col].reshape(query_count * per_group, HEAD)
        keys = window[:, group * HEAD : (group + 1) * HEAD]
        values = window[:, (KV_HEADS + group) * HEAD : (KV_HEADS + group + 1) * HEAD]
        scores = contract(query_group, keys, 1, 1) * factor
        scores = jnp.where(allowed, scores, -1e30)
        peak = jnp.max(scores, axis=1, keepdims=True)
        log_total = peak + jnp.log(jnp.sum(jnp.exp(scores - peak), axis=1, keepdims=True))
        probs = jnp.exp(scores - log_total)
        probs_low = probs.astype(jnp.bfloat16)
        output = jnp.dot(probs_low, values, preferred_element_type=jnp.float32)
        dot_term = jnp.sum(upstream_group.astype(jnp.float32) * output, axis=1, keepdims=True)
        grad_probs = contract(upstream_group, values, 1, 1)
        grad_scores = (probs * (grad_probs - dot_term) * factor).astype(jnp.bfloat16)
        grad_query = jnp.dot(grad_scores, keys, preferred_element_type=jnp.float32)
        grad_query_parts.append(grad_query.reshape(query_count, per_group * HEAD))
        key_parts.append(contract(grad_scores, query_group, 0, 0))
        value_parts.append(contract(probs_low, upstream_group, 0, 0))
    return (
        jnp.concatenate(grad_query_parts, axis=1),
        jnp.concatenate(key_parts + value_parts, axis=1),
    )


def fetch_direct(pair, offset):
    return shifted((pair[0], pair[1]), ("outer", "inner"), offset)


def return_direct(parcel, offset):
    return shifted(parcel, ("outer", "inner"), offset).astype(jnp.float32)


def weight_kernel(
    n_dp, n_outer, n_inner, in_ref, gkv_ref, out_ref,
    part, pair_out, pair_in, row_out, row_in, col_out, col_in, dp_buf,
    pair_send, pair_recv, row_send, row_recv, col_send, col_recv, dp_send, dp_recv,
):
    f32, bf16 = jnp.float32, jnp.bfloat16
    n_x = n_inner // 2
    dp = lax.axis_index("dp")
    outer = lax.axis_index("outer")
    inner = lax.axis_index("inner")
    x, core = inner // 2, inner % 2
    sibling = (dp, outer, x * 2 + 1 - core)
    row_peers = [(dp, outer, lax.rem(x + s, n_x) * 2 + core) for s in range(1, n_x)]
    col_peers = [(dp, lax.rem(outer + s, n_outer), inner) for s in range(1, n_outer)]
    dp_peers = [(lax.rem(dp + s, n_dp), outer, inner) for s in range(1, n_dp)]
    peers = [sibling] + row_peers + col_peers + dp_peers

    barrier = pltpu.get_barrier_semaphore()
    for peer in peers:
        pl.semaphore_signal(barrier, inc=1, device_id=peer, device_id_type=MESH)

    grad_kv = gkv_ref[...]

    def product(i, carry):
        rows = in_ref[:, pl.ds(pl.multiple_of(i * 128, 128), 128)]
        block = lax.dot_general(rows, grad_kv, (((0,), (0,)), ((), ())), preferred_element_type=f32)
        for j in range(16):
            g, at_x, at_core = j // (2 * n_x), (j // 2) % n_x, j % 2
            piece = block[8 * j : 8 * j + 8, :]
            piece = jnp.concatenate([piece[:, :256], piece[:, 256:]], axis=0)
            start = pl.multiple_of((i * 2 + g) * 16, 16)
            part[at_core, at_x, pl.ds(start, 16), :] = piece
        return carry

    lax.fori_loop(0, in_ref.shape[1] // 128, product, 0)
    pair_out[...] = part[1 - core].astype(bf16)
    pl.semaphore_wait(barrier, len(peers))
    pair = pltpu.make_async_remote_copy(
        src_ref=pair_out, dst_ref=pair_in, send_sem=pair_send, recv_sem=pair_recv,
        device_id=sibling, device_id_type=MESH,
    )
    pair.start()
    pair.wait()

    copies = []
    for s in range(1, n_x):
        to = lax.rem(x + s, n_x)
        row_out[s - 1] = (part[core, to] + pair_in[to].astype(f32)).astype(bf16)
        copy = pltpu.make_async_remote_copy(
            src_ref=row_out.at[s - 1], dst_ref=row_in.at[s - 1],
            send_sem=row_send.at[s - 1], recv_sem=row_recv.at[s - 1],
            device_id=row_peers[s - 1], device_id_type=MESH,
        )
        copy.start()
        copies.append(copy)
    total = part[core, x] + pair_in[x].astype(f32)
    for s, copy in enumerate(copies):
        copy.wait()
        total = total + row_in[s].astype(f32)
    part[core, x] = total
    col_out[...] = total.astype(bf16)

    copies = []
    for s in range(1, n_outer):
        to = lax.rem(outer + s, n_outer)
        copy = pltpu.make_async_remote_copy(
            src_ref=col_out.at[pl.ds(pl.multiple_of(to * 16, 16), 16)], dst_ref=col_in.at[s - 1],
            send_sem=col_send.at[s - 1], recv_sem=col_recv.at[s - 1],
            device_id=col_peers[s - 1], device_id_type=MESH,
        )
        copy.start()
        copies.append(copy)
    mine = part[core, x, pl.ds(pl.multiple_of(outer * 16, 16), 16), :]
    for s, copy in enumerate(copies):
        copy.wait()
        mine = mine + col_in[s].astype(f32)
    dp_buf[dp] = mine

    copies = []
    for s in range(1, n_dp):
        copy = pltpu.make_async_remote_copy(
            src_ref=dp_buf.at[dp], dst_ref=dp_buf.at[dp],
            send_sem=dp_send.at[s - 1], recv_sem=dp_recv.at[s - 1],
            device_id=dp_peers[s - 1], device_id_type=MESH,
        )
        copy.start()
        copies.append(copy)
    for copy in copies:
        copy.wait()
    whole = dp_buf[0]
    for r in range(1, n_dp):
        whole = whole + dp_buf[r]
    out_ref[:, :256] = whole[:8]
    out_ref[:, 256:] = whole[8:]


def weight_gradient(mesh, input_rows, grad_kv):
    f32, bf16 = jnp.float32, jnp.bfloat16
    n_dp, n_outer, n_inner = mesh.shape["dp"], mesh.shape["outer"], mesh.shape["inner"]
    n_x = n_inner // 2
    rows = 16 * n_outer
    dma = pltpu.SemaphoreType.DMA
    return pl.pallas_call(
        functools.partial(weight_kernel, n_dp, n_outer, n_inner),
        out_shape=jax.ShapeDtypeStruct((8, 512), f32),
        in_specs=[pl.BlockSpec(memory_space=pltpu.VMEM)] * 2,
        out_specs=pl.BlockSpec(memory_space=pltpu.VMEM),
        scratch_shapes=[
            pltpu.VMEM((2, n_x, rows, 256), f32),
            pltpu.VMEM((n_x, rows, 256), bf16),
            pltpu.VMEM((n_x, rows, 256), bf16),
            pltpu.VMEM((n_x - 1, rows, 256), bf16),
            pltpu.VMEM((n_x - 1, rows, 256), bf16),
            pltpu.VMEM((rows, 256), bf16),
            pltpu.VMEM((n_outer - 1, 16, 256), bf16),
            pltpu.VMEM((n_dp, 16, 256), f32),
            dma, dma, dma((n_x - 1,)), dma((n_x - 1,)),
            dma((n_outer - 1,)), dma((n_outer - 1,)), dma((n_dp - 1,)), dma((n_dp - 1,)),
        ],
        compiler_params=pltpu.CompilerParams(
            collective_id=0, has_side_effects=True, vmem_limit_bytes=32 * 2**20
        ),
    )(input_rows, grad_kv)


def on_device(mesh, queries, inputs, kv_weight, grad_out, segment_ids):
    query_rows = queries[0]
    input_rows = inputs[0]
    upstream = grad_out[0]
    volume_here = segment_ids[0] + 1
    tok_rows = query_rows.shape[0]
    key_value = jnp.dot(input_rows, kv_weight, preferred_element_type=jnp.float32).astype(
        jnp.bfloat16
    )
    pieces = {0: (key_value, volume_here)}
    for offset in range(1, REACH + 1):
        pieces[-offset] = fetch_direct(pieces[0], offset)
        pieces[offset] = fetch_direct(pieces[0], -offset)
    window = jnp.concatenate([pieces[offset][0] for offset in range(-REACH, REACH + 1)], axis=0)
    volume_window = jnp.concatenate(
        [pieces[offset][1] for offset in range(-REACH, REACH + 1)], axis=0
    )
    grad_query, grad_window = attend(query_rows, upstream, window, volume_here, volume_window)
    parcels = grad_window.astype(jnp.bfloat16)
    parcels = [parcels[index * tok_rows : (index + 1) * tok_rows] for index in range(2 * REACH + 1)]
    total = lax.optimization_barrier(parcels[REACH]).astype(jnp.float32)
    for offset in range(1, REACH + 1):
        total = total + return_direct(parcels[REACH - offset], -offset)
        total = total + return_direct(parcels[REACH + offset], offset)
    grad_kv = total.astype(jnp.bfloat16)
    grad_input = contract(grad_kv, kv_weight, 1, 1).astype(jnp.bfloat16)
    grad_weight = weight_gradient(mesh, input_rows, grad_kv)
    return (grad_query.astype(jnp.bfloat16)[None], grad_input[None], grad_weight)


def solution(mesh):
    in_specs = (
        P("dp", ("outer", "inner"), None),
        P("dp", ("outer", "inner"), None),
        P(),
        P("dp", ("outer", "inner"), None),
        P("dp", ("outer", "inner")),
    )
    out_specs = (
        P("dp", ("outer", "inner"), None),
        P("dp", ("outer", "inner"), None),
        P(("outer", "inner"), None),
    )
    return jax.shard_map(
        functools.partial(on_device, mesh), mesh=mesh, in_specs=in_specs, out_specs=out_specs, check_vma=False
    )
```

```python
import functools
import math

import jax
import jax.numpy as jnp
from jax import lax
from jax.experimental import pallas as pl
from jax.experimental.pallas import tpu as pltpu
from jax.sharding import PartitionSpec as P

MESH = pl.DeviceIdType.MESH
HEADS = 8
GROUPS = 2
PER_GROUP = HEADS // GROUPS
HEAD = 128
TOK = 192
PAIR = 2 * TOK
SENT = TOK + 16
WIDTH = 2 * GROUPS * HEAD
MODEL = HEADS * HEAD
SPAN = 5
HERE = 2
FACTOR = HEAD**-0.5
LOG2E = math.log2(math.e)
FAR = -1e30
F32 = jnp.float32
BF16 = jnp.bfloat16


def product(left, right, left_dim, right_dim):
    return lax.dot_general(
        left, right, (((left_dim,), (right_dim,)), ((), ())), preferred_element_type=F32
    )


def thrice(rows):
    return jnp.concatenate([rows, rows, rows], axis=1)


def columns(index):
    return pl.ds(pl.multiple_of(index * HEAD, HEAD), HEAD)


def remote(source, target, send, recv, device):
    return pltpu.make_async_remote_copy(
        src_ref=source, dst_ref=target, send_sem=send, recv_sem=recv,
        device_id=device, device_id_type=MESH,
    )


def kernel(
    n_dp, n_outer, n_inner,
    q_hbm, in_hbm, w_hbm, up_hbm, ids_ref,
    dq_hbm, dx_hbm, gw_ref,
    raw, rows_in, weight, queries, upstream,
    window, ids_col, scores, grads, peak, total, dots,
    probs_low, grad_scores, grad_query,
    own, sib_out, sib_in, ring_out, ring_in, grad_kv,
    dq_out, dx_out,
    part, pair_out, pair_in, row_out, row_in, col_out, col_in, dp_buf,
    load_sem, store_sem,
    halo_send, halo_recv, sib_send, sib_recv, ring_send, ring_recv,
    pair_send, pair_recv, row_send, row_recv, col_send, col_recv, dp_send, dp_recv,
):
    n_x = n_inner // 2
    chips = n_outer * n_x
    dp = lax.axis_index("dp")
    outer = lax.axis_index("outer")
    inner = lax.axis_index("inner")
    x, core = inner // 2, inner % 2
    chip = outer * n_x + x

    def chip_at(steps):
        there = lax.rem(chip + steps + chips, chips)
        return (dp, there // n_x, lax.rem(there, n_x) * 2 + core)

    sibling = (dp, outer, x * 2 + 1 - core)
    right, left = chip_at(1), chip_at(-1)
    row_peers = [(dp, outer, lax.rem(x + s, n_x) * 2 + core) for s in range(1, n_x)]
    col_peers = [(dp, lax.rem(outer + s, n_outer), inner) for s in range(1, n_outer)]
    dp_peers = [(lax.rem(dp + s, n_dp), outer, inner) for s in range(1, n_dp)]
    peers = [sibling, right, left] + row_peers + col_peers + dp_peers

    barrier = pltpu.get_barrier_semaphore()
    for peer in peers:
        pl.semaphore_signal(barrier, inc=1, device_id=peer, device_id_type=MESH)

    loads = [
        pltpu.make_async_copy(source, target, load_sem.at[i])
        for i, (source, target) in enumerate(
            [(in_hbm, rows_in), (w_hbm, weight), (q_hbm, raw.at[0]), (up_hbm, raw.at[1])]
        )
    ]
    for load in loads:
        load.start()

    ids_row = ids_ref[...].astype(F32)
    twice = jnp.concatenate([ids_row, ids_row, jnp.zeros((1, WIDTH - PAIR), F32)], axis=1)
    window[HERE, 0, TOK:SENT, :] = jnp.broadcast_to(twice, (SENT - TOK, WIDTH)).astype(BF16)
    ids_col[...] = jnp.transpose(jnp.broadcast_to(twice[:, :256], (HEAD, 256)))[:TOK]

    loads[0].wait()
    loads[1].wait()
    window[HERE, 0, 0:TOK, :] = product(rows_in[...], weight[...], 1, 0).astype(BF16)
    pl.semaphore_wait(barrier, len(peers))

    halo = [
        remote(source, target, halo_send.at[i], halo_recv.at[i], device)
        for i, (source, target, device) in enumerate(
            [
                (window.at[2, 0], window.at[2, 1], sibling),
                (window.at[2, 0], window.at[1, 0], right),
                (window.at[2, 0], window.at[3, 0], left),
                (window.at[1, 0], window.at[0, 0], right),
                (window.at[3, 0], window.at[4, 0], left),
                (window.at[1, 0], window.at[1, 1], sibling),
                (window.at[3, 0], window.at[3, 1], sibling),
                (window.at[0, 0], window.at[0, 1], sibling),
                (window.at[4, 0], window.at[4, 1], sibling),
            ]
        )
    ]
    for i in (1, 2, 0):
        halo[i].start()

    loads[2].wait()
    loads[3].wait()
    for h in range(HEADS):
        at = slice(h * HEAD, (h + 1) * HEAD)
        queries[h] = raw[0, :, at]
        upstream[h] = raw[1, :, at]

    def keys_of(j, at):
        return jnp.concatenate(
            [window[j, 0, 0:TOK, columns(at)], window[j, 1, 0:TOK, columns(at)]], axis=0
        )

    def first_pass(j, opening):
        lane = lax.broadcasted_iota(jnp.int32, (1, PAIR), 1)
        ids_key = jnp.where(
            lane < TOK,
            window[j, 0, TOK:SENT, :PAIR].astype(F32)[:1],
            window[j, 1, TOK:SENT, :PAIR].astype(F32)[:1],
        )
        mask = jnp.where(thrice(ids_col[...]) == ids_key, 0.0, FAR)

        def group(g, carry):
            keys = keys_of(j, g)
            values = keys_of(j, GROUPS + g)
            for member in range(PER_GROUP):
                h = g * PER_GROUP + member
                score = product(queries[h], keys, 1, 1) * (FACTOR * LOG2E) + mask
                grad = product(upstream[h], values, 1, 1)
                scores[j, h] = score
                grads[j, h] = grad
                top = jnp.maximum(
                    jnp.maximum(score[:, :128], score[:, 128:256]), score[:, 256:]
                )
                if not opening:
                    before = peak[h]
                    top = jnp.maximum(before, top)
                weights = jnp.exp2(score - thrice(top))
                dot = weights * grad
                weights = weights[:, :128] + weights[:, 128:256] + weights[:, 256:]
                dot = dot[:, :128] + dot[:, 128:256] + dot[:, 256:]
                if not opening:
                    scale = jnp.exp2(before - top)
                    weights = weights + total[h] * scale
                    dot = dot + dots[h] * scale
                peak[h] = top
                total[h] = weights
                dots[h] = dot
            return carry

        lax.fori_loop(0, GROUPS, group, 0)

    halo[0].wait_recv()
    first_pass(HERE, True)
    halo[1].wait_recv()
    halo[3].start()
    halo[5].start()
    halo[2].wait_recv()
    halo[4].start()
    halo[6].start()
    halo[5].wait_recv()
    halo[6].wait_recv()

    def near(t, carry):
        first_pass(1 + 2 * t, False)
        return carry

    lax.fori_loop(0, 2, near, 0)
    halo[3].wait_recv()
    halo[7].start()
    halo[4].wait_recv()
    halo[8].start()
    halo[7].wait_recv()
    halo[8].wait_recv()

    def distant(t, carry):
        first_pass(4 * t, False)
        return carry

    lax.fori_loop(0, 2, distant, 0)

    def merge(h, carry):
        top = jnp.max(peak[h], axis=1, keepdims=True)
        scale = jnp.exp2(peak[h] - top)
        weights = jnp.sum(total[h] * scale, axis=1, keepdims=True)
        dot = jnp.sum(dots[h] * scale, axis=1, keepdims=True) / weights
        peak[h] = jnp.broadcast_to(top + jnp.log(weights) * LOG2E, (TOK, HEAD))
        dots[h] = jnp.broadcast_to(dot, (TOK, HEAD))
        return carry

    lax.fori_loop(0, HEADS, merge, 0)

    def second_pass(j, opening):
        def group(g, carry):
            for member in range(PER_GROUP):
                h = g * PER_GROUP + member
                probs = jnp.exp2(scores[j, h] - thrice(peak[h]))
                at = slice(member * TOK, (member + 1) * TOK)
                probs_low[at, :] = probs.astype(BF16)
                grad_scores[at, :] = (probs * (grads[j, h] - thrice(dots[h]))).astype(BF16)
            low = grad_scores[...]
            part_query = product(low, keys_of(j, g), 1, 0)
            start = g * PER_GROUP
            query = queries[pl.ds(start, PER_GROUP)].reshape(PER_GROUP * TOK, HEAD)
            up = upstream[pl.ds(start, PER_GROUP)].reshape(PER_GROUP * TOK, HEAD)
            if opening:
                grad_query[g] = part_query
            else:
                grad_query[g] = grad_query[g] + part_query
            key = product(low, query, 0, 0) * FACTOR
            value = product(probs_low[...], up, 0, 0)
            own[j, :, columns(g)] = key[:TOK]
            own[j, :, columns(GROUPS + g)] = value[:TOK]
            sib_out[j, :, columns(g)] = key[TOK:].astype(BF16)
            sib_out[j, :, columns(GROUPS + g)] = value[TOK:].astype(BF16)
            return carry

        lax.fori_loop(0, GROUPS, group, 0)

    sib = [
        remote(sib_out.at[j], sib_in.at[j], sib_send.at[j], sib_recv.at[j], sibling)
        for j in range(SPAN)
    ]
    ring = [
        remote(ring_out.at[i], ring_in.at[i], ring_send.at[i], ring_recv.at[i], device)
        for i, device in enumerate([left, right, left, right])
    ]

    second_pass(0, True)
    sib[0].start()
    second_pass(4, False)
    sib[4].start()
    for i, j in enumerate((0, 4)):
        sib[j].wait_recv()
        ring_out[i] = (own[j] + sib_in[j].astype(F32)).astype(BF16)
        ring[i].start()
    second_pass(1, False)
    sib[1].start()
    second_pass(3, False)
    sib[3].start()
    for i, j in enumerate((1, 3)):
        sib[j].wait_recv()
        ring[i].wait_recv()
        ring_out[2 + i] = (
            own[j] + sib_in[j].astype(F32) + ring_in[i].astype(F32)
        ).astype(BF16)
        ring[2 + i].start()
    second_pass(2, False)
    sib[2].start()
    for h in range(HEADS):
        at = slice((h % PER_GROUP) * TOK, (h % PER_GROUP + 1) * TOK)
        dq_out[:, h * HEAD : (h + 1) * HEAD] = (
            grad_query[h // PER_GROUP, at, :] * FACTOR
        ).astype(BF16)
    dq_store = pltpu.make_async_copy(dq_out, dq_hbm, store_sem.at[0])
    dq_store.start()
    sib[2].wait_recv()
    ring[2].wait_recv()
    ring[3].wait_recv()
    grad_kv[...] = (
        own[2] + sib_in[2].astype(F32) + ring_in[2].astype(F32) + ring_in[3].astype(F32)
    ).astype(BF16)

    def weight_rows(i, carry):
        block = product(rows_in[:, pl.ds(pl.multiple_of(i * 128, 128), 128)], grad_kv[...], 0, 0)
        for j in range(16):
            g, at_x, at_core = j // (2 * n_x), (j // 2) % n_x, j % 2
            piece = block[8 * j : 8 * j + 8, :]
            piece = jnp.concatenate([piece[:, :256], piece[:, 256:]], axis=0)
            start = pl.multiple_of((i * 2 + g) * 16, 16)
            part[at_core, at_x, pl.ds(start, 16), :] = piece
        return carry

    lax.fori_loop(0, MODEL // 128, weight_rows, 0)
    pair_out[...] = part[1 - core].astype(BF16)
    pair = remote(pair_out, pair_in, pair_send, pair_recv, sibling)
    pair.start()
    dx_out[...] = product(grad_kv[...], weight[...], 1, 1).astype(BF16)
    dx_store = pltpu.make_async_copy(dx_out, dx_hbm, store_sem.at[1])
    dx_store.start()
    pair.wait()

    copies = []
    for s in range(1, n_x):
        to = lax.rem(x + s, n_x)
        row_out[s - 1] = (part[core, to] + pair_in[to].astype(F32)).astype(BF16)
        copy = remote(
            row_out.at[s - 1], row_in.at[s - 1], row_send.at[s - 1], row_recv.at[s - 1],
            row_peers[s - 1],
        )
        copy.start()
        copies.append(copy)
    mine = part[core, x] + pair_in[x].astype(F32)
    for s, copy in enumerate(copies):
        copy.wait()
        mine = mine + row_in[s].astype(F32)
    part[core, x] = mine
    col_out[...] = mine.astype(BF16)

    copies = []
    for s in range(1, n_outer):
        to = lax.rem(outer + s, n_outer)
        copy = remote(
            col_out.at[pl.ds(pl.multiple_of(to * 16, 16), 16)], col_in.at[s - 1],
            col_send.at[s - 1], col_recv.at[s - 1], col_peers[s - 1],
        )
        copy.start()
        copies.append(copy)
    mine = part[core, x, pl.ds(pl.multiple_of(outer * 16, 16), 16), :]
    for s, copy in enumerate(copies):
        copy.wait()
        mine = mine + col_in[s].astype(F32)
    dp_buf[dp] = mine

    copies = []
    for s in range(1, n_dp):
        copy = remote(
            dp_buf.at[dp], dp_buf.at[dp], dp_send.at[s - 1], dp_recv.at[s - 1], dp_peers[s - 1]
        )
        copy.start()
        copies.append(copy)
    for copy in copies:
        copy.wait()
    whole = dp_buf[0]
    for r in range(1, n_dp):
        whole = whole + dp_buf[r]
    gw_ref[:, :256] = whole[:8]
    gw_ref[:, 256:] = whole[8:]

    for copy in halo + sib + ring:
        copy.wait_send()
    dq_store.wait()
    dx_store.wait()


def on_device(sizes, queries, inputs, kv_weight, grad_out, segment_ids):
    n_dp, n_outer, n_inner = sizes
    n_x = n_inner // 2
    rows = 16 * n_outer
    vmem, dma = pltpu.VMEM, pltpu.SemaphoreType.DMA
    anywhere = pl.BlockSpec(memory_space=pl.ANY)
    inside = pl.BlockSpec(memory_space=pltpu.VMEM)
    tokens = jax.ShapeDtypeStruct((TOK, MODEL), BF16)
    grad_query, grad_input, grad_weight = pl.pallas_call(
        functools.partial(kernel, *sizes),
        out_shape=(tokens, tokens, jax.ShapeDtypeStruct((8, WIDTH), F32)),
        in_specs=[anywhere] * 4 + [inside],
        out_specs=(anywhere, anywhere, inside),
        scratch_shapes=[
            vmem((2, TOK, MODEL), BF16),
            vmem((TOK, MODEL), BF16),
            vmem((MODEL, WIDTH), BF16),
            vmem((HEADS, TOK, HEAD), BF16),
            vmem((HEADS, TOK, HEAD), BF16),
            vmem((SPAN, 2, SENT, WIDTH), BF16),
            vmem((TOK, HEAD), F32),
            vmem((SPAN, HEADS, TOK, PAIR), F32),
            vmem((SPAN, HEADS, TOK, PAIR), F32),
            vmem((HEADS, TOK, HEAD), F32),
            vmem((HEADS, TOK, HEAD), F32),
            vmem((HEADS, TOK, HEAD), F32),
            vmem((PER_GROUP * TOK, PAIR), BF16),
            vmem((PER_GROUP * TOK, PAIR), BF16),
            vmem((GROUPS, PER_GROUP * TOK, HEAD), F32),
            vmem((SPAN, TOK, WIDTH), F32),
            vmem((SPAN, TOK, WIDTH), BF16),
            vmem((SPAN, TOK, WIDTH), BF16),
            vmem((4, TOK, WIDTH), BF16),
            vmem((4, TOK, WIDTH), BF16),
            vmem((TOK, WIDTH), BF16),
            vmem((TOK, MODEL), BF16),
            vmem((TOK, MODEL), BF16),
            vmem((2, n_x, rows, 256), F32),
            vmem((n_x, rows, 256), BF16),
            vmem((n_x, rows, 256), BF16),
            vmem((n_x - 1, rows, 256), BF16),
            vmem((n_x - 1, rows, 256), BF16),
            vmem((rows, 256), BF16),
            vmem((n_outer - 1, 16, 256), BF16),
            vmem((n_dp, 16, 256), F32),
            dma((4,)), dma((2,)),
            dma((9,)), dma((9,)), dma((SPAN,)), dma((SPAN,)), dma((4,)), dma((4,)),
            dma, dma, dma((n_x - 1,)), dma((n_x - 1,)),
            dma((n_outer - 1,)), dma((n_outer - 1,)), dma((n_dp - 1,)), dma((n_dp - 1,)),
        ],
        compiler_params=pltpu.CompilerParams(
            collective_id=0, has_side_effects=True, vmem_limit_bytes=56 * 2**20
        ),
    )(queries[0], inputs[0], kv_weight, grad_out[0], segment_ids)
    return grad_query[None], grad_input[None], grad_weight


def solution(mesh):
    spread = P("dp", ("outer", "inner"), None)
    sizes = (mesh.shape["dp"], mesh.shape["outer"], mesh.shape["inner"])
    return jax.shard_map(
        functools.partial(on_device, sizes),
        mesh=mesh,
        in_specs=(spread, spread, P(), spread, P("dp", ("outer", "inner"))),
        out_specs=(spread, spread, P(("outer", "inner"), None)),
        check_vma=False,
    )
```

```python
import functools
import math

import jax
import jax.numpy as jnp
from jax import lax
from jax.experimental import pallas as pl
from jax.experimental.pallas import tpu as pltpu
from jax.sharding import PartitionSpec as P

MESH = pl.DeviceIdType.MESH
HEADS = 8
GROUPS = 2
PER_GROUP = HEADS // GROUPS
HEAD = 128
TOK = 192
PAIR = 2 * TOK
SENT = TOK + 16
HALF = 2 * HEAD
TILES = PAIR // 8
WIDTH = 2 * GROUPS * HEAD
MODEL = HEADS * HEAD
SPAN = 5
HERE = 2
FACTOR = HEAD**-0.5
LOG2E = math.log2(math.e)
FAR = -1e30
F32 = jnp.float32
BF16 = jnp.bfloat16


def product(left, right, left_dim, right_dim):
    return lax.dot_general(
        left, right, (((left_dim,), (right_dim,)), ((), ())), preferred_element_type=F32
    )


def thrice(rows):
    return jnp.concatenate([rows, rows, rows], axis=1)


def remote(source, target, send, recv, device):
    return pltpu.make_async_remote_copy(
        src_ref=source, dst_ref=target, send_sem=send, recv_sem=recv,
        device_id=device, device_id_type=MESH,
    )


def kernel(
    n_dp, n_outer, n_inner,
    q_hbm, in_hbm, w_hbm, up_hbm, ids_ref,
    dq_hbm, dx_hbm, gw_ref,
    raw, rows_in, rows_sib, weight, queries, upstream,
    window, ids_query, mask, scores, grads, peak, total, dots, grad_query,
    own, sib_out, sib_in, ring_out, ring_in, grad_kv, grad_kv_sib,
    dq_out, dx_out,
    part, row_out, row_in, col_out, col_in, mine, dp_buf,
    load_sem, store_sem,
    halo_send, halo_recv, rows_send, rows_recv, sib_send, sib_recv, ring_send, ring_recv,
    pair_send, pair_recv, row_send, row_recv, col_send, col_recv, dp_send, dp_recv,
):
    n_x = n_inner // 2
    chips = n_outer * n_x
    dp = lax.axis_index("dp")
    outer = lax.axis_index("outer")
    inner = lax.axis_index("inner")
    x, core = inner // 2, inner % 2
    chip = outer * n_x + x

    def chip_at(steps):
        there = lax.rem(chip + steps + chips, chips)
        return (dp, there // n_x, lax.rem(there, n_x) * 2 + core)

    sibling = (dp, outer, x * 2 + 1 - core)
    right, left = chip_at(1), chip_at(-1)
    row_right = (dp, outer, lax.rem(x + 1, n_x) * 2 + core)
    row_left = (dp, outer, lax.rem(x + n_x - 1, n_x) * 2 + core)
    col_peers = [(dp, lax.rem(outer + s, n_outer), inner) for s in range(1, n_outer)]
    dp_peers = [
        (s, flip, (lax.rem(dp + s, n_dp), outer, x * 2 + (1 - core if flip else core)))
        for s in range(n_dp)
        for flip in (0, 1)
        if s or flip
    ]
    peers = [right, left, row_right, row_left] + col_peers + [peer for _, _, peer in dp_peers]

    barrier = pltpu.get_barrier_semaphore()
    for peer in peers:
        pl.semaphore_signal(barrier, inc=1, device_id=peer, device_id_type=MESH)

    loads = [
        pltpu.make_async_copy(source, target, load_sem.at[i])
        for i, (source, target) in enumerate(
            [(in_hbm, rows_in), (w_hbm, weight), (q_hbm, raw.at[0]), (up_hbm, raw.at[1])]
        )
    ]
    for load in loads:
        load.start()

    ids_row = ids_ref[...].astype(F32)
    twice = jnp.concatenate([ids_row, ids_row, jnp.zeros((1, 2 * HALF - PAIR), F32)], axis=1)
    first_row = lax.broadcasted_iota(jnp.int32, (SENT - TOK, HALF), 0) == 0
    window[HERE, 0, 0, TOK:SENT, :] = jnp.where(
        first_row, twice[:, :HALF], twice[:, HALF:]
    ).astype(BF16)
    ids_query[...] = jnp.broadcast_to(twice[:, :PAIR], (8, PAIR))

    loads[0].wait()
    loads[1].wait()
    key_value = product(rows_in[...], weight[...], 1, 0).astype(BF16)
    for g in range(GROUPS):
        window[HERE, 0, g, 0:TOK, :HEAD] = key_value[:, g * HEAD : (g + 1) * HEAD]
        window[HERE, 0, g, 0:TOK, HEAD:] = key_value[
            :, (GROUPS + g) * HEAD : (GROUPS + g + 1) * HEAD
        ]
    pl.semaphore_wait(barrier, len(peers))

    halo = []
    for g in range(GROUPS):
        rows = pl.ds(0, TOK if g else SENT)
        for i, (source, target, device) in enumerate(
            [
                ((2, 0), (2, 1), sibling),
                ((2, 0), (1, 0), right),
                ((2, 0), (3, 0), left),
                ((1, 0), (0, 0), right),
                ((3, 0), (4, 0), left),
                ((1, 0), (1, 1), sibling),
                ((3, 0), (3, 1), sibling),
                ((0, 0), (0, 1), sibling),
                ((4, 0), (4, 1), sibling),
            ]
        ):
            halo.append(
                remote(
                    window.at[source[0], source[1], g, rows],
                    window.at[target[0], target[1], g, rows],
                    halo_send.at[9 * g + i], halo_recv.at[9 * g + i], device,
                )
            )
    for g in range(GROUPS):
        for i in (1, 2, 0):
            halo[9 * g + i].start()
    rows_copy = remote(rows_in, rows_sib, rows_send, rows_recv, sibling)
    rows_copy.start()

    loads[2].wait()
    loads[3].wait()
    for h in range(HEADS):
        g, member = h // PER_GROUP, h % PER_GROUP
        at = slice(h * HEAD, (h + 1) * HEAD)
        queries[g, member * TOK : (member + 1) * TOK, :] = raw[0, :, at]
        upstream[g, member * TOK : (member + 1) * TOK, :] = raw[1, :, at]

    def of_chunk(j, g, at):
        return jnp.concatenate([window[j, 0, g, 0:TOK, at], window[j, 1, g, 0:TOK, at]], axis=0)

    keys_at, values_at = slice(0, HEAD), slice(HEAD, HALF)

    def make_mask(j):
        lane = lax.broadcasted_iota(jnp.int32, (1, PAIR), 1)
        near, far = (
            jnp.concatenate([ids[0:1], ids[1:2, : PAIR - HALF]], axis=1)
            for ids in (window[j, side, 0, TOK:SENT, :].astype(F32) for side in (0, 1))
        )
        ids_key = jnp.where(lane < TOK, near, far)
        ids_col = jnp.transpose(jnp.broadcast_to(ids_key, (HEAD, PAIR)))
        mask[j] = jnp.where(thrice(ids_col) == ids_query[0:1, :], 0.0, FAR)

    def first_pass(j, g, opening):
        keys, values = of_chunk(j, g, keys_at), of_chunk(j, g, values_at)
        for b in range(2):
            at = slice(b * PAIR, (b + 1) * PAIR)
            score = product(keys, queries[g, at, :], 1, 1) * (FACTOR * LOG2E) + mask[j]
            grad = product(values, upstream[g, at, :], 1, 1)
            scores[j, g, b] = score
            grads[j, g, b] = grad
            score = score.reshape(TILES, 8, PAIR)
            top = jnp.max(score, axis=0)
            if not opening:
                before = peak[g, b]
                top = jnp.maximum(before, top)
            weights = jnp.exp2(score - top[None])
            dot = jnp.sum(weights * grad.reshape(TILES, 8, PAIR), axis=0)
            weights = jnp.sum(weights, axis=0)
            if not opening:
                scale = jnp.exp2(before - top)
                weights = weights + total[g, b] * scale
                dot = dot + dots[g, b] * scale
            peak[g, b] = top
            total[g, b] = weights
            dots[g, b] = dot

    def both(visit, first, stride):
        def step(t, carry):
            visit(first + stride * t)
            return carry

        lax.fori_loop(0, 2, step, 0)

    def merge(g):
        for b in range(2):
            top = jnp.max(peak[g, b], axis=0, keepdims=True)
            scale = jnp.exp2(peak[g, b] - top)
            weights = jnp.sum(total[g, b] * scale, axis=0, keepdims=True)
            dot = jnp.sum(dots[g, b] * scale, axis=0, keepdims=True) / weights
            peak[g, b] = jnp.broadcast_to(top + jnp.log(weights) * LOG2E, (8, PAIR))
            dots[g, b] = jnp.broadcast_to(dot, (8, PAIR))

    def second_pass(j, g, opening):
        keys = of_chunk(j, g, keys_at)
        key, value = 0.0, 0.0
        for b in range(2):
            at = slice(b * PAIR, (b + 1) * PAIR)
            probs = jnp.exp2(scores[j, g, b].reshape(TILES, 8, PAIR) - peak[g, b][None])
            low = probs.reshape(PAIR, PAIR).astype(BF16)
            grad = probs * (grads[j, g, b].reshape(TILES, 8, PAIR) - dots[g, b][None])
            grad = grad.reshape(PAIR, PAIR).astype(BF16)
            key = key + product(grad, queries[g, at, :], 1, 0)
            value = value + product(low, upstream[g, at, :], 1, 0)
            query = product(keys, grad, 0, 0)
            grad_query[g, b] = query if opening else grad_query[g, b] + query
        key = key * FACTOR
        own[j, g, :, :HEAD] = key[:TOK]
        own[j, g, :, HEAD:] = value[:TOK]
        sib_out[j, g, :, :HEAD] = key[TOK:].astype(BF16)
        sib_out[j, g, :, HEAD:] = value[TOK:].astype(BF16)

    sib = [
        [
            remote(
                sib_out.at[j, g], sib_in.at[j, g],
                sib_send.at[GROUPS * j + g], sib_recv.at[GROUPS * j + g], sibling,
            )
            for g in range(GROUPS)
        ]
        for j in range(SPAN)
    ]
    ring = [
        [
            remote(
                ring_out.at[i, g], ring_in.at[i, g],
                ring_send.at[GROUPS * i + g], ring_recv.at[GROUPS * i + g], device,
            )
            for g in range(GROUPS)
        ]
        for i, device in enumerate([left, right, left, right])
    ]

    def near_arrived(g):
        halo[9 * g + 1].wait_recv()
        halo[9 * g + 3].start()
        halo[9 * g + 2].wait_recv()
        halo[9 * g + 4].start()
        halo[9 * g + 5].start()
        halo[9 * g + 6].start()

    def distant_arrived(g):
        halo[9 * g + 3].wait_recv()
        halo[9 * g + 7].start()
        halo[9 * g + 4].wait_recv()
        halo[9 * g + 8].start()

    def send_distant(g):
        for i, j in enumerate((0, 4)):
            sib[j][g].wait_recv()
            ring_out[i, g] = (own[j, g] + sib_in[j, g].astype(F32)).astype(BF16)
            ring[i][g].start()

    def send_near(g):
        for i, j in enumerate((1, 3)):
            sib[j][g].wait_recv()
            ring[i][g].wait_recv()
            ring_out[2 + i, g] = (
                own[j, g] + sib_in[j, g].astype(F32) + ring_in[i, g].astype(F32)
            ).astype(BF16)
            ring[2 + i][g].start()

    halo[0].wait_recv()
    make_mask(HERE)
    first_pass(HERE, 0, True)
    halo[9].wait_recv()
    first_pass(HERE, 1, True)

    near_arrived(0)
    halo[5].wait_recv()
    halo[6].wait_recv()
    both(make_mask, 1, 2)
    both(lambda j: first_pass(j, 0, False), 1, 2)
    near_arrived(1)
    halo[14].wait_recv()
    halo[15].wait_recv()
    both(lambda j: first_pass(j, 1, False), 1, 2)

    distant_arrived(0)
    halo[7].wait_recv()
    halo[8].wait_recv()
    both(make_mask, 0, 4)
    both(lambda j: first_pass(j, 0, False), 0, 4)
    merge(0)
    grad_query[...] = jnp.zeros_like(grad_query)
    distant_arrived(1)
    both(lambda j: second_pass(j, 0, False), 0, 4)
    sib[0][0].start()
    sib[4][0].start()
    halo[16].wait_recv()
    halo[17].wait_recv()
    both(lambda j: first_pass(j, 1, False), 0, 4)
    send_distant(0)
    merge(1)
    both(lambda j: second_pass(j, 1, False), 0, 4)
    sib[0][1].start()
    sib[4][1].start()
    both(lambda j: second_pass(j, 0, False), 1, 2)
    sib[1][0].start()
    sib[3][0].start()
    send_distant(1)
    send_near(0)
    both(lambda j: second_pass(j, 1, False), 1, 2)
    sib[1][1].start()
    sib[3][1].start()
    second_pass(HERE, 0, False)
    sib[2][0].start()
    send_near(1)
    second_pass(HERE, 1, False)
    sib[2][1].start()

    for g in range(GROUPS):
        for b in range(2):
            rows = jnp.transpose(grad_query[g, b]) * FACTOR
            for m in range(2):
                h = g * PER_GROUP + 2 * b + m
                dq_out[:, h * HEAD : (h + 1) * HEAD] = rows[m * TOK : (m + 1) * TOK].astype(BF16)
    dq_store = pltpu.make_async_copy(dq_out, dq_hbm, store_sem.at[0])
    dq_store.start()

    for g in range(GROUPS):
        sib[2][g].wait_recv()
        ring[2][g].wait_recv()
        ring[3][g].wait_recv()
        grad_kv[g] = (
            own[2, g] + sib_in[2, g].astype(F32)
            + ring_in[2, g].astype(F32) + ring_in[3, g].astype(F32)
        ).astype(BF16)
    pair = remote(grad_kv.at[1 - core], grad_kv_sib, pair_send, pair_recv, sibling)
    pair.start()
    rows_copy.wait_recv()
    pair.wait_recv()

    def weight_rows(i, carry):
        at = pl.ds(pl.multiple_of(i * 128, 128), 128)
        block = product(rows_in[:, at], grad_kv[core], 0, 0)
        block = block + product(rows_sib[:, at], grad_kv_sib[...], 0, 0)
        for s in range(128 // (16 * n_x)):
            start = pl.multiple_of((i * (128 // (16 * n_x)) + s) * 16, 16)
            for to in range(n_x):
                lo = (s * n_x + to) * 16
                part[to, pl.ds(start, 16), :] = block[lo : lo + 16, :]
        return carry

    lax.fori_loop(0, MODEL // 128, weight_rows, 0)

    rows_x = 16 * n_outer // 2
    top, bottom = pl.ds(0, rows_x), pl.ds(rows_x, rows_x)
    at_right, at_left = lax.rem(x + 1, n_x), lax.rem(x + n_x - 1, n_x)
    opposite = lax.rem(x + 2, n_x)
    row = [
        remote(row_out.at[i], row_in.at[i], row_send.at[i], row_recv.at[i], device)
        for i, device in enumerate(
            [row_right, row_left, row_right, row_left, row_right, row_left]
        )
    ]
    for i, (to, rows) in enumerate(
        [(opposite, top), (opposite, bottom), (at_right, bottom), (at_left, top)]
    ):
        row_out[i] = part[to, rows, :].astype(BF16)
        row[i].start()
    kv_rows = jnp.concatenate(
        [grad_kv[0, :, :HEAD], grad_kv[1, :, :HEAD], grad_kv[0, :, HEAD:], grad_kv[1, :, HEAD:]],
        axis=1,
    )
    dx_out[...] = product(kv_rows, weight[...], 1, 1).astype(BF16)
    dx_store = pltpu.make_async_copy(dx_out, dx_hbm, store_sem.at[1])
    dx_store.start()
    for i, (to, rows) in enumerate([(at_right, top), (at_left, bottom)]):
        row[i].wait_recv()
        row_out[4 + i] = (part[to, rows, :] + row_in[i].astype(F32)).astype(BF16)
        row[4 + i].start()
    for i in range(2, 6):
        row[i].wait_recv()
    upper = part[x, top, :] + row_in[3].astype(F32) + row_in[4].astype(F32)
    lower = part[x, bottom, :] + row_in[2].astype(F32) + row_in[5].astype(F32)
    part[x, top, :] = upper
    part[x, bottom, :] = lower
    col_out[top, :] = upper.astype(BF16)
    col_out[bottom, :] = lower.astype(BF16)

    col = []
    for s in range(1, n_outer):
        to = lax.rem(outer + s, n_outer)
        copy = remote(
            col_out.at[pl.ds(pl.multiple_of(to * 16, 16), 16)], col_in.at[s - 1],
            col_send.at[s - 1], col_recv.at[s - 1], col_peers[s - 1],
        )
        copy.start()
        col.append(copy)
    share = part[x, pl.ds(pl.multiple_of(outer * 16, 16), 16), :]
    for s, copy in enumerate(col):
        copy.wait_recv()
        share = share + col_in[s].astype(F32)
    mine[...] = share

    last = []
    for i, (s, flip, peer) in enumerate(dp_peers):
        half = 1 - core if flip else core
        copy = remote(
            mine.at[pl.ds(pl.multiple_of(half * 8, 8), 8)], dp_buf.at[dp, core],
            dp_send.at[i], dp_recv.at[i], peer,
        )
        copy.start()
        last.append(copy)
    dp_buf[dp, core] = mine[pl.ds(pl.multiple_of(core * 8, 8), 8), :]
    for copy in last:
        copy.wait_recv()
    for g in range(GROUPS):
        whole = dp_buf[0, g]
        for r in range(1, n_dp):
            whole = whole + dp_buf[r, g]
        gw_ref[:, g * HEAD : (g + 1) * HEAD] = whole[:, :HEAD]
        gw_ref[:, (GROUPS + g) * HEAD : (GROUPS + g + 1) * HEAD] = whole[:, HEAD:]

    for copy in halo + sum(sib, []) + sum(ring, []) + [rows_copy, pair] + row + col + last:
        copy.wait_send()
    dq_store.wait()
    dx_store.wait()


def on_device(sizes, queries, inputs, kv_weight, grad_out, segment_ids):
    n_dp, n_outer, n_inner = sizes
    n_x = n_inner // 2
    rows = 16 * n_outer
    vmem, dma = pltpu.VMEM, pltpu.SemaphoreType.DMA
    anywhere = pl.BlockSpec(memory_space=pl.ANY)
    inside = pl.BlockSpec(memory_space=pltpu.VMEM)
    tokens = jax.ShapeDtypeStruct((TOK, MODEL), BF16)
    grad_query, grad_input, grad_weight = pl.pallas_call(
        functools.partial(kernel, *sizes),
        out_shape=(tokens, tokens, jax.ShapeDtypeStruct((8, WIDTH), F32)),
        in_specs=[anywhere] * 4 + [inside],
        out_specs=(anywhere, anywhere, inside),
        scratch_shapes=[
            vmem((2, TOK, MODEL), BF16),
            vmem((TOK, MODEL), BF16),
            vmem((TOK, MODEL), BF16),
            vmem((MODEL, WIDTH), BF16),
            vmem((GROUPS, PER_GROUP * TOK, HEAD), BF16),
            vmem((GROUPS, PER_GROUP * TOK, HEAD), BF16),
            vmem((SPAN, 2, GROUPS, SENT, HALF), BF16),
            vmem((8, PAIR), F32),
            vmem((SPAN, PAIR, PAIR), F32),
            vmem((SPAN, GROUPS, 2, PAIR, PAIR), F32),
            vmem((SPAN, GROUPS, 2, PAIR, PAIR), F32),
            vmem((GROUPS, 2, 8, PAIR), F32),
            vmem((GROUPS, 2, 8, PAIR), F32),
            vmem((GROUPS, 2, 8, PAIR), F32),
            vmem((GROUPS, 2, HEAD, PAIR), F32),
            vmem((SPAN, GROUPS, TOK, HALF), F32),
            vmem((SPAN, GROUPS, TOK, HALF), BF16),
            vmem((SPAN, GROUPS, TOK, HALF), BF16),
            vmem((4, GROUPS, TOK, HALF), BF16),
            vmem((4, GROUPS, TOK, HALF), BF16),
            vmem((GROUPS, TOK, HALF), BF16),
            vmem((TOK, HALF), BF16),
            vmem((TOK, MODEL), BF16),
            vmem((TOK, MODEL), BF16),
            vmem((n_x, rows, HALF), F32),
            vmem((6, rows // 2, HALF), BF16),
            vmem((6, rows // 2, HALF), BF16),
            vmem((rows, HALF), BF16),
            vmem((n_outer - 1, 16, HALF), BF16),
            vmem((16, HALF), F32),
            vmem((n_dp, 2, 8, HALF), F32),
            dma((4,)), dma((2,)),
            dma((18,)), dma((18,)), dma, dma, dma((10,)), dma((10,)), dma((8,)), dma((8,)),
            dma, dma, dma((6,)), dma((6,)),
            dma((n_outer - 1,)), dma((n_outer - 1,)), dma((2 * n_dp - 1,)), dma((2 * n_dp - 1,)),
        ],
        compiler_params=pltpu.CompilerParams(
            collective_id=0, has_side_effects=True, vmem_limit_bytes=56 * 2**20
        ),
    )(queries[0], inputs[0], kv_weight, grad_out[0], segment_ids)
    return grad_query[None], grad_input[None], grad_weight


def solution(mesh):
    spread = P("dp", ("outer", "inner"), None)
    sizes = (mesh.shape["dp"], mesh.shape["outer"], mesh.shape["inner"])
    return jax.shard_map(
        functools.partial(on_device, sizes),
        mesh=mesh,
        in_specs=(spread, spread, P(), spread, P("dp", ("outer", "inner"))),
        out_specs=(spread, spread, P(("outer", "inner"), None)),
        check_vma=False,
    )
```

```python
import functools
import math

import jax
import jax.numpy as jnp
from jax import lax
from jax.experimental import pallas as pl
from jax.experimental.pallas import tpu as pltpu
from jax.sharding import PartitionSpec as P

MESH = pl.DeviceIdType.MESH
HEADS = 8
GROUPS = 2
PER_GROUP = HEADS // GROUPS
HEAD = 128
TOK = 192
PAIR = 2 * TOK
SENT = TOK + 16
HALF = 2 * HEAD
TILES = PAIR // 8
WIDTH = 2 * GROUPS * HEAD
MODEL = HEADS * HEAD
SPAN = 5
HERE = 2
FACTOR = HEAD**-0.5
LOG2E = math.log2(math.e)
FAR = -1e30
F32 = jnp.float32
BF16 = jnp.bfloat16


def product(left, right, left_dim, right_dim):
    return lax.dot_general(
        left, right, (((left_dim,), (right_dim,)), ((), ())), preferred_element_type=F32
    )


def thrice(rows):
    return jnp.concatenate([rows, rows, rows], axis=1)


def remote(source, target, send, recv, device):
    return pltpu.make_async_remote_copy(
        src_ref=source, dst_ref=target, send_sem=send, recv_sem=recv,
        device_id=device, device_id_type=MESH,
    )


def kernel(
    n_dp, n_outer, n_inner,
    q_hbm, in_hbm, w_hbm, up_hbm, ids_ref,
    dq_out, dx_out, gw_ref,
    raw, rows_in, rows_sib, rows_turned, weight, queries, upstream,
    window, ids_query, mask, scores, grads, peak, total, dots, grad_query,
    own, sib_out, sib_in, ring_out, ring_in, grad_kv, grad_kv_sib,
    part, row_out, row_in, col_out, col_in, mine, dp_buf,
    load_sem,
    halo_send, halo_recv, rows_send, rows_recv, sib_send, sib_recv, ring_send, ring_recv,
    pair_send, pair_recv, row_send, row_recv, col_send, col_recv, dp_send, dp_recv,
):
    n_x = n_inner // 2
    chips = n_outer * n_x
    dp = lax.axis_index("dp")
    outer = lax.axis_index("outer")
    inner = lax.axis_index("inner")
    x, core = inner // 2, inner % 2
    chip = outer * n_x + x

    def chip_at(steps):
        there = lax.rem(chip + steps + chips, chips)
        return (dp, there // n_x, lax.rem(there, n_x) * 2 + core)

    sibling = (dp, outer, x * 2 + 1 - core)
    right, left = chip_at(1), chip_at(-1)
    row_order = sorted(range(1, n_x), key=lambda s: -min(s, n_x - s))
    row_peers = [(dp, outer, lax.rem(x + s, n_x) * 2 + core) for s in row_order]
    n_y = n_outer // 2
    z, y = outer // n_y, outer % n_y
    col_order = sorted(
        ((sz, sy) for sy in range(n_y) for sz in range(2) if sy or sz),
        key=lambda s: (-min(s[1], n_y - s[1]), -s[0], s[1]),
    )
    col_at = [lax.rem(z + sz, 2) * n_y + lax.rem(y + sy, n_y) for sz, sy in col_order]
    col_peers = [(dp, at, inner) for at in col_at]
    dp_peers = [
        (s, flip, (lax.rem(dp + s, n_dp), outer, x * 2 + (1 - core if flip else core)))
        for s in range(n_dp)
        for flip in (0, 1)
        if s or flip
    ]
    peers = [right, left] + row_peers + col_peers + [peer for _, _, peer in dp_peers]

    barrier = pltpu.get_barrier_semaphore()
    for peer in peers:
        pl.semaphore_signal(barrier, inc=1, device_id=peer, device_id_type=MESH)

    loads = [
        pltpu.make_async_copy(source, target, load_sem.at[i])
        for i, (source, target) in enumerate(
            [(in_hbm, rows_in), (w_hbm, weight), (q_hbm, raw.at[0]), (up_hbm, raw.at[1])]
        )
    ]
    for load in loads:
        load.start()

    ids_row = ids_ref[...].astype(F32)
    twice = jnp.concatenate([ids_row, ids_row, jnp.zeros((1, 2 * HALF - PAIR), F32)], axis=1)
    first_row = lax.broadcasted_iota(jnp.int32, (SENT - TOK, HALF), 0) == 0
    window[HERE, 0, 0, TOK:SENT, :] = jnp.where(
        first_row, twice[:, :HALF], twice[:, HALF:]
    ).astype(BF16)
    ids_query[...] = jnp.broadcast_to(twice[:, :PAIR], (8, PAIR))

    pl.semaphore_wait(barrier, len(peers))
    loads[0].wait()
    rows_copy = remote(rows_in, rows_sib, rows_send, rows_recv, sibling)
    rows_copy.start()
    loads[1].wait()
    key_value = product(rows_in[...], weight[...], 1, 0).astype(BF16)
    for g in range(GROUPS):
        window[HERE, 0, g, 0:TOK, :HEAD] = key_value[:, g * HEAD : (g + 1) * HEAD]
        window[HERE, 0, g, 0:TOK, HEAD:] = key_value[
            :, (GROUPS + g) * HEAD : (GROUPS + g + 1) * HEAD
        ]
    halo = []
    for g in range(GROUPS):
        rows = pl.ds(0, TOK if g else SENT)
        for i, (source, target, device) in enumerate(
            [
                ((2, 0), (2, 1), sibling),
                ((2, 0), (1, 0), right),
                ((2, 0), (3, 0), left),
                ((1, 0), (0, 0), right),
                ((3, 0), (4, 0), left),
                ((1, 0), (1, 1), sibling),
                ((3, 0), (3, 1), sibling),
                ((0, 0), (0, 1), sibling),
                ((4, 0), (4, 1), sibling),
            ]
        ):
            halo.append(
                remote(
                    window.at[source[0], source[1], g, rows],
                    window.at[target[0], target[1], g, rows],
                    halo_send.at[9 * g + i], halo_recv.at[9 * g + i], device,
                )
            )
    for g in range(GROUPS):
        for i in (1, 2, 0):
            halo[9 * g + i].start()

    loads[2].wait()
    loads[3].wait()
    for h in range(HEADS):
        g, member = h // PER_GROUP, h % PER_GROUP
        at = slice(h * HEAD, (h + 1) * HEAD)
        queries[g, member * TOK : (member + 1) * TOK, :] = raw[0, :, at]
        upstream[g, member * TOK : (member + 1) * TOK, :] = raw[1, :, at]

    def of_chunk(j, g, at):
        return jnp.concatenate([window[j, 0, g, 0:TOK, at], window[j, 1, g, 0:TOK, at]], axis=0)

    keys_at, values_at = slice(0, HEAD), slice(HEAD, HALF)

    def make_mask(j):
        lane = lax.broadcasted_iota(jnp.int32, (1, PAIR), 1)
        near, far = (
            jnp.concatenate([ids[0:1], ids[1:2, : PAIR - HALF]], axis=1)
            for ids in (window[j, side, 0, TOK:SENT, :].astype(F32) for side in (0, 1))
        )
        ids_key = jnp.where(lane < TOK, near, far)
        ids_col = jnp.transpose(jnp.broadcast_to(ids_key, (HEAD, PAIR)))
        mask[j] = jnp.where(thrice(ids_col) == ids_query[0:1, :], 0.0, FAR)

    def first_pass(j, g, opening):
        keys, values = of_chunk(j, g, keys_at), of_chunk(j, g, values_at)
        for b in range(2):
            at = slice(b * PAIR, (b + 1) * PAIR)
            score = product(keys, queries[g, at, :], 1, 1) * (FACTOR * LOG2E) + mask[j]
            grad = product(values, upstream[g, at, :], 1, 1)
            scores[j, g, b] = score
            grads[j, g, b] = grad
            score = score.reshape(TILES, 8, PAIR)
            top = jnp.max(score, axis=0)
            if not opening:
                before = peak[g, b]
                top = jnp.maximum(before, top)
            weights = jnp.exp2(score - top[None])
            dot = jnp.sum(weights * grad.reshape(TILES, 8, PAIR), axis=0)
            weights = jnp.sum(weights, axis=0)
            if not opening:
                scale = jnp.exp2(before - top)
                weights = weights + total[g, b] * scale
                dot = dot + dots[g, b] * scale
            peak[g, b] = top
            total[g, b] = weights
            dots[g, b] = dot

    def both(visit, first, stride):
        def step(t, carry):
            visit(first + stride * t)
            return carry

        lax.fori_loop(0, 2, step, 0)

    def merge(g):
        for b in range(2):
            top = jnp.max(peak[g, b], axis=0, keepdims=True)
            scale = jnp.exp2(peak[g, b] - top)
            weights = jnp.sum(total[g, b] * scale, axis=0, keepdims=True)
            dot = jnp.sum(dots[g, b] * scale, axis=0, keepdims=True) / weights
            peak[g, b] = jnp.broadcast_to(top + jnp.log(weights) * LOG2E, (8, PAIR))
            dots[g, b] = jnp.broadcast_to(dot, (8, PAIR))

    def second_pass(j, g, opening):
        keys = of_chunk(j, g, keys_at)
        key, value = 0.0, 0.0
        for b in range(2):
            at = slice(b * PAIR, (b + 1) * PAIR)
            probs = jnp.exp2(scores[j, g, b].reshape(TILES, 8, PAIR) - peak[g, b][None])
            low = probs.reshape(PAIR, PAIR).astype(BF16)
            grad = probs * (grads[j, g, b].reshape(TILES, 8, PAIR) - dots[g, b][None])
            grad = grad.reshape(PAIR, PAIR).astype(BF16)
            key = key + product(grad, queries[g, at, :], 1, 0)
            value = value + product(low, upstream[g, at, :], 1, 0)
            query = product(keys, grad, 0, 0)
            grad_query[g, b] = query if opening else grad_query[g, b] + query
        key = key * FACTOR
        own[j, g, :, :HEAD] = key[:TOK]
        own[j, g, :, HEAD:] = value[:TOK]
        sib_out[j, g, :, :HEAD] = key[TOK:].astype(BF16)
        sib_out[j, g, :, HEAD:] = value[TOK:].astype(BF16)

    sib = [
        [
            remote(
                sib_out.at[j, g], sib_in.at[j, g],
                sib_send.at[GROUPS * j + g], sib_recv.at[GROUPS * j + g], sibling,
            )
            for g in range(GROUPS)
        ]
        for j in range(SPAN)
    ]
    ring = [
        [
            remote(
                ring_out.at[i, g], ring_in.at[i, g],
                ring_send.at[GROUPS * i + g], ring_recv.at[GROUPS * i + g], device,
            )
            for g in range(GROUPS)
        ]
        for i, device in enumerate([left, right, left, right])
    ]

    def turn_inputs():
        rows_copy.wait_recv()

        def turn(i, carry):
            at = pl.ds(pl.multiple_of(i * 128, 128), 128)
            rows = jnp.concatenate([rows_in[:, at], rows_sib[:, at]], axis=0)
            rows_turned[at, :] = jnp.transpose(rows)
            return carry

        lax.fori_loop(0, MODEL // 128, turn, 0)

    def near_arrived(g):
        halo[9 * g + 1].wait_recv()
        halo[9 * g + 3].start()
        halo[9 * g + 2].wait_recv()
        halo[9 * g + 4].start()
        halo[9 * g + 5].start()
        halo[9 * g + 6].start()

    def distant_arrived(g):
        halo[9 * g + 3].wait_recv()
        halo[9 * g + 7].start()
        halo[9 * g + 4].wait_recv()
        halo[9 * g + 8].start()

    def send_distant(g):
        for i, j in enumerate((0, 4)):
            sib[j][g].wait_recv()
            ring_out[i, g] = (own[j, g] + sib_in[j, g].astype(F32)).astype(BF16)
            ring[i][g].start()

    def send_near(g):
        for i, j in enumerate((1, 3)):
            sib[j][g].wait_recv()
            ring[i][g].wait_recv()
            ring_out[2 + i, g] = (
                own[j, g] + sib_in[j, g].astype(F32) + ring_in[i, g].astype(F32)
            ).astype(BF16)
            ring[2 + i][g].start()

    halo[0].wait_recv()
    make_mask(HERE)
    first_pass(HERE, 0, True)
    halo[9].wait_recv()
    first_pass(HERE, 1, True)

    turn_inputs()
    near_arrived(0)
    halo[5].wait_recv()
    halo[6].wait_recv()
    both(make_mask, 1, 2)
    both(lambda j: first_pass(j, 0, False), 1, 2)
    near_arrived(1)
    halo[14].wait_recv()
    halo[15].wait_recv()
    both(lambda j: first_pass(j, 1, False), 1, 2)

    distant_arrived(0)
    halo[7].wait_recv()
    halo[8].wait_recv()
    both(make_mask, 0, 4)
    both(lambda j: first_pass(j, 0, False), 0, 4)
    merge(0)
    grad_query[...] = jnp.zeros_like(grad_query)
    distant_arrived(1)
    both(lambda j: second_pass(j, 0, False), 0, 4)
    sib[0][0].start()
    sib[4][0].start()
    halo[16].wait_recv()
    halo[17].wait_recv()
    both(lambda j: first_pass(j, 1, False), 0, 4)
    send_distant(0)
    merge(1)
    both(lambda j: second_pass(j, 1, False), 0, 4)
    sib[0][1].start()
    sib[4][1].start()
    both(lambda j: second_pass(j, 0, False), 1, 2)
    sib[1][0].start()
    sib[3][0].start()
    send_distant(1)
    send_near(0)
    both(lambda j: second_pass(j, 1, False), 1, 2)
    sib[1][1].start()
    sib[3][1].start()
    second_pass(HERE, 0, False)
    sib[2][0].start()
    send_near(1)
    second_pass(HERE, 1, False)
    sib[2][1].start()

    pair = [
        remote(
            grad_kv.at[g, 1 - core], grad_kv_sib.at[g], pair_send.at[g], pair_recv.at[g], sibling
        )
        for g in range(GROUPS)
    ]
    row = [
        [
            remote(
                row_out.at[g, i], row_in.at[g, i],
                row_send.at[(n_x - 1) * g + i], row_recv.at[(n_x - 1) * g + i], row_peers[i],
            )
            for i in range(n_x - 1)
        ]
        for g in range(GROUPS)
    ]
    col = [
        [
            remote(
                col_out.at[g, col_at[i]], col_in.at[g, i],
                col_send.at[(n_outer - 1) * g + i], col_recv.at[(n_outer - 1) * g + i],
                col_peers[i],
            )
            for i in range(n_outer - 1)
        ]
        for g in range(GROUPS)
    ]

    def finish_kv(g):
        sib[2][g].wait_recv()
        ring[2][g].wait_recv()
        ring[3][g].wait_recv()
        whole = (
            own[2, g] + sib_in[2, g].astype(F32)
            + ring_in[2, g].astype(F32) + ring_in[3, g].astype(F32)
        ).astype(BF16)
        grad_kv[g, 0] = whole[:, :HEAD]
        grad_kv[g, 1] = whole[:, HEAD:]
        pair[g].start()

    def row_first(g):
        pair[g].wait_recv()
        both_kv = jnp.concatenate([grad_kv[g, core], grad_kv_sib[g]], axis=0)
        part[g] = product(rows_turned[...], both_kv, 1, 0).reshape(n_outer, n_x, 16, HEAD)
        for i, s in enumerate(row_order):
            row_out[g, i] = part[g, :, lax.rem(x + s, n_x)].astype(BF16)
            row[g][i].start()

    def row_last(g):
        share = part[g, :, x]
        for i in range(n_x - 1):
            row[g][i].wait_recv()
            share = share + row_in[g, i].astype(F32)
        part[g, :, x] = share
        col_out[g] = share.astype(BF16)
        for copy in col[g]:
            copy.start()

    def col_last(g):
        share = part[g, outer, x]
        for s, copy in enumerate(col[g]):
            copy.wait_recv()
            share = share + col_in[g, s].astype(F32)
        mine[0, g] = share[:8]
        mine[1, g] = share[8:]

    finish_kv(0)
    for g in range(GROUPS):
        for b in range(2):
            rows = jnp.transpose(grad_query[g, b]) * FACTOR
            for m in range(2):
                h = g * PER_GROUP + 2 * b + m
                dq_out[:, h * HEAD : (h + 1) * HEAD] = rows[m * TOK : (m + 1) * TOK].astype(BF16)
    row_first(0)
    finish_kv(1)
    row_first(1)
    row_last(0)
    kv_rows = jnp.concatenate(
        [grad_kv[0, 0], grad_kv[1, 0], grad_kv[0, 1], grad_kv[1, 1]], axis=1
    )
    dx_out[...] = product(kv_rows, weight[...], 1, 1).astype(BF16)
    row_last(1)
    col_last(0)
    col_last(1)

    last = []
    for i, (s, flip, peer) in enumerate(dp_peers):
        copy = remote(
            mine.at[1 - core if flip else core], dp_buf.at[dp, core],
            dp_send.at[i], dp_recv.at[i], peer,
        )
        copy.start()
        last.append(copy)
    dp_buf[dp, core] = mine[core]
    for copy in last:
        copy.wait_recv()
    for kind in range(2):
        whole = dp_buf[0, kind]
        for r in range(1, n_dp):
            whole = whole + dp_buf[r, kind]
        for g in range(GROUPS):
            at = kind * GROUPS + g
            gw_ref[:, at * HEAD : (at + 1) * HEAD] = whole[g]

    for copy in halo + sum(sib, []) + sum(ring, []) + [rows_copy] + pair + sum(row, []) + sum(col, []) + last:
        copy.wait_send()


PARTS = 4


def place(*refs):
    count = len(refs) // 2
    sems = refs[-1]
    copies = []
    for source, target in zip(refs[:count], refs[count:-1]):
        rows = source.shape[0] // PARTS if source.shape[0] == TOK else source.shape[0]
        for start in range(0, source.shape[0], rows):
            at = pl.ds(start, rows)
            copies.append(
                pltpu.make_async_copy(source.at[at], target.at[at], sems.at[len(copies)])
            )
    for copy in copies:
        copy.start()
    for copy in copies:
        copy.wait()


def on_device(sizes, queries, inputs, kv_weight, grad_out, segment_ids):
    n_dp, n_outer, n_inner = sizes
    n_x = n_inner // 2
    vmem, dma = pltpu.VMEM, pltpu.SemaphoreType.DMA
    anywhere = pl.BlockSpec(memory_space=pl.ANY)
    inside = pl.BlockSpec(memory_space=pltpu.VMEM)
    tokens = jax.ShapeDtypeStruct((TOK, MODEL), BF16)
    shapes = (tokens, tokens, jax.ShapeDtypeStruct((8, WIDTH), F32))
    results = pl.pallas_call(
        functools.partial(kernel, *sizes),
        out_shape=tuple(pltpu.VMEM(leaf.shape, leaf.dtype) for leaf in shapes),
        in_specs=[anywhere] * 4 + [inside],
        out_specs=(inside,) * 3,
        scratch_shapes=[
            vmem((2, TOK, MODEL), BF16),
            vmem((TOK, MODEL), BF16),
            vmem((TOK, MODEL), BF16),
            vmem((MODEL, PAIR), BF16),
            vmem((MODEL, WIDTH), BF16),
            vmem((GROUPS, PER_GROUP * TOK, HEAD), BF16),
            vmem((GROUPS, PER_GROUP * TOK, HEAD), BF16),
            vmem((SPAN, 2, GROUPS, SENT, HALF), BF16),
            vmem((8, PAIR), F32),
            vmem((SPAN, PAIR, PAIR), F32),
            vmem((SPAN, GROUPS, 2, PAIR, PAIR), F32),
            vmem((SPAN, GROUPS, 2, PAIR, PAIR), F32),
            vmem((GROUPS, 2, 8, PAIR), F32),
            vmem((GROUPS, 2, 8, PAIR), F32),
            vmem((GROUPS, 2, 8, PAIR), F32),
            vmem((GROUPS, 2, HEAD, PAIR), F32),
            vmem((SPAN, GROUPS, TOK, HALF), F32),
            vmem((SPAN, GROUPS, TOK, HALF), BF16),
            vmem((SPAN, GROUPS, TOK, HALF), BF16),
            vmem((4, GROUPS, TOK, HALF), BF16),
            vmem((4, GROUPS, TOK, HALF), BF16),
            vmem((GROUPS, 2, TOK, HEAD), BF16),
            vmem((GROUPS, TOK, HEAD), BF16),
            vmem((GROUPS, n_outer, n_x, 16, HEAD), F32),
            vmem((GROUPS, n_x - 1, n_outer, 16, HEAD), BF16),
            vmem((GROUPS, n_x - 1, n_outer, 16, HEAD), BF16),
            vmem((GROUPS, n_outer, 16, HEAD), BF16),
            vmem((GROUPS, n_outer - 1, 16, HEAD), BF16),
            vmem((2, GROUPS, 8, HEAD), F32),
            vmem((n_dp, 2, GROUPS, 8, HEAD), F32),
            dma((4,)),
            dma((18,)), dma((18,)), dma, dma, dma((10,)), dma((10,)), dma((8,)), dma((8,)),
            dma((2,)), dma((2,)), dma((2 * (n_x - 1),)), dma((2 * (n_x - 1),)),
            dma((2 * (n_outer - 1),)), dma((2 * (n_outer - 1),)), dma((2 * n_dp - 1,)), dma((2 * n_dp - 1,)),
        ],
        compiler_params=pltpu.CompilerParams(
            collective_id=0, has_side_effects=True, vmem_limit_bytes=56 * 2**20
        ),
    )(queries[0], inputs[0], kv_weight, grad_out[0], segment_ids)
    grad_query, grad_input, grad_weight = pl.pallas_call(
        place,
        out_shape=shapes,
        in_specs=[inside] * 3,
        out_specs=(anywhere,) * 3,
        scratch_shapes=[dma((2 * PARTS + 1,))],
    )(*results)
    return grad_query[None], grad_input[None], grad_weight


def solution(mesh):
    spread = P("dp", ("outer", "inner"), None)
    sizes = (mesh.shape["dp"], mesh.shape["outer"], mesh.shape["inner"])
    return jax.shard_map(
        functools.partial(on_device, sizes),
        mesh=mesh,
        in_specs=(spread, spread, P(), spread, P("dp", ("outer", "inner"))),
        out_specs=(spread, spread, P(("outer", "inner"), None)),
        check_vma=False,
    )
```

```python
import functools
import math

import jax
import jax.numpy as jnp
from jax import lax
from jax.experimental import pallas as pl
from jax.experimental.pallas import tpu as pltpu
from jax.sharding import PartitionSpec as P

MESH = pl.DeviceIdType.MESH
HEADS = 8
GROUPS = 2
PER_GROUP = HEADS // GROUPS
HEAD = 128
TOK = 192
PAIR = 2 * TOK
SENT = TOK + 16
HALF = 2 * HEAD
TILES = PAIR // 8
WIDTH = 2 * GROUPS * HEAD
MODEL = HEADS * HEAD
SPAN = 5
HERE = 2
FACTOR = HEAD**-0.5
LOG2E = math.log2(math.e)
FAR = -1e30
F32 = jnp.float32
BF16 = jnp.bfloat16


def product(left, right, left_dim, right_dim):
    return lax.dot_general(
        left, right, (((left_dim,), (right_dim,)), ((), ())), preferred_element_type=F32
    )


def thrice(rows):
    return jnp.concatenate([rows, rows, rows], axis=1)


def remote(source, target, send, recv, device):
    return pltpu.make_async_remote_copy(
        src_ref=source, dst_ref=target, send_sem=send, recv_sem=recv,
        device_id=device, device_id_type=MESH,
    )


def kernel(
    n_dp, n_outer, n_inner,
    q_hbm, in_hbm, w_hbm, up_hbm, ids_ref,
    dq_out, dx_out, gw_ref,
    raw, rows_in, rows_sib, rows_turned, weight, queries, upstream,
    window, ids_query, mask, scores, grads, peak, total, dots, grad_query,
    own, sib_out, sib_in, ring_out, ring_in, grad_kv, grad_kv_sib,
    part, row_out, row_in, col_out, col_in, mine, dp_buf,
    load_sem,
    halo_send, halo_recv, rows_send, rows_recv, sib_send, sib_recv, ring_send, ring_recv,
    pair_send, pair_recv, row_send, row_recv, col_send, col_recv, dp_send, dp_recv,
):
    n_x = n_inner // 2
    chips = n_outer * n_x
    dp = lax.axis_index("dp")
    outer = lax.axis_index("outer")
    inner = lax.axis_index("inner")
    x, core = inner // 2, inner % 2
    chip = outer * n_x + x

    def chip_at(steps):
        there = lax.rem(chip + steps + chips, chips)
        return (dp, there // n_x, lax.rem(there, n_x) * 2 + core)

    sibling = (dp, outer, x * 2 + 1 - core)
    right, left = chip_at(1), chip_at(-1)
    row_order = sorted(range(1, n_x), key=lambda s: -min(s, n_x - s))
    row_peers = [(dp, outer, lax.rem(x + s, n_x) * 2 + core) for s in row_order]
    n_y = n_outer // 2
    z, y = outer // n_y, outer % n_y
    col_order = sorted(
        ((sz, sy) for sy in range(n_y) for sz in range(2) if sy or sz),
        key=lambda s: (-min(s[1], n_y - s[1]), -s[0], s[1]),
    )
    col_at = [lax.rem(z + sz, 2) * n_y + lax.rem(y + sy, n_y) for sz, sy in col_order]
    col_peers = [(dp, at, inner) for at in col_at]
    dp_peers = [
        (s, flip, (lax.rem(dp + s, n_dp), outer, x * 2 + (1 - core if flip else core)))
        for s in range(n_dp)
        for flip in (0, 1)
        if s or flip
    ]
    peers = [peer for _, _, peer in dp_peers] + col_peers + row_peers + [right, left]

    blocks = [(g + GROUPS * kind) * HEAD for g in range(GROUPS) for kind in range(2)]
    loads = [
        pltpu.make_async_copy(source, target, load_sem.at[i])
        for i, (source, target) in enumerate(
            [(in_hbm, rows_in)]
            + [(w_hbm.at[:, pl.ds(at, HEAD)], weight.at[:, pl.ds(at, HEAD)]) for at in blocks]
            + [(q_hbm, raw.at[0]), (up_hbm, raw.at[1])]
        )
    ]
    for load in loads:
        load.start()

    barrier = pltpu.get_barrier_semaphore()
    for peer in peers:
        pl.semaphore_signal(barrier, inc=1, device_id=peer, device_id_type=MESH)

    ids_row = ids_ref[...].astype(F32)
    twice = jnp.concatenate([ids_row, ids_row, jnp.zeros((1, 2 * HALF - PAIR), F32)], axis=1)
    first_row = lax.broadcasted_iota(jnp.int32, (SENT - TOK, HALF), 0) == 0
    window[HERE, 0, 0, TOK:SENT, :] = jnp.where(
        first_row, twice[:, :HALF], twice[:, HALF:]
    ).astype(BF16)
    ids_query[...] = jnp.broadcast_to(twice[:, :PAIR], (8, PAIR))

    pl.semaphore_wait(barrier, len(peers))
    loads[0].wait()
    rows_copy = remote(rows_in, rows_sib, rows_send, rows_recv, sibling)
    rows_copy.start()
    halo = []
    for g in range(GROUPS):
        rows = pl.ds(0, TOK if g else SENT)
        for i, (source, target, device) in enumerate(
            [
                ((2, 0), (2, 1), sibling),
                ((2, 0), (1, 0), right),
                ((2, 0), (3, 0), left),
                ((1, 0), (0, 0), right),
                ((3, 0), (4, 0), left),
                ((1, 0), (1, 1), sibling),
                ((3, 0), (3, 1), sibling),
                ((0, 0), (0, 1), sibling),
                ((4, 0), (4, 1), sibling),
            ]
        ):
            halo.append(
                remote(
                    window.at[source[0], source[1], g, rows],
                    window.at[target[0], target[1], g, rows],
                    halo_send.at[9 * g + i], halo_recv.at[9 * g + i], device,
                )
            )
    for g in range(GROUPS):
        loads[1 + 2 * g].wait()
        loads[2 + 2 * g].wait()
        columns = jnp.concatenate(
            [weight[:, at : at + HEAD] for at in blocks[2 * g : 2 * g + 2]], axis=1
        )
        window[HERE, 0, g, 0:TOK, :] = product(rows_in[...], columns, 1, 0).astype(BF16)
        for i in (1, 2, 0):
            halo[9 * g + i].start()

    loads[5].wait()
    loads[6].wait()
    for h in range(HEADS):
        g, member = h // PER_GROUP, h % PER_GROUP
        at = slice(h * HEAD, (h + 1) * HEAD)
        queries[g, member * TOK : (member + 1) * TOK, :] = raw[0, :, at]
        upstream[g, member * TOK : (member + 1) * TOK, :] = raw[1, :, at]

    def of_chunk(j, g, at):
        return jnp.concatenate([window[j, 0, g, 0:TOK, at], window[j, 1, g, 0:TOK, at]], axis=0)

    keys_at, values_at = slice(0, HEAD), slice(HEAD, HALF)

    def make_mask(j):
        lane = lax.broadcasted_iota(jnp.int32, (1, PAIR), 1)
        near, far = (
            jnp.concatenate([ids[0:1], ids[1:2, : PAIR - HALF]], axis=1)
            for ids in (window[j, side, 0, TOK:SENT, :].astype(F32) for side in (0, 1))
        )
        ids_key = jnp.where(lane < TOK, near, far)
        ids_col = jnp.transpose(jnp.broadcast_to(ids_key, (HEAD, PAIR)))
        mask[j] = jnp.where(thrice(ids_col) == ids_query[0:1, :], 0.0, FAR)

    def first_pass(j, g, opening):
        keys, values = of_chunk(j, g, keys_at), of_chunk(j, g, values_at)
        for b in range(2):
            at = slice(b * PAIR, (b + 1) * PAIR)
            score = product(keys, queries[g, at, :], 1, 1) * (FACTOR * LOG2E) + mask[j]
            grad = product(values, upstream[g, at, :], 1, 1)
            scores[j, g, b] = score
            grads[j, g, b] = grad
            score = score.reshape(TILES, 8, PAIR)
            top = jnp.max(score, axis=0)
            if not opening:
                before = peak[g, b]
                top = jnp.maximum(before, top)
            weights = jnp.exp2(score - top[None])
            dot = jnp.sum(weights * grad.reshape(TILES, 8, PAIR), axis=0)
            weights = jnp.sum(weights, axis=0)
            if not opening:
                scale = jnp.exp2(before - top)
                weights = weights + total[g, b] * scale
                dot = dot + dots[g, b] * scale
            peak[g, b] = top
            total[g, b] = weights
            dots[g, b] = dot

    def both(visit, first, stride):
        def step(t, carry):
            visit(first + stride * t)
            return carry

        lax.fori_loop(0, 2, step, 0)

    def merge(g):
        for b in range(2):
            top = jnp.max(peak[g, b], axis=0, keepdims=True)
            scale = jnp.exp2(peak[g, b] - top)
            weights = jnp.sum(total[g, b] * scale, axis=0, keepdims=True)
            dot = jnp.sum(dots[g, b] * scale, axis=0, keepdims=True) / weights
            peak[g, b] = jnp.broadcast_to(top + jnp.log(weights) * LOG2E, (8, PAIR))
            dots[g, b] = jnp.broadcast_to(dot, (8, PAIR))

    def second_pass(j, g, opening):
        keys = of_chunk(j, g, keys_at)
        key, value = 0.0, 0.0
        for b in range(2):
            at = slice(b * PAIR, (b + 1) * PAIR)
            probs = jnp.exp2(scores[j, g, b].reshape(TILES, 8, PAIR) - peak[g, b][None])
            low = probs.reshape(PAIR, PAIR).astype(BF16)
            grad = probs * (grads[j, g, b].reshape(TILES, 8, PAIR) - dots[g, b][None])
            grad = grad.reshape(PAIR, PAIR).astype(BF16)
            key = key + product(grad, queries[g, at, :], 1, 0)
            value = value + product(low, upstream[g, at, :], 1, 0)
            query = product(keys, grad, 0, 0)
            grad_query[g, b] = query if opening else grad_query[g, b] + query
        key = key * FACTOR
        own[j, g, :, :HEAD] = key[:TOK]
        own[j, g, :, HEAD:] = value[:TOK]
        sib_out[j, g, :, :HEAD] = key[TOK:].astype(BF16)
        sib_out[j, g, :, HEAD:] = value[TOK:].astype(BF16)

    def to_sibling(j, g):
        at = GROUPS * j + g
        return remote(sib_out.at[j, g], sib_in.at[j, g], sib_send.at[at], sib_recv.at[at], sibling)

    sib = [[to_sibling(j, g) for g in range(GROUPS)] for j in range(SPAN)]
    ring = [
        [
            remote(
                ring_out.at[i, g], ring_in.at[i, g],
                ring_send.at[GROUPS * i + g], ring_recv.at[GROUPS * i + g], device,
            )
            for g in range(GROUPS)
        ]
        for i, device in enumerate([left, right, left, right])
    ]

    def turn_inputs():
        rows_copy.wait_recv()

        def turn(i, carry):
            at = pl.ds(pl.multiple_of(i * 128, 128), 128)
            rows = jnp.concatenate([rows_in[:, at], rows_sib[:, at]], axis=0)
            rows_turned[at, :] = jnp.transpose(rows)
            return carry

        lax.fori_loop(0, MODEL // 128, turn, 0)

    def near_arrived(g):
        halo[9 * g + 1].wait_recv()
        halo[9 * g + 3].start()
        halo[9 * g + 2].wait_recv()
        halo[9 * g + 4].start()
        halo[9 * g + 5].start()
        halo[9 * g + 6].start()

    def distant_arrived(g):
        halo[9 * g + 3].wait_recv()
        halo[9 * g + 7].start()
        halo[9 * g + 4].wait_recv()
        halo[9 * g + 8].start()

    def send_distant(g):
        for i, j in enumerate((0, 4)):
            sib[j][g].wait_recv()
            ring_out[i, g] = (own[j, g] + sib_in[j, g].astype(F32)).astype(BF16)
            ring[i][g].start()

    def send_near(g):
        for i, j in enumerate((1, 3)):
            sib[j][g].wait_recv()
            ring[i][g].wait_recv()
            ring_out[2 + i, g] = (
                own[j, g] + sib_in[j, g].astype(F32) + ring_in[i, g].astype(F32)
            ).astype(BF16)
            ring[2 + i][g].start()

    halo[0].wait_recv()
    make_mask(HERE)
    first_pass(HERE, 0, True)
    halo[9].wait_recv()
    first_pass(HERE, 1, True)

    turn_inputs()
    near_arrived(0)
    halo[5].wait_recv()
    halo[6].wait_recv()
    both(make_mask, 1, 2)
    both(lambda j: first_pass(j, 0, False), 1, 2)
    near_arrived(1)
    halo[14].wait_recv()
    halo[15].wait_recv()
    both(lambda j: first_pass(j, 1, False), 1, 2)

    def distant(g):
        def step(t, carry):
            j = 4 * t
            rows = pl.ds(0, TOK if g else SENT)
            remote(
                window.at[j, 0, g, rows], window.at[j, 1, g, rows],
                halo_send.at[9 * g + 7 + t], halo_recv.at[9 * g + 7 + t], sibling,
            ).wait_recv()
            if not g:
                make_mask(j)
            first_pass(j, g, False)
            return carry

        lax.fori_loop(0, 2, step, 0)
        merge(g)

    def second_and_send(j, g):
        second_pass(j, g, False)
        to_sibling(j, g).start()

    grad_query[...] = jnp.zeros_like(grad_query)
    distant_arrived(0)
    distant(0)
    distant_arrived(1)
    both(lambda j: second_and_send(j, 0), 0, 4)
    distant(1)
    send_distant(0)
    both(lambda j: second_and_send(j, 1), 0, 4)
    second_and_send(1, 0)
    send_distant(1)
    second_and_send(3, 0)
    second_and_send(1, 1)
    send_near(0)
    second_and_send(3, 1)
    second_and_send(HERE, 0)
    send_near(1)
    second_and_send(HERE, 1)

    pair = [
        remote(
            grad_kv.at[g, 1 - core], grad_kv_sib.at[g], pair_send.at[g], pair_recv.at[g], sibling
        )
        for g in range(GROUPS)
    ]
    row = [
        [
            remote(
                row_out.at[g, i], row_in.at[g, i],
                row_send.at[(n_x - 1) * g + i], row_recv.at[(n_x - 1) * g + i], row_peers[i],
            )
            for i in range(n_x - 1)
        ]
        for g in range(GROUPS)
    ]
    col = [
        [
            remote(
                col_out.at[g, col_at[i]], col_in.at[g, i],
                col_send.at[(n_outer - 1) * g + i], col_recv.at[(n_outer - 1) * g + i],
                col_peers[i],
            )
            for i in range(n_outer - 1)
        ]
        for g in range(GROUPS)
    ]

    def finish_kv(g):
        sib[2][g].wait_recv()
        ring[2][g].wait_recv()
        ring[3][g].wait_recv()
        whole = (
            own[2, g] + sib_in[2, g].astype(F32)
            + ring_in[2, g].astype(F32) + ring_in[3, g].astype(F32)
        ).astype(BF16)
        grad_kv[g, 0] = whole[:, :HEAD]
        grad_kv[g, 1] = whole[:, HEAD:]
        pair[g].start()

    def row_first(g):
        pair[g].wait_recv()
        both_kv = jnp.concatenate([grad_kv[g, core], grad_kv_sib[g]], axis=0)
        part[g] = product(rows_turned[...], both_kv, 1, 0).reshape(n_outer, n_x, 16, HEAD)
        for i, s in enumerate(row_order):
            row_out[g, i] = part[g, :, lax.rem(x + s, n_x)].astype(BF16)
            row[g][i].start()

    def row_last(g):
        share = part[g, :, x]
        for i in range(n_x - 1):
            row[g][i].wait_recv()
            share = share + row_in[g, i].astype(F32)
        part[g, :, x] = share
        col_out[g] = share.astype(BF16)
        for copy in col[g]:
            copy.start()

    def col_last(g):
        share = part[g, outer, x]
        for s, copy in enumerate(col[g]):
            copy.wait_recv()
            share = share + col_in[g, s].astype(F32)
        mine[0, g] = share[:8]
        mine[1, g] = share[8:]

    finish_kv(0)
    for g in range(GROUPS):
        for b in range(2):
            rows = jnp.transpose(grad_query[g, b]) * FACTOR
            for m in range(2):
                h = g * PER_GROUP + 2 * b + m
                dq_out[:, h * HEAD : (h + 1) * HEAD] = rows[m * TOK : (m + 1) * TOK].astype(BF16)
    row_first(0)
    finish_kv(1)
    row_first(1)
    row_last(0)
    kv_rows = jnp.concatenate(
        [grad_kv[0, 0], grad_kv[1, 0], grad_kv[0, 1], grad_kv[1, 1]], axis=1
    )
    dx_out[...] = product(kv_rows, weight[...], 1, 1).astype(BF16)
    row_last(1)
    col_last(0)
    col_last(1)

    last = []
    for i, (s, flip, peer) in enumerate(dp_peers):
        copy = remote(
            mine.at[1 - core if flip else core], dp_buf.at[dp, core],
            dp_send.at[i], dp_recv.at[i], peer,
        )
        copy.start()
        last.append(copy)
    dp_buf[dp, core] = mine[core]
    for copy in last:
        copy.wait_recv()
    for kind in range(2):
        whole = dp_buf[0, kind]
        for r in range(1, n_dp):
            whole = whole + dp_buf[r, kind]
        for g in range(GROUPS):
            at = kind * GROUPS + g
            gw_ref[:, at * HEAD : (at + 1) * HEAD] = whole[g]

    for copy in halo + sum(sib, []) + sum(ring, []) + [rows_copy] + pair + sum(row, []) + sum(col, []) + last:
        copy.wait_send()


PARTS = 4


def place(*refs):
    count = len(refs) // 2
    sems = refs[-1]
    copies = []
    for source, target in zip(refs[:count], refs[count:-1]):
        rows = source.shape[0] // PARTS if source.shape[0] == TOK else source.shape[0]
        for start in range(0, source.shape[0], rows):
            at = pl.ds(start, rows)
            copies.append(
                pltpu.make_async_copy(source.at[at], target.at[at], sems.at[len(copies)])
            )
    for copy in copies:
        copy.start()
    for copy in copies:
        copy.wait()


def on_device(sizes, queries, inputs, kv_weight, grad_out, segment_ids):
    n_dp, n_outer, n_inner = sizes
    n_x = n_inner // 2
    vmem, dma = pltpu.VMEM, pltpu.SemaphoreType.DMA
    anywhere = pl.BlockSpec(memory_space=pl.ANY)
    inside = pl.BlockSpec(memory_space=pltpu.VMEM)
    tokens = jax.ShapeDtypeStruct((TOK, MODEL), BF16)
    shapes = (tokens, tokens, jax.ShapeDtypeStruct((8, WIDTH), F32))
    results = pl.pallas_call(
        functools.partial(kernel, *sizes),
        out_shape=tuple(pltpu.VMEM(leaf.shape, leaf.dtype) for leaf in shapes),
        in_specs=[anywhere] * 4 + [inside],
        out_specs=(inside,) * 3,
        scratch_shapes=[
            vmem((2, TOK, MODEL), BF16),
            vmem((TOK, MODEL), BF16),
            vmem((TOK, MODEL), BF16),
            vmem((MODEL, PAIR), BF16),
            vmem((MODEL, WIDTH), BF16),
            vmem((GROUPS, PER_GROUP * TOK, HEAD), BF16),
            vmem((GROUPS, PER_GROUP * TOK, HEAD), BF16),
            vmem((SPAN, 2, GROUPS, SENT, HALF), BF16),
            vmem((8, PAIR), F32),
            vmem((SPAN, PAIR, PAIR), F32),
            vmem((SPAN, GROUPS, 2, PAIR, PAIR), F32),
            vmem((SPAN, GROUPS, 2, PAIR, PAIR), F32),
            vmem((GROUPS, 2, 8, PAIR), F32),
            vmem((GROUPS, 2, 8, PAIR), F32),
            vmem((GROUPS, 2, 8, PAIR), F32),
            vmem((GROUPS, 2, HEAD, PAIR), F32),
            vmem((SPAN, GROUPS, TOK, HALF), F32),
            vmem((SPAN, GROUPS, TOK, HALF), BF16),
            vmem((SPAN, GROUPS, TOK, HALF), BF16),
            vmem((4, GROUPS, TOK, HALF), BF16),
            vmem((4, GROUPS, TOK, HALF), BF16),
            vmem((GROUPS, 2, TOK, HEAD), BF16),
            vmem((GROUPS, TOK, HEAD), BF16),
            vmem((GROUPS, n_outer, n_x, 16, HEAD), F32),
            vmem((GROUPS, n_x - 1, n_outer, 16, HEAD), BF16),
            vmem((GROUPS, n_x - 1, n_outer, 16, HEAD), BF16),
            vmem((GROUPS, n_outer, 16, HEAD), BF16),
            vmem((GROUPS, n_outer - 1, 16, HEAD), BF16),
            vmem((2, GROUPS, 8, HEAD), F32),
            vmem((n_dp, 2, GROUPS, 8, HEAD), F32),
            dma((7,)),
            dma((18,)), dma((18,)), dma, dma, dma((10,)), dma((10,)), dma((8,)), dma((8,)),
            dma((2,)), dma((2,)), dma((2 * (n_x - 1),)), dma((2 * (n_x - 1),)),
            dma((2 * (n_outer - 1),)), dma((2 * (n_outer - 1),)), dma((2 * n_dp - 1,)), dma((2 * n_dp - 1,)),
        ],
        compiler_params=pltpu.CompilerParams(
            collective_id=0, has_side_effects=True, vmem_limit_bytes=56 * 2**20
        ),
    )(queries[0], inputs[0], kv_weight, grad_out[0], segment_ids)
    grad_query, grad_input, grad_weight = pl.pallas_call(
        place,
        out_shape=shapes,
        in_specs=[inside] * 3,
        out_specs=(anywhere,) * 3,
        scratch_shapes=[dma((2 * PARTS + 1,))],
    )(*results)
    return grad_query[None], grad_input[None], grad_weight


def solution(mesh):
    spread = P("dp", ("outer", "inner"), None)
    sizes = (mesh.shape["dp"], mesh.shape["outer"], mesh.shape["inner"])
    return jax.shard_map(
        functools.partial(on_device, sizes),
        mesh=mesh,
        in_specs=(spread, spread, P(), spread, P("dp", ("outer", "inner"))),
        out_specs=(spread, spread, P(("outer", "inner"), None)),
        check_vma=False,
    )
```

```python
import functools
import math

import jax
import jax.numpy as jnp
from jax import lax
from jax.experimental import pallas as pl
from jax.experimental.pallas import tpu as pltpu
from jax.sharding import PartitionSpec as P

MESH = pl.DeviceIdType.MESH
HEADS = 8
GROUPS = 2
PER_GROUP = HEADS // GROUPS
HEAD = 128
TOK = 192
PAIR = 2 * TOK
SENT = TOK + 16
HALF = 2 * HEAD
TILES = PAIR // 8
WIDTH = 2 * GROUPS * HEAD
MODEL = HEADS * HEAD
SPAN = 5
HERE = 2
FACTOR = HEAD**-0.5
LOG2E = math.log2(math.e)
FAR = -1e30
F32 = jnp.float32
BF16 = jnp.bfloat16


def product(left, right, left_dim, right_dim):
    return lax.dot_general(
        left, right, (((left_dim,), (right_dim,)), ((), ())), preferred_element_type=F32
    )


def thrice(rows):
    return jnp.concatenate([rows, rows, rows], axis=1)


def remote(source, target, send, recv, device):
    return pltpu.make_async_remote_copy(
        src_ref=source, dst_ref=target, send_sem=send, recv_sem=recv,
        device_id=device, device_id_type=MESH,
    )


def kernel(
    n_dp, n_outer, n_inner,
    q_hbm, in_hbm, w_hbm, up_hbm, ids_ref,
    dq_out, dx_out, gw_ref,
    raw, rows_in, rows_sib, rows_turned, weight, queries, upstream,
    window, ids_query, mask, scores, grads, peak, total, dots, grad_query,
    own, sib_out, sib_in, here_out, far_out, far_in, near_out, near_in, kv_pair, kv_own,
    part, row_out, row_in, col_out, col_in, mine, dp_buf,
    load_sem,
    halo_send, halo_recv, rows_send, rows_recv, sib_send, sib_recv,
    far_send, far_recv, near_send, near_recv,
    pair_send, pair_recv, row_send, row_recv, col_send, col_recv, dp_send, dp_recv,
):
    n_x = n_inner // 2
    chips = n_outer * n_x
    dp = lax.axis_index("dp")
    outer = lax.axis_index("outer")
    inner = lax.axis_index("inner")
    x, core = inner // 2, inner % 2
    chip = outer * n_x + x

    def chip_at(steps, at_core):
        there = lax.rem(chip + steps + chips, chips)
        return (dp, there // n_x, lax.rem(there, n_x) * 2 + at_core)

    sibling = (dp, outer, x * 2 + 1 - core)
    right, left = chip_at(1, core), chip_at(-1, core)
    across = [chip_at(1, 1 - core), chip_at(-1, 1 - core)]
    row_order = sorted(range(1, n_x), key=lambda s: -min(s, n_x - s))
    row_peers = [(dp, outer, lax.rem(x + s, n_x) * 2 + core) for s in row_order]
    n_y = n_outer // 2
    z, y = outer // n_y, outer % n_y
    col_order = sorted(
        ((sz, sy) for sy in range(n_y) for sz in range(2) if sy or sz),
        key=lambda s: (-min(s[1], n_y - s[1]), -s[0], s[1]),
    )
    col_at = [lax.rem(z + sz, 2) * n_y + lax.rem(y + sy, n_y) for sz, sy in col_order]
    col_peers = [(dp, at, inner) for at in col_at]
    dp_peers = [
        (s, flip, (lax.rem(dp + s, n_dp), outer, x * 2 + (1 - core if flip else core)))
        for s in range(n_dp)
        for flip in (0, 1)
        if s or flip
    ]
    peers = [peer for _, _, peer in dp_peers] + col_peers + row_peers + across + [right, left]

    blocks = [(g + GROUPS * kind) * HEAD for g in range(GROUPS) for kind in range(2)]
    loads = [
        pltpu.make_async_copy(source, target, load_sem.at[i])
        for i, (source, target) in enumerate(
            [(in_hbm, rows_in)]
            + [(w_hbm.at[:, pl.ds(at, HEAD)], weight.at[:, pl.ds(at, HEAD)]) for at in blocks]
            + [(q_hbm, raw.at[0]), (up_hbm, raw.at[1])]
        )
    ]
    for load in loads:
        load.start()

    barrier = pltpu.get_barrier_semaphore()
    for peer in peers:
        pl.semaphore_signal(barrier, inc=1, device_id=peer, device_id_type=MESH)

    ids_row = ids_ref[...].astype(F32)
    twice = jnp.concatenate([ids_row, ids_row, jnp.zeros((1, 2 * HALF - PAIR), F32)], axis=1)
    first_row = lax.broadcasted_iota(jnp.int32, (SENT - TOK, HALF), 0) == 0
    window[HERE, 0, 0, TOK:SENT, :] = jnp.where(
        first_row, twice[:, :HALF], twice[:, HALF:]
    ).astype(BF16)
    ids_query[...] = jnp.broadcast_to(twice[:, :PAIR], (8, PAIR))

    pl.semaphore_wait(barrier, len(peers))
    loads[0].wait()
    rows_copy = remote(rows_in, rows_sib, rows_send, rows_recv, sibling)
    rows_copy.start()
    halo = []
    for g in range(GROUPS):
        rows = pl.ds(0, TOK if g else SENT)
        for i, (source, target, device) in enumerate(
            [
                ((2, 0), (2, 1), sibling),
                ((2, 0), (1, 0), right),
                ((2, 0), (3, 0), left),
                ((1, 0), (0, 0), right),
                ((3, 0), (4, 0), left),
                ((1, 0), (1, 1), sibling),
                ((3, 0), (3, 1), sibling),
                ((0, 0), (0, 1), sibling),
                ((4, 0), (4, 1), sibling),
            ]
        ):
            halo.append(
                remote(
                    window.at[source[0], source[1], g, rows],
                    window.at[target[0], target[1], g, rows],
                    halo_send.at[9 * g + i], halo_recv.at[9 * g + i], device,
                )
            )
    for g in range(GROUPS):
        loads[1 + 2 * g].wait()
        loads[2 + 2 * g].wait()
        columns = jnp.concatenate(
            [weight[:, at : at + HEAD] for at in blocks[2 * g : 2 * g + 2]], axis=1
        )
        window[HERE, 0, g, 0:TOK, :] = product(rows_in[...], columns, 1, 0).astype(BF16)
        for i in (1, 2, 0):
            halo[9 * g + i].start()

    loads[5].wait()
    loads[6].wait()
    for h in range(HEADS):
        g, member = h // PER_GROUP, h % PER_GROUP
        at = slice(h * HEAD, (h + 1) * HEAD)
        queries[g, member * TOK : (member + 1) * TOK, :] = raw[0, :, at]
        upstream[g, member * TOK : (member + 1) * TOK, :] = raw[1, :, at]

    def of_chunk(j, g, at):
        return jnp.concatenate([window[j, 0, g, 0:TOK, at], window[j, 1, g, 0:TOK, at]], axis=0)

    keys_at, values_at = slice(0, HEAD), slice(HEAD, HALF)

    def make_mask(j):
        lane = lax.broadcasted_iota(jnp.int32, (1, PAIR), 1)
        near, far = (
            jnp.concatenate([ids[0:1], ids[1:2, : PAIR - HALF]], axis=1)
            for ids in (window[j, side, 0, TOK:SENT, :].astype(F32) for side in (0, 1))
        )
        ids_key = jnp.where(lane < TOK, near, far)
        ids_col = jnp.transpose(jnp.broadcast_to(ids_key, (HEAD, PAIR)))
        mask[j] = jnp.where(thrice(ids_col) == ids_query[0:1, :], 0.0, FAR)

    def first_pass(j, g, opening):
        keys, values = of_chunk(j, g, keys_at), of_chunk(j, g, values_at)
        for b in range(2):
            at = slice(b * PAIR, (b + 1) * PAIR)
            score = product(keys, queries[g, at, :], 1, 1) * (FACTOR * LOG2E) + mask[j]
            grad = product(values, upstream[g, at, :], 1, 1)
            scores[j, g, b] = score
            grads[j, g, b] = grad
            score = score.reshape(TILES, 8, PAIR)
            top = jnp.max(score, axis=0)
            if not opening:
                before = peak[g, b]
                top = jnp.maximum(before, top)
            weights = jnp.exp2(score - top[None])
            dot = jnp.sum(weights * grad.reshape(TILES, 8, PAIR), axis=0)
            weights = jnp.sum(weights, axis=0)
            if not opening:
                scale = jnp.exp2(before - top)
                weights = weights + total[g, b] * scale
                dot = dot + dots[g, b] * scale
            peak[g, b] = top
            total[g, b] = weights
            dots[g, b] = dot

    def both(visit, first, stride):
        def step(t, carry):
            visit(first + stride * t)
            return carry

        lax.fori_loop(0, 2, step, 0)

    def merge(g):
        for b in range(2):
            top = jnp.max(peak[g, b], axis=0, keepdims=True)
            scale = jnp.exp2(peak[g, b] - top)
            weights = jnp.sum(total[g, b] * scale, axis=0, keepdims=True)
            dot = jnp.sum(dots[g, b] * scale, axis=0, keepdims=True) / weights
            peak[g, b] = jnp.broadcast_to(top + jnp.log(weights) * LOG2E, (8, PAIR))
            dots[g, b] = jnp.broadcast_to(dot, (8, PAIR))

    def second_pass(j, g, opening):
        keys = of_chunk(j, g, keys_at)
        key, value = 0.0, 0.0
        for b in range(2):
            at = slice(b * PAIR, (b + 1) * PAIR)
            probs = jnp.exp2(scores[j, g, b].reshape(TILES, 8, PAIR) - peak[g, b][None])
            low = probs.reshape(PAIR, PAIR).astype(BF16)
            grad = probs * (grads[j, g, b].reshape(TILES, 8, PAIR) - dots[g, b][None])
            grad = grad.reshape(PAIR, PAIR).astype(BF16)
            key = key + product(grad, queries[g, at, :], 1, 0)
            value = value + product(low, upstream[g, at, :], 1, 0)
            query = product(keys, grad, 0, 0)
            grad_query[g, b] = query if opening else grad_query[g, b] + query
        key = key * FACTOR
        own[j, g, 0] = key[:TOK]
        own[j, g, 1] = value[:TOK]
        sib_out[j, g, 0] = key[TOK:].astype(BF16)
        sib_out[j, g, 1] = value[TOK:].astype(BF16)

    def to_sibling(j, g):
        at = GROUPS * j + g
        return remote(sib_out.at[j, g], sib_in.at[j, g], sib_send.at[at], sib_recv.at[at], sibling)

    sib = [[to_sibling(j, g) for g in range(GROUPS)] for j in range(SPAN)]
    far = [
        [
            [
                remote(
                    far_out.at[i, g, kind], far_in.at[i, g, kind],
                    far_send.at[4 * i + 2 * g + kind], far_recv.at[4 * i + 2 * g + kind], device,
                )
                for kind in range(2)
            ]
            for g in range(GROUPS)
        ]
        for i, device in enumerate([left, right])
    ]

    def to_neighbour(i, g, kind):
        side = lax.rem(core + kind, 2)
        return remote(
            near_out.at[i, g, kind], near_in.at[i, g, side],
            near_send.at[4 * i + 2 * g + kind], near_recv.at[4 * i + 2 * g + side],
            chip_at(2 * i - 1, kind),
        )

    near = [
        [[to_neighbour(i, g, kind) for kind in range(2)] for g in range(GROUPS)] for i in range(2)
    ]
    here = [
        remote(
            here_out.at[g], sib_in.at[HERE, g],
            sib_send.at[GROUPS * HERE + g], sib_recv.at[GROUPS * HERE + g], sibling,
        )
        for g in range(GROUPS)
    ]
    swap = [
        remote(
            kv_pair.at[g, pl.ds(TOK, TOK)], kv_own.at[core, g],
            pair_send.at[g], pair_recv.at[g], sibling,
        )
        for g in range(GROUPS)
    ]

    def turn_inputs():
        rows_copy.wait_recv()

        def turn(i, carry):
            at = pl.ds(pl.multiple_of(i * 128, 128), 128)
            rows = jnp.concatenate([rows_in[:, at], rows_sib[:, at]], axis=0)
            rows_turned[at, :] = jnp.transpose(rows)
            return carry

        lax.fori_loop(0, MODEL // 128, turn, 0)

    def near_arrived(g):
        halo[9 * g + 1].wait_recv()
        halo[9 * g + 3].start()
        halo[9 * g + 2].wait_recv()
        halo[9 * g + 4].start()
        halo[9 * g + 5].start()
        halo[9 * g + 6].start()

    def distant_arrived(g):
        halo[9 * g + 3].wait_recv()
        halo[9 * g + 7].start()
        halo[9 * g + 4].wait_recv()
        halo[9 * g + 8].start()

    def send_distant(g):
        for i, j in enumerate((0, 4)):
            sib[j][g].wait_recv()
            for kind in range(2):
                far_out[i, g, kind] = (
                    own[j, g, kind] + sib_in[j, g, kind].astype(F32)
                ).astype(BF16)
                far[i][g][kind].start()

    def send_near(g):
        for i, j in enumerate((1, 3)):
            sib[j][g].wait_recv()
        for kind in range(2):
            for i, j in enumerate((1, 3)):
                far[i][g][kind].wait_recv()
                near_out[i, g, kind] = (
                    own[j, g, kind] + sib_in[j, g, kind].astype(F32)
                    + far_in[i, g, kind].astype(F32)
                ).astype(BF16)
                near[i][g][kind].start()

    def send_here(g):
        second_pass(HERE, g, False)
        here_out[g, 0] = own[HERE, g, 1 - core].astype(BF16)
        here_out[g, 1] = sib_out[HERE, g, 1 - core]
        here[g].start()

    halo[0].wait_recv()
    make_mask(HERE)
    first_pass(HERE, 0, True)
    halo[9].wait_recv()
    first_pass(HERE, 1, True)

    turn_inputs()
    near_arrived(0)
    halo[5].wait_recv()
    halo[6].wait_recv()
    both(make_mask, 1, 2)
    both(lambda j: first_pass(j, 0, False), 1, 2)
    near_arrived(1)
    halo[14].wait_recv()
    halo[15].wait_recv()
    both(lambda j: first_pass(j, 1, False), 1, 2)

    def distant(g):
        def step(t, carry):
            j = 4 * t
            rows = pl.ds(0, TOK if g else SENT)
            remote(
                window.at[j, 0, g, rows], window.at[j, 1, g, rows],
                halo_send.at[9 * g + 7 + t], halo_recv.at[9 * g + 7 + t], sibling,
            ).wait_recv()
            if not g:
                make_mask(j)
            first_pass(j, g, False)
            return carry

        lax.fori_loop(0, 2, step, 0)
        merge(g)

    def second_and_send(j, g):
        second_pass(j, g, False)
        to_sibling(j, g).start()

    grad_query[...] = jnp.zeros_like(grad_query)
    distant_arrived(0)
    distant(0)
    distant_arrived(1)
    both(lambda j: second_and_send(j, 0), 0, 4)
    distant(1)
    send_distant(0)
    both(lambda j: second_and_send(j, 1), 0, 4)
    second_and_send(1, 0)
    send_distant(1)
    second_and_send(3, 0)
    second_and_send(1, 1)
    send_near(0)
    second_and_send(3, 1)
    send_here(0)
    send_near(1)
    send_here(1)

    row = [
        [
            remote(
                row_out.at[g, i], row_in.at[g, i],
                row_send.at[(n_x - 1) * g + i], row_recv.at[(n_x - 1) * g + i], row_peers[i],
            )
            for i in range(n_x - 1)
        ]
        for g in range(GROUPS)
    ]
    col = [
        [
            remote(
                col_out.at[g, col_at[i]], col_in.at[g, i],
                col_send.at[(n_outer - 1) * g + i], col_recv.at[(n_outer - 1) * g + i],
                col_peers[i],
            )
            for i in range(n_outer - 1)
        ]
        for g in range(GROUPS)
    ]

    def finish_kv(g):
        here[g].wait_recv()
        for i in range(2):
            for side in range(2):
                remote(
                    near_out.at[i, g, side], near_in.at[i, g, side],
                    near_send.at[4 * i + 2 * g + side], near_recv.at[4 * i + 2 * g + side], right,
                ).wait_recv()
        mine_kv = own[HERE, g, core] + sib_in[HERE, g, 1].astype(F32)
        sib_kv = sib_out[HERE, g, core].astype(F32) + sib_in[HERE, g, 0].astype(F32)
        for i in range(2):
            mine_kv = mine_kv + near_in[i, g, 0].astype(F32)
            sib_kv = sib_kv + near_in[i, g, 1].astype(F32)
        mine_kv = mine_kv.astype(BF16)
        kv_own[core, g] = mine_kv
        kv_pair[g, 0:TOK, :] = mine_kv
        kv_pair[g, TOK:PAIR, :] = sib_kv.astype(BF16)
        swap[g].start()

    def row_first(g):
        whole = product(rows_turned[...], kv_pair[g], 1, 0)
        part[g] = whole.reshape(n_outer, n_x, 16, HEAD)
        for i, s in enumerate(row_order):
            row_out[g, i] = part[g, :, lax.rem(x + s, n_x)].astype(BF16)
            row[g][i].start()

    def row_last(g):
        share = part[g, :, x]
        for i in range(n_x - 1):
            row[g][i].wait_recv()
            share = share + row_in[g, i].astype(F32)
        part[g, :, x] = share
        col_out[g] = share.astype(BF16)
        for copy in col[g]:
            copy.start()

    def col_last(g):
        share = part[g, outer, x]
        for s, copy in enumerate(col[g]):
            copy.wait_recv()
            share = share + col_in[g, s].astype(F32)
        mine[0, g] = share[:8]
        mine[1, g] = share[8:]

    finish_kv(0)
    for g in range(GROUPS):
        for b in range(2):
            rows = jnp.transpose(grad_query[g, b]) * FACTOR
            for m in range(2):
                h = g * PER_GROUP + 2 * b + m
                dq_out[:, h * HEAD : (h + 1) * HEAD] = rows[m * TOK : (m + 1) * TOK].astype(BF16)
    row_first(0)
    finish_kv(1)
    row_first(1)
    row_last(0)
    for g in range(GROUPS):
        swap[g].wait_recv()
    kv_rows = jnp.concatenate(
        [kv_own[kind, g] for kind in range(2) for g in range(GROUPS)], axis=1
    )
    dx_out[...] = product(kv_rows, weight[...], 1, 1).astype(BF16)
    row_last(1)
    col_last(0)
    col_last(1)

    last = []
    for i, (s, flip, peer) in enumerate(dp_peers):
        copy = remote(
            mine.at[1 - core if flip else core], dp_buf.at[dp, core],
            dp_send.at[i], dp_recv.at[i], peer,
        )
        copy.start()
        last.append(copy)
    dp_buf[dp, core] = mine[core]
    for copy in last:
        copy.wait_recv()
    for kind in range(2):
        whole = dp_buf[0, kind]
        for r in range(1, n_dp):
            whole = whole + dp_buf[r, kind]
        for g in range(GROUPS):
            at = kind * GROUPS + g
            gw_ref[:, at * HEAD : (at + 1) * HEAD] = whole[g]

    others = [copy for j in range(SPAN) if j != HERE for copy in sib[j]]
    by_kind = [copy for group in far + near for kinds in group for copy in kinds]
    for copy in halo + others + by_kind + here + swap + [rows_copy] + sum(row + col, []) + last:
        copy.wait_send()


PARTS = 4


def place(*refs):
    count = len(refs) // 2
    sems = refs[-1]
    copies = []
    for source, target in zip(refs[:count], refs[count:-1]):
        rows = source.shape[0] // PARTS if source.shape[0] == TOK else source.shape[0]
        for start in range(0, source.shape[0], rows):
            at = pl.ds(start, rows)
            copies.append(
                pltpu.make_async_copy(source.at[at], target.at[at], sems.at[len(copies)])
            )
    for copy in copies:
        copy.start()
    for copy in copies:
        copy.wait()


def on_device(sizes, queries, inputs, kv_weight, grad_out, segment_ids):
    n_dp, n_outer, n_inner = sizes
    n_x = n_inner // 2
    vmem, dma = pltpu.VMEM, pltpu.SemaphoreType.DMA
    anywhere = pl.BlockSpec(memory_space=pl.ANY)
    inside = pl.BlockSpec(memory_space=pltpu.VMEM)
    tokens = jax.ShapeDtypeStruct((TOK, MODEL), BF16)
    shapes = (tokens, tokens, jax.ShapeDtypeStruct((8, WIDTH), F32))
    results = pl.pallas_call(
        functools.partial(kernel, *sizes),
        out_shape=tuple(pltpu.VMEM(leaf.shape, leaf.dtype) for leaf in shapes),
        in_specs=[anywhere] * 4 + [inside],
        out_specs=(inside,) * 3,
        scratch_shapes=[
            vmem((2, TOK, MODEL), BF16),
            vmem((TOK, MODEL), BF16),
            vmem((TOK, MODEL), BF16),
            vmem((MODEL, PAIR), BF16),
            vmem((MODEL, WIDTH), BF16),
            vmem((GROUPS, PER_GROUP * TOK, HEAD), BF16),
            vmem((GROUPS, PER_GROUP * TOK, HEAD), BF16),
            vmem((SPAN, 2, GROUPS, SENT, HALF), BF16),
            vmem((8, PAIR), F32),
            vmem((SPAN, PAIR, PAIR), F32),
            vmem((SPAN, GROUPS, 2, PAIR, PAIR), F32),
            vmem((SPAN, GROUPS, 2, PAIR, PAIR), F32),
            vmem((GROUPS, 2, 8, PAIR), F32),
            vmem((GROUPS, 2, 8, PAIR), F32),
            vmem((GROUPS, 2, 8, PAIR), F32),
            vmem((GROUPS, 2, HEAD, PAIR), F32),
            vmem((SPAN, GROUPS, 2, TOK, HEAD), F32),
            vmem((SPAN, GROUPS, 2, TOK, HEAD), BF16),
            vmem((SPAN, GROUPS, 2, TOK, HEAD), BF16),
            vmem((GROUPS, 2, TOK, HEAD), BF16),
            vmem((2, GROUPS, 2, TOK, HEAD), BF16),
            vmem((2, GROUPS, 2, TOK, HEAD), BF16),
            vmem((2, GROUPS, 2, TOK, HEAD), BF16),
            vmem((2, GROUPS, 2, TOK, HEAD), BF16),
            vmem((GROUPS, PAIR, HEAD), BF16),
            vmem((2, GROUPS, TOK, HEAD), BF16),
            vmem((GROUPS, n_outer, n_x, 16, HEAD), F32),
            vmem((GROUPS, n_x - 1, n_outer, 16, HEAD), BF16),
            vmem((GROUPS, n_x - 1, n_outer, 16, HEAD), BF16),
            vmem((GROUPS, n_outer, 16, HEAD), BF16),
            vmem((GROUPS, n_outer - 1, 16, HEAD), BF16),
            vmem((2, GROUPS, 8, HEAD), F32),
            vmem((n_dp, 2, GROUPS, 8, HEAD), F32),
            dma((7,)),
            dma((18,)), dma((18,)), dma, dma, dma((10,)), dma((10,)),
            dma((8,)), dma((8,)), dma((8,)), dma((8,)),
            dma((2,)), dma((2,)), dma((2 * (n_x - 1),)), dma((2 * (n_x - 1),)),
            dma((2 * (n_outer - 1),)), dma((2 * (n_outer - 1),)), dma((2 * n_dp - 1,)), dma((2 * n_dp - 1,)),
        ],
        compiler_params=pltpu.CompilerParams(
            collective_id=0, has_side_effects=True, vmem_limit_bytes=56 * 2**20
        ),
    )(queries[0], inputs[0], kv_weight, grad_out[0], segment_ids)
    grad_query, grad_input, grad_weight = pl.pallas_call(
        place,
        out_shape=shapes,
        in_specs=[inside] * 3,
        out_specs=(anywhere,) * 3,
        scratch_shapes=[dma((2 * PARTS + 1,))],
    )(*results)
    return grad_query[None], grad_input[None], grad_weight


def solution(mesh):
    spread = P("dp", ("outer", "inner"), None)
    sizes = (mesh.shape["dp"], mesh.shape["outer"], mesh.shape["inner"])
    return jax.shard_map(
        functools.partial(on_device, sizes),
        mesh=mesh,
        in_specs=(spread, spread, P(), spread, P("dp", ("outer", "inner"))),
        out_specs=(spread, spread, P(("outer", "inner"), None)),
        check_vma=False,
    )
```

```python
import functools
import math

import jax
import jax.numpy as jnp
from jax import lax
from jax.experimental import pallas as pl
from jax.experimental.pallas import tpu as pltpu
from jax.sharding import PartitionSpec as P

MESH = pl.DeviceIdType.MESH
HEADS = 8
GROUPS = 2
PER_GROUP = HEADS // GROUPS
HEAD = 128
TOK = 192
PAIR = 2 * TOK
SENT = TOK + 16
HALF = 2 * HEAD
WIDTH = 2 * GROUPS * HEAD
MODEL = HEADS * HEAD
SPAN = 5
HERE = 2
FACTOR = HEAD**-0.5
LOG2E = math.log2(math.e)
FAR = -1e30
F32 = jnp.float32
BF16 = jnp.bfloat16


def product(left, right, left_dim, right_dim):
    return lax.dot_general(
        left, right, (((left_dim,), (right_dim,)), ((), ())), preferred_element_type=F32
    )


def thrice(rows):
    return jnp.concatenate([rows, rows, rows], axis=1)


def remote(source, target, send, recv, device):
    return pltpu.make_async_remote_copy(
        src_ref=source, dst_ref=target, send_sem=send, recv_sem=recv,
        device_id=device, device_id_type=MESH,
    )


def kernel(
    n_dp, n_outer, n_inner,
    q_hbm, in_hbm, w_hbm, up_hbm, ids_ref,
    dq_out, dx_out, gw_ref,
    raw, rows_in, rows_sib, rows_turned, weight, queries, upstream,
    window, ids_query, mask, scores, grads, peak, total, dots, grad_query,
    own, sib_out, sib_in, here_out, far_out, far_in, near_out, near_in, kv_pair, kv_own,
    part, row_out, row_in, col_out, col_in, mine, dp_buf,
    load_sem,
    halo_send, halo_recv, rows_send, rows_recv, sib_send, sib_recv,
    far_send, far_recv, near_send, near_recv,
    pair_send, pair_recv, row_send, row_recv, col_send, col_recv, dp_send, dp_recv,
):
    n_x = n_inner // 2
    chips = n_outer * n_x
    dp = lax.axis_index("dp")
    outer = lax.axis_index("outer")
    inner = lax.axis_index("inner")
    x, core = inner // 2, inner % 2
    chip = outer * n_x + x

    def chip_at(steps, at_core):
        there = lax.rem(chip + steps + chips, chips)
        return (dp, there // n_x, lax.rem(there, n_x) * 2 + at_core)

    sibling = (dp, outer, x * 2 + 1 - core)
    right, left = chip_at(1, core), chip_at(-1, core)
    across = [chip_at(1, 1 - core), chip_at(-1, 1 - core)]
    row_order = sorted(range(1, n_x), key=lambda s: -min(s, n_x - s))
    row_peers = [(dp, outer, lax.rem(x + s, n_x) * 2 + core) for s in row_order]
    n_y = n_outer // 2
    z, y = outer // n_y, outer % n_y
    col_order = sorted(
        ((sz, sy) for sy in range(n_y) for sz in range(2) if sy or sz),
        key=lambda s: (-min(s[1], n_y - s[1]), -s[0], s[1]),
    )
    col_at = [lax.rem(z + sz, 2) * n_y + lax.rem(y + sy, n_y) for sz, sy in col_order]
    col_peers = [(dp, at, inner) for at in col_at]
    dp_peers = [
        (s, flip, (lax.rem(dp + s, n_dp), outer, x * 2 + (1 - core if flip else core)))
        for s in range(n_dp)
        for flip in (0, 1)
        if s or flip
    ]
    peers = [peer for _, _, peer in dp_peers] + col_peers + row_peers + across + [right, left]

    blocks = [(g + GROUPS * kind) * HEAD for g in range(GROUPS) for kind in range(2)]
    loads = [
        pltpu.make_async_copy(source, target, load_sem.at[i])
        for i, (source, target) in enumerate(
            [(in_hbm, rows_in)]
            + [(w_hbm.at[:, pl.ds(at, HEAD)], weight.at[:, pl.ds(at, HEAD)]) for at in blocks]
            + [(q_hbm, raw.at[0]), (up_hbm, raw.at[1])]
        )
    ]
    for load in loads:
        load.start()

    barrier = pltpu.get_barrier_semaphore()
    for peer in peers:
        pl.semaphore_signal(barrier, inc=1, device_id=peer, device_id_type=MESH)

    ids_row = ids_ref[...].astype(F32)
    twice = jnp.concatenate([ids_row, ids_row, jnp.zeros((1, 2 * HALF - PAIR), F32)], axis=1)
    first_row = lax.broadcasted_iota(jnp.int32, (SENT - TOK, HALF), 0) == 0
    window[HERE, 0, 0, TOK:SENT, :] = jnp.where(
        first_row, twice[:, :HALF], twice[:, HALF:]
    ).astype(BF16)
    ids_query[...] = jnp.broadcast_to(twice[:, :PAIR], (8, PAIR))

    pl.semaphore_wait(barrier, len(peers))
    loads[0].wait()
    rows_copy = remote(rows_in, rows_sib, rows_send, rows_recv, sibling)
    rows_copy.start()
    far_whole, far_half = 4 * core, 4 * (1 - core)

    halo = []
    for g in range(GROUPS):
        rows = pl.ds(0, TOK if g else SENT)
        for i, (source, target, device) in enumerate(
            [
                ((2, 0), (2, 1), sibling),
                ((2, 0), (1, 0), right),
                ((2, 0), (3, 0), left),
                ((1, 0), (0, 0), right),
                ((3, 0), (4, 0), left),
                ((1, 0), (1, 1), sibling),
                ((3, 0), (3, 1), sibling),
                ((far_half, 0), (far_half, 1), sibling),
            ]
        ):
            halo.append(
                remote(
                    window.at[source[0], source[1], g, rows],
                    window.at[target[0], target[1], g, rows],
                    halo_send.at[8 * g + i], halo_recv.at[8 * g + i], device,
                )
            )
    for g in range(GROUPS):
        loads[1 + 2 * g].wait()
        loads[2 + 2 * g].wait()
        columns = jnp.concatenate(
            [weight[:, at : at + HEAD] for at in blocks[2 * g : 2 * g + 2]], axis=1
        )
        window[HERE, 0, g, 0:TOK, :] = product(rows_in[...], columns, 1, 0).astype(BF16)
        for i in (1, 2, 0):
            halo[8 * g + i].start()

    loads[5].wait()
    loads[6].wait()
    for h in range(HEADS):
        g, member = h // PER_GROUP, h % PER_GROUP
        at = slice(h * HEAD, (h + 1) * HEAD)
        queries[g, member * TOK : (member + 1) * TOK, :] = raw[0, :, at]
        upstream[g, member * TOK : (member + 1) * TOK, :] = raw[1, :, at]

    def of_chunk(j, g, at, whole=True):
        if not whole:
            return window[j, 0, g, 0:TOK, at]
        return jnp.concatenate([window[j, 0, g, 0:TOK, at], window[j, 1, g, 0:TOK, at]], axis=0)

    keys_at, values_at = slice(0, HEAD), slice(HEAD, HALF)

    def make_mask(j, whole=True):
        count = PAIR if whole else TOK
        lane = lax.broadcasted_iota(jnp.int32, (1, PAIR), 1)
        near, far = (
            jnp.concatenate([ids[0:1], ids[1:2, : PAIR - HALF]], axis=1)
            for ids in (
                window[j, side, 0, TOK:SENT, :].astype(F32) for side in (0, 1 if whole else 0)
            )
        )
        ids_key = jnp.where(lane < TOK, near, far)
        ids_col = jnp.transpose(jnp.broadcast_to(ids_key, (HEAD, PAIR)))
        mask[j, 0:count, :] = jnp.where(
            thrice(ids_col[:count]) == ids_query[0:1, :], 0.0, FAR
        )

    def first_pass(j, g, opening, whole=True):
        count = PAIR if whole else TOK
        keys, values = of_chunk(j, g, keys_at, whole), of_chunk(j, g, values_at, whole)
        for b in range(2):
            at = slice(b * PAIR, (b + 1) * PAIR)
            score = product(keys, queries[g, at, :], 1, 1) * (FACTOR * LOG2E)
            score = score + mask[j, 0:count, :]
            grad = product(values, upstream[g, at, :], 1, 1)
            scores[j, g, b, 0:count, :] = score
            grads[j, g, b, 0:count, :] = grad
            score = score.reshape(count // 8, 8, PAIR)
            top = jnp.max(score, axis=0)
            if not opening:
                before = peak[g, b]
                top = jnp.maximum(before, top)
            weights = jnp.exp2(score - top[None])
            dot = jnp.sum(weights * grad.reshape(count // 8, 8, PAIR), axis=0)
            weights = jnp.sum(weights, axis=0)
            if not opening:
                scale = jnp.exp2(before - top)
                weights = weights + total[g, b] * scale
                dot = dot + dots[g, b] * scale
            peak[g, b] = top
            total[g, b] = weights
            dots[g, b] = dot

    def both(visit, first, stride):
        def step(t, carry):
            visit(first + stride * t)
            return carry

        lax.fori_loop(0, 2, step, 0)

    def merge(g):
        for b in range(2):
            top = jnp.max(peak[g, b], axis=0, keepdims=True)
            scale = jnp.exp2(peak[g, b] - top)
            weights = jnp.sum(total[g, b] * scale, axis=0, keepdims=True)
            dot = jnp.sum(dots[g, b] * scale, axis=0, keepdims=True) / weights
            peak[g, b] = jnp.broadcast_to(top + jnp.log(weights) * LOG2E, (8, PAIR))
            dots[g, b] = jnp.broadcast_to(dot, (8, PAIR))

    def second_pass(j, g, opening, whole=True):
        count = PAIR if whole else TOK
        keys = of_chunk(j, g, keys_at, whole)
        key, value = 0.0, 0.0
        for b in range(2):
            at = slice(b * PAIR, (b + 1) * PAIR)
            score = scores[j, g, b, 0:count, :].reshape(count // 8, 8, PAIR)
            probs = jnp.exp2(score - peak[g, b][None])
            low = probs.reshape(count, PAIR).astype(BF16)
            grad = grads[j, g, b, 0:count, :].reshape(count // 8, 8, PAIR)
            grad = probs * (grad - dots[g, b][None])
            grad = grad.reshape(count, PAIR).astype(BF16)
            key = key + product(grad, queries[g, at, :], 1, 0)
            value = value + product(low, upstream[g, at, :], 1, 0)
            query = product(keys, grad, 0, 0)
            grad_query[g, b] = query if opening else grad_query[g, b] + query
        key = key * FACTOR
        own[j, g, 0] = key[:TOK]
        own[j, g, 1] = value[:TOK]
        if whole:
            sib_out[j, g, 0] = key[TOK:].astype(BF16)
            sib_out[j, g, 1] = value[TOK:].astype(BF16)

    def to_sibling(j, g):
        at = GROUPS * j + g
        return remote(sib_out.at[j, g], sib_in.at[j, g], sib_send.at[at], sib_recv.at[at], sibling)

    sib = {j: [to_sibling(j, g) for g in range(GROUPS)] for j in (1, 3)}
    def far_copy(i, g, kind):
        at = 4 * i + 2 * g + kind
        return remote(
            far_out.at[i, g, kind], far_in.at[i, g, kind], far_send.at[at], far_recv.at[at],
            chip_at(2 * i - 1, core),
        )

    far = [
        [[far_copy(i, g, kind) for kind in range(2)] for g in range(GROUPS)] for i in range(2)
    ]

    def to_neighbour(i, g, kind):
        side = lax.rem(core + kind, 2)
        return remote(
            near_out.at[i, g, kind], near_in.at[i, g, side],
            near_send.at[4 * i + 2 * g + kind], near_recv.at[4 * i + 2 * g + side],
            chip_at(2 * i - 1, kind),
        )

    near = [
        [[to_neighbour(i, g, kind) for kind in range(2)] for g in range(GROUPS)] for i in range(2)
    ]
    here = [
        remote(
            here_out.at[g], sib_in.at[HERE, g],
            sib_send.at[GROUPS * HERE + g], sib_recv.at[GROUPS * HERE + g], sibling,
        )
        for g in range(GROUPS)
    ]
    swap = [
        remote(
            kv_pair.at[g, pl.ds(TOK, TOK)], kv_own.at[core, g],
            pair_send.at[g], pair_recv.at[g], sibling,
        )
        for g in range(GROUPS)
    ]

    def turn_inputs():
        rows_copy.wait_recv()

        def turn(i, carry):
            at = pl.ds(pl.multiple_of(i * 128, 128), 128)
            rows = jnp.concatenate([rows_in[:, at], rows_sib[:, at]], axis=0)
            rows_turned[at, :] = jnp.transpose(rows)
            return carry

        lax.fori_loop(0, MODEL // 128, turn, 0)

    def near_arrived(g):
        halo[8 * g + 1].wait_recv()
        halo[8 * g + 3].start()
        halo[8 * g + 2].wait_recv()
        halo[8 * g + 4].start()
        halo[8 * g + 5].start()
        halo[8 * g + 6].start()

    def distant_arrived(g):
        halo[8 * g + 3].wait_recv()
        halo[8 * g + 4].wait_recv()
        halo[8 * g + 7].start()

    def send_whole(g):
        second_pass(far_whole, g, False)
        to_sibling(far_whole, g).start()
        for kind in range(2):
            far_out[core, g, kind] = own[far_whole, g, kind].astype(BF16)
            far_copy(core, g, kind).start()

    def send_half(g):
        to_sibling(far_half, g).wait_recv()
        for kind in range(2):
            far_out[1 - core, g, kind] = (
                own[far_half, g, kind] + sib_in[far_half, g, kind].astype(F32)
            ).astype(BF16)
            far_copy(1 - core, g, kind).start()

    def send_near(g):
        for i, j in enumerate((1, 3)):
            sib[j][g].wait_recv()
        for kind in range(2):
            for i, j in enumerate((1, 3)):
                far[i][g][kind].wait_recv()
                near_out[i, g, kind] = (
                    own[j, g, kind] + sib_in[j, g, kind].astype(F32)
                    + far_in[i, g, kind].astype(F32)
                ).astype(BF16)
                near[i][g][kind].start()

    def send_here(g):
        second_pass(HERE, g, False)
        here_out[g, 0] = own[HERE, g, 1 - core].astype(BF16)
        here_out[g, 1] = sib_out[HERE, g, 1 - core]
        here[g].start()

    halo[0].wait_recv()
    make_mask(HERE)
    first_pass(HERE, 0, True)
    halo[8].wait_recv()
    first_pass(HERE, 1, True)

    turn_inputs()
    near_arrived(0)
    halo[5].wait_recv()
    halo[6].wait_recv()
    both(make_mask, 1, 2)
    both(lambda j: first_pass(j, 0, False), 1, 2)
    near_arrived(1)
    halo[13].wait_recv()
    halo[14].wait_recv()
    both(lambda j: first_pass(j, 1, False), 1, 2)

    def distant(g):
        if not g:
            make_mask(far_half, False)
        first_pass(far_half, g, False, False)
        halo[8 * g + 7].wait_recv()
        if not g:
            make_mask(far_whole)
        first_pass(far_whole, g, False)
        merge(g)

    def second_and_send(j, g):
        second_pass(j, g, False)
        to_sibling(j, g).start()

    grad_query[...] = jnp.zeros_like(grad_query)
    distant_arrived(0)
    distant(0)
    distant_arrived(1)
    send_whole(0)
    second_pass(far_half, 0, False, False)
    send_half(0)
    distant(1)
    send_whole(1)
    second_pass(far_half, 1, False, False)
    second_and_send(1, 0)
    send_half(1)
    second_and_send(3, 0)
    second_and_send(1, 1)
    send_near(0)
    second_and_send(3, 1)
    send_here(0)
    send_near(1)
    send_here(1)

    row = [
        [
            remote(
                row_out.at[g, i], row_in.at[g, i],
                row_send.at[(n_x - 1) * g + i], row_recv.at[(n_x - 1) * g + i], row_peers[i],
            )
            for i in range(n_x - 1)
        ]
        for g in range(GROUPS)
    ]
    col = [
        [
            remote(
                col_out.at[g, col_at[i]], col_in.at[g, i],
                col_send.at[(n_outer - 1) * g + i], col_recv.at[(n_outer - 1) * g + i],
                col_peers[i],
            )
            for i in range(n_outer - 1)
        ]
        for g in range(GROUPS)
    ]

    def finish_kv(g):
        here[g].wait_recv()
        for i in range(2):
            for side in range(2):
                remote(
                    near_out.at[i, g, side], near_in.at[i, g, side],
                    near_send.at[4 * i + 2 * g + side], near_recv.at[4 * i + 2 * g + side], right,
                ).wait_recv()
        mine_kv = own[HERE, g, core] + sib_in[HERE, g, 1].astype(F32)
        sib_kv = sib_out[HERE, g, core].astype(F32) + sib_in[HERE, g, 0].astype(F32)
        for i in range(2):
            mine_kv = mine_kv + near_in[i, g, 0].astype(F32)
            sib_kv = sib_kv + near_in[i, g, 1].astype(F32)
        mine_kv = mine_kv.astype(BF16)
        kv_own[core, g] = mine_kv
        kv_pair[g, 0:TOK, :] = mine_kv
        kv_pair[g, TOK:PAIR, :] = sib_kv.astype(BF16)
        swap[g].start()

    def row_first(g):
        whole = product(rows_turned[...], kv_pair[g], 1, 0)
        part[g] = whole.reshape(n_outer, n_x, 16, HEAD)
        for i, s in enumerate(row_order):
            row_out[g, i] = part[g, :, lax.rem(x + s, n_x)].astype(BF16)
            row[g][i].start()

    def row_last(g):
        share = part[g, :, x]
        for i in range(n_x - 1):
            row[g][i].wait_recv()
            share = share + row_in[g, i].astype(F32)
        part[g, :, x] = share
        col_out[g] = share.astype(BF16)
        for copy in col[g]:
            copy.start()

    def col_last(g):
        share = part[g, outer, x]
        for s, copy in enumerate(col[g]):
            copy.wait_recv()
            share = share + col_in[g, s].astype(F32)
        mine[0, g] = share[:8]
        mine[1, g] = share[8:]

    finish_kv(0)
    for g in range(GROUPS):
        for b in range(2):
            rows = jnp.transpose(grad_query[g, b]) * FACTOR
            for m in range(2):
                h = g * PER_GROUP + 2 * b + m
                dq_out[:, h * HEAD : (h + 1) * HEAD] = rows[m * TOK : (m + 1) * TOK].astype(BF16)
    row_first(0)
    finish_kv(1)
    row_first(1)
    row_last(0)
    for g in range(GROUPS):
        swap[g].wait_recv()
    kv_rows = jnp.concatenate(
        [kv_own[kind, g] for kind in range(2) for g in range(GROUPS)], axis=1
    )
    dx_out[...] = product(kv_rows, weight[...], 1, 1).astype(BF16)
    row_last(1)
    col_last(0)
    col_last(1)

    last = []
    for i, (s, flip, peer) in enumerate(dp_peers):
        copy = remote(
            mine.at[1 - core if flip else core], dp_buf.at[dp, core],
            dp_send.at[i], dp_recv.at[i], peer,
        )
        copy.start()
        last.append(copy)
    dp_buf[dp, core] = mine[core]
    for copy in last:
        copy.wait_recv()
    for kind in range(2):
        whole = dp_buf[0, kind]
        for r in range(1, n_dp):
            whole = whole + dp_buf[r, kind]
        for g in range(GROUPS):
            at = kind * GROUPS + g
            gw_ref[:, at * HEAD : (at + 1) * HEAD] = whole[g]

    others = [to_sibling(far_whole, g) for g in range(GROUPS)] + sib[1] + sib[3]
    by_kind = [copy for group in far + near for kinds in group for copy in kinds]
    for copy in halo + others + by_kind + here + swap + [rows_copy] + sum(row + col, []) + last:
        copy.wait_send()


PARTS = 4


def place(*refs):
    count = len(refs) // 2
    sems = refs[-1]
    copies = []
    for source, target in zip(refs[:count], refs[count:-1]):
        rows = source.shape[0] // PARTS if source.shape[0] == TOK else source.shape[0]
        for start in range(0, source.shape[0], rows):
            at = pl.ds(start, rows)
            copies.append(
                pltpu.make_async_copy(source.at[at], target.at[at], sems.at[len(copies)])
            )
    for copy in copies:
        copy.start()
    for copy in copies:
        copy.wait()


def on_device(sizes, queries, inputs, kv_weight, grad_out, segment_ids):
    n_dp, n_outer, n_inner = sizes
    n_x = n_inner // 2
    vmem, dma = pltpu.VMEM, pltpu.SemaphoreType.DMA
    anywhere = pl.BlockSpec(memory_space=pl.ANY)
    inside = pl.BlockSpec(memory_space=pltpu.VMEM)
    tokens = jax.ShapeDtypeStruct((TOK, MODEL), BF16)
    shapes = (tokens, tokens, jax.ShapeDtypeStruct((8, WIDTH), F32))
    results = pl.pallas_call(
        functools.partial(kernel, *sizes),
        out_shape=tuple(pltpu.VMEM(leaf.shape, leaf.dtype) for leaf in shapes),
        in_specs=[anywhere] * 4 + [inside],
        out_specs=(inside,) * 3,
        scratch_shapes=[
            vmem((2, TOK, MODEL), BF16),
            vmem((TOK, MODEL), BF16),
            vmem((TOK, MODEL), BF16),
            vmem((MODEL, PAIR), BF16),
            vmem((MODEL, WIDTH), BF16),
            vmem((GROUPS, PER_GROUP * TOK, HEAD), BF16),
            vmem((GROUPS, PER_GROUP * TOK, HEAD), BF16),
            vmem((SPAN, 2, GROUPS, SENT, HALF), BF16),
            vmem((8, PAIR), F32),
            vmem((SPAN, PAIR, PAIR), F32),
            vmem((SPAN, GROUPS, 2, PAIR, PAIR), F32),
            vmem((SPAN, GROUPS, 2, PAIR, PAIR), F32),
            vmem((GROUPS, 2, 8, PAIR), F32),
            vmem((GROUPS, 2, 8, PAIR), F32),
            vmem((GROUPS, 2, 8, PAIR), F32),
            vmem((GROUPS, 2, HEAD, PAIR), F32),
            vmem((SPAN, GROUPS, 2, TOK, HEAD), F32),
            vmem((SPAN, GROUPS, 2, TOK, HEAD), BF16),
            vmem((SPAN, GROUPS, 2, TOK, HEAD), BF16),
            vmem((GROUPS, 2, TOK, HEAD), BF16),
            vmem((2, GROUPS, 2, TOK, HEAD), BF16),
            vmem((2, GROUPS, 2, TOK, HEAD), BF16),
            vmem((2, GROUPS, 2, TOK, HEAD), BF16),
            vmem((2, GROUPS, 2, TOK, HEAD), BF16),
            vmem((GROUPS, PAIR, HEAD), BF16),
            vmem((2, GROUPS, TOK, HEAD), BF16),
            vmem((GROUPS, n_outer, n_x, 16, HEAD), F32),
            vmem((GROUPS, n_x - 1, n_outer, 16, HEAD), BF16),
            vmem((GROUPS, n_x - 1, n_outer, 16, HEAD), BF16),
            vmem((GROUPS, n_outer, 16, HEAD), BF16),
            vmem((GROUPS, n_outer - 1, 16, HEAD), BF16),
            vmem((2, GROUPS, 8, HEAD), F32),
            vmem((n_dp, 2, GROUPS, 8, HEAD), F32),
            dma((7,)),
            dma((16,)), dma((16,)), dma, dma, dma((10,)), dma((10,)),
            dma((8,)), dma((8,)), dma((8,)), dma((8,)),
            dma((2,)), dma((2,)), dma((2 * (n_x - 1),)), dma((2 * (n_x - 1),)),
            dma((2 * (n_outer - 1),)), dma((2 * (n_outer - 1),)), dma((2 * n_dp - 1,)), dma((2 * n_dp - 1,)),
        ],
        compiler_params=pltpu.CompilerParams(
            collective_id=0, has_side_effects=True, vmem_limit_bytes=56 * 2**20
        ),
    )(queries[0], inputs[0], kv_weight, grad_out[0], segment_ids)
    grad_query, grad_input, grad_weight = pl.pallas_call(
        place,
        out_shape=shapes,
        in_specs=[inside] * 3,
        out_specs=(anywhere,) * 3,
        scratch_shapes=[dma((2 * PARTS + 1,))],
    )(*results)
    return grad_query[None], grad_input[None], grad_weight


def solution(mesh):
    spread = P("dp", ("outer", "inner"), None)
    sizes = (mesh.shape["dp"], mesh.shape["outer"], mesh.shape["inner"])
    return jax.shard_map(
        functools.partial(on_device, sizes),
        mesh=mesh,
        in_specs=(spread, spread, P(), spread, P("dp", ("outer", "inner"))),
        out_specs=(spread, spread, P(("outer", "inner"), None)),
        check_vma=False,
    )
```

```python
import functools
import math

import jax
import jax.numpy as jnp
from jax import lax
from jax.experimental import pallas as pl
from jax.experimental.pallas import tpu as pltpu
from jax.sharding import PartitionSpec as P

MESH = pl.DeviceIdType.MESH
HEADS = 8
GROUPS = 2
PER_GROUP = HEADS // GROUPS
HEAD = 128
TOK = 192
PAIR = 2 * TOK
SENT = TOK + 16
HALF = 2 * HEAD
WIDTH = 2 * GROUPS * HEAD
MODEL = HEADS * HEAD
SPAN = 5
HERE = 2
FACTOR = HEAD**-0.5
LOG2E = math.log2(math.e)
FAR = -1e30
F32 = jnp.float32
BF16 = jnp.bfloat16


def product(left, right, left_dim, right_dim):
    return lax.dot_general(
        left, right, (((left_dim,), (right_dim,)), ((), ())), preferred_element_type=F32
    )


def thrice(rows):
    return jnp.concatenate([rows, rows, rows], axis=1)


def remote(source, target, send, recv, device):
    return pltpu.make_async_remote_copy(
        src_ref=source, dst_ref=target, send_sem=send, recv_sem=recv,
        device_id=device, device_id_type=MESH,
    )


def kernel(
    n_dp, n_outer, n_inner,
    q_hbm, in_hbm, w_hbm, up_hbm, ids_ref,
    dq_out, dx_out, gw_ref,
    raw, rows_in, rows_sib, rows_turned, weight, queries, upstream,
    window, ids_query, mask, scores, grads, peak, total, dots, grad_query,
    own, sib_out, sib_in, here_out, far_out, far_in, near_out, near_in, kv_pair, kv_own,
    part, row_out, row_in, col_out, col_in, mine, dp_buf,
    load_sem,
    halo_send, halo_recv, rows_send, rows_recv, sib_send, sib_recv,
    far_send, far_recv, near_send, near_recv,
    pair_send, pair_recv, row_send, row_recv, col_send, col_recv, dp_send, dp_recv,
):
    n_x = n_inner // 2
    chips = n_outer * n_x
    dp = lax.axis_index("dp")
    outer = lax.axis_index("outer")
    inner = lax.axis_index("inner")
    x, core = inner // 2, inner % 2
    chip = outer * n_x + x

    def chip_at(steps, at_core):
        there = lax.rem(chip + steps + chips, chips)
        return (dp, there // n_x, lax.rem(there, n_x) * 2 + at_core)

    sibling = (dp, outer, x * 2 + 1 - core)
    right, left = chip_at(1, core), chip_at(-1, core)
    across = [chip_at(1, 1 - core), chip_at(-1, 1 - core)]
    row_order = sorted(range(1, n_x), key=lambda s: -min(s, n_x - s))
    row_peers = [(dp, outer, lax.rem(x + s, n_x) * 2 + core) for s in row_order]
    n_y = n_outer // 2
    z, y = outer // n_y, outer % n_y
    col_order = sorted(
        ((sz, sy) for sy in range(n_y) for sz in range(2) if sy or sz),
        key=lambda s: (-min(s[1], n_y - s[1]), -s[0], s[1]),
    )
    col_at = [lax.rem(z + sz, 2) * n_y + lax.rem(y + sy, n_y) for sz, sy in col_order]
    col_peers = [(dp, at, inner) for at in col_at]
    dp_peers = [
        (s, flip, (lax.rem(dp + s, n_dp), outer, x * 2 + (1 - core if flip else core)))
        for s in sorted(range(n_dp), key=lambda s: -min(s, n_dp - s))
        for flip in (0, 1)
        if s or flip
    ]
    peers = [peer for _, _, peer in dp_peers] + col_peers + row_peers + across + [right, left]

    blocks = [(g + GROUPS * kind) * HEAD for g in range(GROUPS) for kind in range(2)]
    loads = [
        pltpu.make_async_copy(source, target, load_sem.at[i])
        for i, (source, target) in enumerate(
            [(in_hbm, rows_in)]
            + [(w_hbm.at[:, pl.ds(at, HEAD)], weight.at[:, pl.ds(at, HEAD)]) for at in blocks]
            + [(q_hbm, raw.at[0]), (up_hbm, raw.at[1])]
        )
    ]
    for load in loads:
        load.start()

    barrier = pltpu.get_barrier_semaphore()
    for peer in peers:
        pl.semaphore_signal(barrier, inc=1, device_id=peer, device_id_type=MESH)

    ids_row = ids_ref[...].astype(F32)
    twice = jnp.concatenate([ids_row, ids_row, jnp.zeros((1, 2 * HALF - PAIR), F32)], axis=1)
    first_row = lax.broadcasted_iota(jnp.int32, (SENT - TOK, HALF), 0) == 0
    window[HERE, 0, 0, TOK:SENT, :] = jnp.where(
        first_row, twice[:, :HALF], twice[:, HALF:]
    ).astype(BF16)
    ids_query[...] = jnp.broadcast_to(twice[:, :PAIR], (8, PAIR))

    pl.semaphore_wait(barrier, len(peers))
    loads[0].wait()
    rows_copy = remote(rows_in, rows_sib, rows_send, rows_recv, sibling)
    rows_copy.start()
    far_whole, far_half = 4 * core, 4 * (1 - core)

    halo = []
    for g in range(GROUPS):
        rows = pl.ds(0, TOK if g else SENT)
        for i, (source, target, device) in enumerate(
            [
                ((2, 0), (2, 1), sibling),
                ((2, 0), (1, 0), right),
                ((2, 0), (3, 0), left),
                ((1, 0), (0, 0), right),
                ((3, 0), (4, 0), left),
                ((1, 0), (1, 1), sibling),
                ((3, 0), (3, 1), sibling),
                ((far_half, 0), (far_half, 1), sibling),
            ]
        ):
            halo.append(
                remote(
                    window.at[source[0], source[1], g, rows],
                    window.at[target[0], target[1], g, rows],
                    halo_send.at[8 * g + i], halo_recv.at[8 * g + i], device,
                )
            )
    for g in range(GROUPS):
        loads[1 + 2 * g].wait()
        loads[2 + 2 * g].wait()
        columns = jnp.concatenate(
            [weight[:, at : at + HEAD] for at in blocks[2 * g : 2 * g + 2]], axis=1
        )
        window[HERE, 0, g, 0:TOK, :] = product(rows_in[...], columns, 1, 0).astype(BF16)
        for i in (1, 2, 0):
            halo[8 * g + i].start()

    loads[5].wait()
    loads[6].wait()
    for h in range(HEADS):
        g, member = h // PER_GROUP, h % PER_GROUP
        at = slice(h * HEAD, (h + 1) * HEAD)
        queries[g, member * TOK : (member + 1) * TOK, :] = raw[0, :, at]
        upstream[g, member * TOK : (member + 1) * TOK, :] = raw[1, :, at]

    def of_chunk(j, g, at, whole=True):
        if not whole:
            return window[j, 0, g, 0:TOK, at]
        return jnp.concatenate([window[j, 0, g, 0:TOK, at], window[j, 1, g, 0:TOK, at]], axis=0)

    keys_at, values_at = slice(0, HEAD), slice(HEAD, HALF)

    def make_mask(j, whole=True):
        count = PAIR if whole else TOK
        lane = lax.broadcasted_iota(jnp.int32, (1, PAIR), 1)
        near, far = (
            jnp.concatenate([ids[0:1], ids[1:2, : PAIR - HALF]], axis=1)
            for ids in (
                window[j, side, 0, TOK:SENT, :].astype(F32) for side in (0, 1 if whole else 0)
            )
        )
        ids_key = jnp.where(lane < TOK, near, far)
        ids_col = jnp.transpose(jnp.broadcast_to(ids_key, (HEAD, PAIR)))
        mask[j, 0:count, :] = jnp.where(
            thrice(ids_col[:count]) == ids_query[0:1, :], 0.0, FAR
        )

    def first_pass(j, g, opening, whole=True):
        count = PAIR if whole else TOK
        keys, values = of_chunk(j, g, keys_at, whole), of_chunk(j, g, values_at, whole)
        for b in range(2):
            at = slice(b * PAIR, (b + 1) * PAIR)
            score = product(keys, queries[g, at, :], 1, 1) * (FACTOR * LOG2E)
            score = score + mask[j, 0:count, :]
            grad = product(values, upstream[g, at, :], 1, 1)
            scores[j, g, b, 0:count, :] = score
            grads[j, g, b, 0:count, :] = grad
            score = score.reshape(count // 8, 8, PAIR)
            top = jnp.max(score, axis=0)
            if not opening:
                before = peak[g, b]
                top = jnp.maximum(before, top)
            weights = jnp.exp2(score - top[None])
            dot = jnp.sum(weights * grad.reshape(count // 8, 8, PAIR), axis=0)
            weights = jnp.sum(weights, axis=0)
            if not opening:
                scale = jnp.exp2(before - top)
                weights = weights + total[g, b] * scale
                dot = dot + dots[g, b] * scale
            peak[g, b] = top
            total[g, b] = weights
            dots[g, b] = dot

    def both(visit, first, stride):
        def step(t, carry):
            visit(first + stride * t)
            return carry

        lax.fori_loop(0, 2, step, 0)

    def merge(g):
        for b in range(2):
            top = jnp.max(peak[g, b], axis=0, keepdims=True)
            scale = jnp.exp2(peak[g, b] - top)
            weights = jnp.sum(total[g, b] * scale, axis=0, keepdims=True)
            dot = jnp.sum(dots[g, b] * scale, axis=0, keepdims=True) / weights
            peak[g, b] = jnp.broadcast_to(top + jnp.log(weights) * LOG2E, (8, PAIR))
            dots[g, b] = jnp.broadcast_to(dot, (8, PAIR))

    def second_pass(j, g, opening, whole=True):
        count = PAIR if whole else TOK
        keys = of_chunk(j, g, keys_at, whole)
        key, value = 0.0, 0.0
        for b in range(2):
            at = slice(b * PAIR, (b + 1) * PAIR)
            score = scores[j, g, b, 0:count, :].reshape(count // 8, 8, PAIR)
            probs = jnp.exp2(score - peak[g, b][None])
            low = probs.reshape(count, PAIR).astype(BF16)
            grad = grads[j, g, b, 0:count, :].reshape(count // 8, 8, PAIR)
            grad = probs * (grad - dots[g, b][None])
            grad = grad.reshape(count, PAIR).astype(BF16)
            key = key + product(grad, queries[g, at, :], 1, 0)
            value = value + product(low, upstream[g, at, :], 1, 0)
            query = product(keys, grad, 0, 0)
            grad_query[g, b] = query if opening else grad_query[g, b] + query
        key = key * FACTOR
        own[j, g, 0] = key[:TOK]
        own[j, g, 1] = value[:TOK]
        if whole:
            sib_out[j, g, 0] = key[TOK:].astype(BF16)
            sib_out[j, g, 1] = value[TOK:].astype(BF16)

    def to_sibling(j, g):
        at = GROUPS * j + g
        return remote(sib_out.at[j, g], sib_in.at[j, g], sib_send.at[at], sib_recv.at[at], sibling)

    sib = {j: [to_sibling(j, g) for g in range(GROUPS)] for j in (1, 3)}
    def far_copy(i, g, kind):
        at = 4 * i + 2 * g + kind
        return remote(
            far_out.at[i, g, kind], far_in.at[i, g, kind], far_send.at[at], far_recv.at[at],
            chip_at(2 * i - 1, core),
        )

    far = [
        [[far_copy(i, g, kind) for kind in range(2)] for g in range(GROUPS)] for i in range(2)
    ]

    def to_neighbour(i, g, kind):
        side = lax.rem(core + kind, 2)
        return remote(
            near_out.at[i, g, kind], near_in.at[i, g, side],
            near_send.at[4 * i + 2 * g + kind], near_recv.at[4 * i + 2 * g + side],
            chip_at(2 * i - 1, kind),
        )

    near = [
        [[to_neighbour(i, g, kind) for kind in range(2)] for g in range(GROUPS)] for i in range(2)
    ]
    here = [
        remote(
            here_out.at[g], sib_in.at[HERE, g],
            sib_send.at[GROUPS * HERE + g], sib_recv.at[GROUPS * HERE + g], sibling,
        )
        for g in range(GROUPS)
    ]
    swap = [
        remote(
            kv_pair.at[g, pl.ds(TOK, TOK)], kv_own.at[core, g],
            pair_send.at[g], pair_recv.at[g], sibling,
        )
        for g in range(GROUPS)
    ]

    def turn_inputs():
        rows_copy.wait_recv()

        def turn(i, carry):
            at = pl.ds(pl.multiple_of(i * 128, 128), 128)
            rows = jnp.concatenate([rows_in[:, at], rows_sib[:, at]], axis=0)
            rows_turned[at, :] = jnp.transpose(rows)
            return carry

        lax.fori_loop(0, MODEL // 128, turn, 0)

    def near_arrived(g):
        halo[8 * g + 1].wait_recv()
        halo[8 * g + 3].start()
        halo[8 * g + 2].wait_recv()
        halo[8 * g + 4].start()
        halo[8 * g + 5].start()
        halo[8 * g + 6].start()

    def distant_arrived(g):
        halo[8 * g + 3].wait_recv()
        halo[8 * g + 4].wait_recv()
        halo[8 * g + 7].start()

    def send_whole(g):
        second_pass(far_whole, g, False)
        to_sibling(far_whole, g).start()
        for kind in range(2):
            far_out[core, g, kind] = own[far_whole, g, kind].astype(BF16)
            far_copy(core, g, kind).start()

    def send_half(g):
        to_sibling(far_half, g).wait_recv()
        for kind in range(2):
            far_out[1 - core, g, kind] = (
                own[far_half, g, kind] + sib_in[far_half, g, kind].astype(F32)
            ).astype(BF16)
            far_copy(1 - core, g, kind).start()

    def send_near(g):
        for i, j in enumerate((1, 3)):
            sib[j][g].wait_recv()
        for kind in range(2):
            for i, j in enumerate((1, 3)):
                far[i][g][kind].wait_recv()
                near_out[i, g, kind] = (
                    own[j, g, kind] + sib_in[j, g, kind].astype(F32)
                    + far_in[i, g, kind].astype(F32)
                ).astype(BF16)
                near[i][g][kind].start()

    def send_here(g):
        second_pass(HERE, g, False)
        here_out[g, 0] = own[HERE, g, 1 - core].astype(BF16)
        here_out[g, 1] = sib_out[HERE, g, 1 - core]
        here[g].start()

    halo[0].wait_recv()
    make_mask(HERE)
    first_pass(HERE, 0, True)
    halo[8].wait_recv()
    first_pass(HERE, 1, True)

    turn_inputs()
    near_arrived(0)
    halo[5].wait_recv()
    halo[6].wait_recv()
    both(make_mask, 1, 2)
    both(lambda j: first_pass(j, 0, False), 1, 2)
    near_arrived(1)
    halo[13].wait_recv()
    halo[14].wait_recv()
    both(lambda j: first_pass(j, 1, False), 1, 2)

    def distant(g):
        if not g:
            make_mask(far_half, False)
        first_pass(far_half, g, False, False)
        halo[8 * g + 7].wait_recv()
        if not g:
            make_mask(far_whole)
        first_pass(far_whole, g, False)
        merge(g)

    def second_and_send(j, g):
        second_pass(j, g, False)
        to_sibling(j, g).start()

    grad_query[...] = jnp.zeros_like(grad_query)
    distant_arrived(0)
    distant(0)
    distant_arrived(1)
    send_whole(0)
    second_pass(far_half, 0, False, False)
    send_half(0)
    distant(1)
    send_whole(1)
    second_pass(far_half, 1, False, False)
    second_and_send(1, 0)
    send_half(1)
    second_and_send(3, 0)
    second_and_send(1, 1)
    send_near(0)
    second_and_send(3, 1)
    send_here(0)
    send_near(1)
    send_here(1)

    row = [
        [
            remote(
                row_out.at[g, i], row_in.at[g, i],
                row_send.at[(n_x - 1) * g + i], row_recv.at[(n_x - 1) * g + i], row_peers[i],
            )
            for i in range(n_x - 1)
        ]
        for g in range(GROUPS)
    ]
    col = [
        [
            remote(
                col_out.at[g, col_at[i]], col_in.at[g, i],
                col_send.at[(n_outer - 1) * g + i], col_recv.at[(n_outer - 1) * g + i],
                col_peers[i],
            )
            for i in range(n_outer - 1)
        ]
        for g in range(GROUPS)
    ]

    def finish_kv(g):
        here[g].wait_recv()
        for i in range(2):
            for side in range(2):
                remote(
                    near_out.at[i, g, side], near_in.at[i, g, side],
                    near_send.at[4 * i + 2 * g + side], near_recv.at[4 * i + 2 * g + side], right,
                ).wait_recv()
        mine_kv = own[HERE, g, core] + sib_in[HERE, g, 1].astype(F32)
        sib_kv = sib_out[HERE, g, core].astype(F32) + sib_in[HERE, g, 0].astype(F32)
        for i in range(2):
            mine_kv = mine_kv + near_in[i, g, 0].astype(F32)
            sib_kv = sib_kv + near_in[i, g, 1].astype(F32)
        mine_kv = mine_kv.astype(BF16)
        kv_own[core, g] = mine_kv
        kv_pair[g, 0:TOK, :] = mine_kv
        kv_pair[g, TOK:PAIR, :] = sib_kv.astype(BF16)
        swap[g].start()

    def row_first(g):
        whole = product(rows_turned[...], kv_pair[g], 1, 0)
        part[g] = whole.reshape(n_outer, n_x, 16, HEAD)
        for i, s in enumerate(row_order):
            row_out[g, i] = part[g, :, lax.rem(x + s, n_x)].astype(BF16)
            row[g][i].start()

    def row_last(g):
        share = part[g, :, x]
        for i in range(n_x - 1):
            row[g][i].wait_recv()
            share = share + row_in[g, i].astype(F32)
        part[g, :, x] = share
        col_out[g] = share.astype(BF16)
        for copy in col[g]:
            copy.start()

    def col_last(g):
        share = part[g, outer, x]
        for s, copy in enumerate(col[g]):
            copy.wait_recv()
            share = share + col_in[g, s].astype(F32)
        mine[0, g] = share[:8]
        mine[1, g] = share[8:]

    finish_kv(0)
    row_first(0)
    finish_kv(1)
    row_first(1)
    row_last(0)
    row_last(1)

    for g in range(GROUPS):
        for b in range(2):
            rows = jnp.transpose(grad_query[g, b]) * FACTOR
            for m in range(2):
                h = g * PER_GROUP + 2 * b + m
                dq_out[:, h * HEAD : (h + 1) * HEAD] = rows[m * TOK : (m + 1) * TOK].astype(BF16)
    for g in range(GROUPS):
        swap[g].wait_recv()
    kv_rows = jnp.concatenate(
        [kv_own[kind, g] for kind in range(2) for g in range(GROUPS)], axis=1
    )
    dx_out[...] = product(kv_rows, weight[...], 1, 1).astype(BF16)
    others = [to_sibling(far_whole, g) for g in range(GROUPS)] + sib[1] + sib[3]
    by_kind = [copy for group in far + near for kinds in group for copy in kinds]
    for copy in halo + others + by_kind + here + swap + [rows_copy] + sum(row, []):
        copy.wait_send()
    col_last(0)
    col_last(1)

    last = []
    for i, (s, flip, peer) in enumerate(dp_peers):
        copy = remote(
            mine.at[1 - core if flip else core], dp_buf.at[dp, core],
            dp_send.at[i], dp_recv.at[i], peer,
        )
        copy.start()
        last.append(copy)
    dp_buf[dp, core] = mine[core]
    for copy in sum(col, []):
        copy.wait_send()
    for copy in last:
        copy.wait_recv()
    for kind in range(2):
        whole = dp_buf[0, kind]
        for r in range(1, n_dp):
            whole = whole + dp_buf[r, kind]
        for g in range(GROUPS):
            at = kind * GROUPS + g
            gw_ref[:, at * HEAD : (at + 1) * HEAD] = whole[g]
    for copy in last:
        copy.wait_send()


PARTS = 4


def place(*refs):
    count = len(refs) // 2
    sems = refs[-1]
    copies = []
    for source, target in zip(refs[:count], refs[count:-1]):
        rows = source.shape[0] // PARTS if source.shape[0] == TOK else source.shape[0]
        for start in range(0, source.shape[0], rows):
            at = pl.ds(start, rows)
            copies.append(
                pltpu.make_async_copy(source.at[at], target.at[at], sems.at[len(copies)])
            )
    for copy in copies:
        copy.start()
    for copy in copies:
        copy.wait()


def on_device(sizes, queries, inputs, kv_weight, grad_out, segment_ids):
    n_dp, n_outer, n_inner = sizes
    n_x = n_inner // 2
    vmem, dma = pltpu.VMEM, pltpu.SemaphoreType.DMA
    anywhere = pl.BlockSpec(memory_space=pl.ANY)
    inside = pl.BlockSpec(memory_space=pltpu.VMEM)
    tokens = jax.ShapeDtypeStruct((TOK, MODEL), BF16)
    shapes = (tokens, tokens, jax.ShapeDtypeStruct((8, WIDTH), F32))
    results = pl.pallas_call(
        functools.partial(kernel, *sizes),
        out_shape=tuple(pltpu.VMEM(leaf.shape, leaf.dtype) for leaf in shapes),
        in_specs=[anywhere] * 4 + [inside],
        out_specs=(inside,) * 3,
        scratch_shapes=[
            vmem((2, TOK, MODEL), BF16),
            vmem((TOK, MODEL), BF16),
            vmem((TOK, MODEL), BF16),
            vmem((MODEL, PAIR), BF16),
            vmem((MODEL, WIDTH), BF16),
            vmem((GROUPS, PER_GROUP * TOK, HEAD), BF16),
            vmem((GROUPS, PER_GROUP * TOK, HEAD), BF16),
            vmem((SPAN, 2, GROUPS, SENT, HALF), BF16),
            vmem((8, PAIR), F32),
            vmem((SPAN, PAIR, PAIR), F32),
            vmem((SPAN, GROUPS, 2, PAIR, PAIR), F32),
            vmem((SPAN, GROUPS, 2, PAIR, PAIR), F32),
            vmem((GROUPS, 2, 8, PAIR), F32),
            vmem((GROUPS, 2, 8, PAIR), F32),
            vmem((GROUPS, 2, 8, PAIR), F32),
            vmem((GROUPS, 2, HEAD, PAIR), F32),
            vmem((SPAN, GROUPS, 2, TOK, HEAD), F32),
            vmem((SPAN, GROUPS, 2, TOK, HEAD), BF16),
            vmem((SPAN, GROUPS, 2, TOK, HEAD), BF16),
            vmem((GROUPS, 2, TOK, HEAD), BF16),
            vmem((2, GROUPS, 2, TOK, HEAD), BF16),
            vmem((2, GROUPS, 2, TOK, HEAD), BF16),
            vmem((2, GROUPS, 2, TOK, HEAD), BF16),
            vmem((2, GROUPS, 2, TOK, HEAD), BF16),
            vmem((GROUPS, PAIR, HEAD), BF16),
            vmem((2, GROUPS, TOK, HEAD), BF16),
            vmem((GROUPS, n_outer, n_x, 16, HEAD), F32),
            vmem((GROUPS, n_x - 1, n_outer, 16, HEAD), BF16),
            vmem((GROUPS, n_x - 1, n_outer, 16, HEAD), BF16),
            vmem((GROUPS, n_outer, 16, HEAD), BF16),
            vmem((GROUPS, n_outer - 1, 16, HEAD), BF16),
            vmem((2, GROUPS, 8, HEAD), F32),
            vmem((n_dp, 2, GROUPS, 8, HEAD), F32),
            dma((7,)),
            dma((16,)), dma((16,)), dma, dma, dma((10,)), dma((10,)),
            dma((8,)), dma((8,)), dma((8,)), dma((8,)),
            dma((2,)), dma((2,)), dma((2 * (n_x - 1),)), dma((2 * (n_x - 1),)),
            dma((2 * (n_outer - 1),)), dma((2 * (n_outer - 1),)), dma((2 * n_dp - 1,)), dma((2 * n_dp - 1,)),
        ],
        compiler_params=pltpu.CompilerParams(
            collective_id=0, has_side_effects=True, vmem_limit_bytes=56 * 2**20
        ),
    )(queries[0], inputs[0], kv_weight, grad_out[0], segment_ids)
    grad_query, grad_input, grad_weight = pl.pallas_call(
        place,
        out_shape=shapes,
        in_specs=[inside] * 3,
        out_specs=(anywhere,) * 3,
        scratch_shapes=[dma((2 * PARTS + 1,))],
    )(*results)
    return grad_query[None], grad_input[None], grad_weight


def solution(mesh):
    spread = P("dp", ("outer", "inner"), None)
    sizes = (mesh.shape["dp"], mesh.shape["outer"], mesh.shape["inner"])
    return jax.shard_map(
        functools.partial(on_device, sizes),
        mesh=mesh,
        in_specs=(spread, spread, P(), spread, P("dp", ("outer", "inner"))),
        out_specs=(spread, spread, P(("outer", "inner"), None)),
        check_vma=False,
    )
```

```python
import functools
import math

import jax
import jax.numpy as jnp
from jax import lax
from jax.experimental import pallas as pl
from jax.experimental.pallas import tpu as pltpu
from jax.sharding import PartitionSpec as P

MESH = pl.DeviceIdType.MESH
HEADS = 8
GROUPS = 2
PER_GROUP = HEADS // GROUPS
HEAD = 128
TOK = 192
PAIR = 2 * TOK
SENT = TOK + 16
HALF = 2 * HEAD
WIDTH = 2 * GROUPS * HEAD
MODEL = HEADS * HEAD
SPAN = 5
HERE = 2
FACTOR = HEAD**-0.5
LOG2E = math.log2(math.e)
FAR = -1e30
F32 = jnp.float32
BF16 = jnp.bfloat16


def product(left, right, left_dim, right_dim):
    return lax.dot_general(
        left, right, (((left_dim,), (right_dim,)), ((), ())), preferred_element_type=F32
    )


def thrice(rows):
    return jnp.concatenate([rows, rows, rows], axis=1)


def remote(source, target, send, recv, device):
    return pltpu.make_async_remote_copy(
        src_ref=source, dst_ref=target, send_sem=send, recv_sem=recv,
        device_id=device, device_id_type=MESH,
    )


def kernel(
    n_dp, n_outer, n_inner,
    q_hbm, in_hbm, w_hbm, up_hbm, ids_ref,
    dq_out, dx_out, gw_ref,
    raw, rows_in, rows_sib, rows_turned, weight, queries, upstream,
    window, ids_query, mask, scores, grads, peak, total, dots, grad_query,
    own, sib_out, sib_in, here_out, far_out, far_in, near_out, near_in, kv_pair, kv_own,
    part, row_out, row_in, col_out, col_in, mine, dp_buf,
    load_sem,
    halo_send, halo_recv, rows_send, rows_recv, sib_send, sib_recv,
    far_send, far_recv, near_send, near_recv,
    pair_send, pair_recv, row_send, row_recv, col_send, col_recv, dp_send, dp_recv,
):
    n_x = n_inner // 2
    chips = n_outer * n_x
    dp = lax.axis_index("dp")
    outer = lax.axis_index("outer")
    inner = lax.axis_index("inner")
    x, core = inner // 2, inner % 2
    chip = outer * n_x + x

    def chip_at(steps, at_core):
        there = lax.rem(chip + steps + chips, chips)
        return (dp, there // n_x, lax.rem(there, n_x) * 2 + at_core)

    sibling = (dp, outer, x * 2 + 1 - core)
    right, left = chip_at(1, core), chip_at(-1, core)
    across = [chip_at(1, 1 - core), chip_at(-1, 1 - core)]
    row_order = sorted(range(1, n_x), key=lambda s: -min(s, n_x - s))
    row_peers = [(dp, outer, lax.rem(x + s, n_x) * 2 + core) for s in row_order]
    n_y = n_outer // 2
    z, y = outer // n_y, outer % n_y
    col_order = sorted(
        ((sz, sy) for sy in range(n_y) for sz in range(2) if sy or sz),
        key=lambda s: (-min(s[1], n_y - s[1]), -s[0], s[1]),
    )
    col_at = [lax.rem(z + sz, 2) * n_y + lax.rem(y + sy, n_y) for sz, sy in col_order]
    col_peers = [(dp, at, inner) for at in col_at]
    dp_peers = [
        (s, flip, (lax.rem(dp + s, n_dp), outer, x * 2 + (1 - core if flip else core)))
        for s in sorted(range(n_dp), key=lambda s: -min(s, n_dp - s))
        for flip in (0, 1)
        if s or flip
    ]
    peers = [peer for _, _, peer in dp_peers] + col_peers + row_peers + across + [right, left]

    blocks = [(g + GROUPS * kind) * HEAD for g in range(GROUPS) for kind in range(2)]
    loads = [
        pltpu.make_async_copy(source, target, load_sem.at[i])
        for i, (source, target) in enumerate(
            [(in_hbm, rows_in)]
            + [(w_hbm.at[:, pl.ds(at, HEAD)], weight.at[:, pl.ds(at, HEAD)]) for at in blocks]
            + [(q_hbm, raw.at[0]), (up_hbm, raw.at[1])]
        )
    ]
    for load in loads:
        load.start()

    barrier = pltpu.get_barrier_semaphore()
    for peer in peers:
        pl.semaphore_signal(barrier, inc=1, device_id=peer, device_id_type=MESH)

    ids_row = ids_ref[...].astype(F32)
    twice = jnp.concatenate([ids_row, ids_row, jnp.zeros((1, 2 * HALF - PAIR), F32)], axis=1)
    first_row = lax.broadcasted_iota(jnp.int32, (SENT - TOK, HALF), 0) == 0
    window[HERE, 0, 0, TOK:SENT, :] = jnp.where(
        first_row, twice[:, :HALF], twice[:, HALF:]
    ).astype(BF16)
    ids_query[...] = jnp.broadcast_to(twice[:, :PAIR], (8, PAIR))

    loads[0].wait()
    rows_copy = remote(rows_in, rows_sib, rows_send, rows_recv, sibling)
    far_whole, far_half = 4 * core, 4 * (1 - core)

    halo = []
    for g in range(GROUPS):
        rows = pl.ds(0, TOK if g else SENT)
        for i, (source, target, device) in enumerate(
            [
                ((2, 0), (2, 1), sibling),
                ((2, 0), (1, 0), right),
                ((2, 0), (3, 0), left),
                ((1, 0), (0, 0), right),
                ((3, 0), (4, 0), left),
                ((1, 0), (1, 1), sibling),
                ((3, 0), (3, 1), sibling),
                ((far_half, 0), (far_half, 1), sibling),
            ]
        ):
            halo.append(
                remote(
                    window.at[source[0], source[1], g, rows],
                    window.at[target[0], target[1], g, rows],
                    halo_send.at[8 * g + i], halo_recv.at[8 * g + i], device,
                )
            )
    for g in range(GROUPS):
        loads[1 + 2 * g].wait()
        loads[2 + 2 * g].wait()
        columns = jnp.concatenate(
            [weight[:, at : at + HEAD] for at in blocks[2 * g : 2 * g + 2]], axis=1
        )
        window[HERE, 0, g, 0:TOK, :] = product(rows_in[...], columns, 1, 0).astype(BF16)
        if not g:
            pl.semaphore_wait(barrier, len(peers))
        for i in (1, 2, 0):
            halo[8 * g + i].start()
        if not g:
            rows_copy.start()

    loads[5].wait()
    loads[6].wait()
    for h in range(HEADS):
        g, member = h // PER_GROUP, h % PER_GROUP
        at = slice(h * HEAD, (h + 1) * HEAD)
        queries[g, member * TOK : (member + 1) * TOK, :] = raw[0, :, at]
        upstream[g, member * TOK : (member + 1) * TOK, :] = raw[1, :, at]

    def of_chunk(j, g, at, whole=True):
        if not whole:
            return window[j, 0, g, 0:TOK, at]
        return jnp.concatenate([window[j, 0, g, 0:TOK, at], window[j, 1, g, 0:TOK, at]], axis=0)

    keys_at, values_at = slice(0, HEAD), slice(HEAD, HALF)

    def make_mask(j, whole=True):
        count = PAIR if whole else TOK
        lane = lax.broadcasted_iota(jnp.int32, (1, PAIR), 1)
        near, far = (
            jnp.concatenate([ids[0:1], ids[1:2, : PAIR - HALF]], axis=1)
            for ids in (
                window[j, side, 0, TOK:SENT, :].astype(F32) for side in (0, 1 if whole else 0)
            )
        )
        ids_key = jnp.where(lane < TOK, near, far)
        ids_col = jnp.transpose(jnp.broadcast_to(ids_key, (HEAD, PAIR)))
        mask[j, 0:count, :] = jnp.where(
            thrice(ids_col[:count]) == ids_query[0:1, :], 0.0, FAR
        )

    def first_pass(j, g, opening, whole=True):
        count = PAIR if whole else TOK
        keys, values = of_chunk(j, g, keys_at, whole), of_chunk(j, g, values_at, whole)
        for b in range(2):
            at = slice(b * PAIR, (b + 1) * PAIR)
            score = product(keys, queries[g, at, :], 1, 1) * (FACTOR * LOG2E)
            score = score + mask[j, 0:count, :]
            grad = product(values, upstream[g, at, :], 1, 1)
            scores[j, g, b, 0:count, :] = score
            grads[j, g, b, 0:count, :] = grad
            score = score.reshape(count // 8, 8, PAIR)
            top = jnp.max(score, axis=0)
            if not opening:
                before = peak[g, b]
                top = jnp.maximum(before, top)
            weights = jnp.exp2(score - top[None])
            dot = jnp.sum(weights * grad.reshape(count // 8, 8, PAIR), axis=0)
            weights = jnp.sum(weights, axis=0)
            if not opening:
                scale = jnp.exp2(before - top)
                weights = weights + total[g, b] * scale
                dot = dot + dots[g, b] * scale
            peak[g, b] = top
            total[g, b] = weights
            dots[g, b] = dot

    def both(visit, first, stride):
        def step(t, carry):
            visit(first + stride * t)
            return carry

        lax.fori_loop(0, 2, step, 0)

    def merge(g):
        for b in range(2):
            top = jnp.max(peak[g, b], axis=0, keepdims=True)
            scale = jnp.exp2(peak[g, b] - top)
            weights = jnp.sum(total[g, b] * scale, axis=0, keepdims=True)
            dot = jnp.sum(dots[g, b] * scale, axis=0, keepdims=True) / weights
            peak[g, b] = jnp.broadcast_to(top + jnp.log(weights) * LOG2E, (8, PAIR))
            dots[g, b] = jnp.broadcast_to(dot, (8, PAIR))

    def second_pass(j, g, opening, whole=True):
        count = PAIR if whole else TOK
        keys = of_chunk(j, g, keys_at, whole)
        key, value = 0.0, 0.0
        for b in range(2):
            at = slice(b * PAIR, (b + 1) * PAIR)
            score = scores[j, g, b, 0:count, :].reshape(count // 8, 8, PAIR)
            probs = jnp.exp2(score - peak[g, b][None])
            low = probs.reshape(count, PAIR).astype(BF16)
            grad = grads[j, g, b, 0:count, :].reshape(count // 8, 8, PAIR)
            grad = probs * (grad - dots[g, b][None])
            grad = grad.reshape(count, PAIR).astype(BF16)
            key = key + product(grad, queries[g, at, :], 1, 0)
            value = value + product(low, upstream[g, at, :], 1, 0)
            query = product(keys, grad, 0, 0)
            grad_query[g, b] = query if opening else grad_query[g, b] + query
        key = key * FACTOR
        own[j, g, 0] = key[:TOK]
        own[j, g, 1] = value[:TOK]
        if whole:
            sib_out[j, g, 0] = key[TOK:].astype(BF16)
            sib_out[j, g, 1] = value[TOK:].astype(BF16)

    def to_sibling(j, g):
        at = GROUPS * j + g
        return remote(sib_out.at[j, g], sib_in.at[j, g], sib_send.at[at], sib_recv.at[at], sibling)

    sib = {j: [to_sibling(j, g) for g in range(GROUPS)] for j in (1, 3)}
    def far_copy(i, g, kind):
        at = 4 * i + 2 * g + kind
        return remote(
            far_out.at[i, g, kind], far_in.at[i, g, kind], far_send.at[at], far_recv.at[at],
            chip_at(2 * i - 1, core),
        )

    far = [
        [[far_copy(i, g, kind) for kind in range(2)] for g in range(GROUPS)] for i in range(2)
    ]

    def to_neighbour(i, g, kind):
        side = lax.rem(core + kind, 2)
        return remote(
            near_out.at[i, g, kind], near_in.at[i, g, side],
            near_send.at[4 * i + 2 * g + kind], near_recv.at[4 * i + 2 * g + side],
            chip_at(2 * i - 1, kind),
        )

    near = [
        [[to_neighbour(i, g, kind) for kind in range(2)] for g in range(GROUPS)] for i in range(2)
    ]
    here = [
        remote(
            here_out.at[g], sib_in.at[HERE, g],
            sib_send.at[GROUPS * HERE + g], sib_recv.at[GROUPS * HERE + g], sibling,
        )
        for g in range(GROUPS)
    ]
    swap = [
        remote(
            kv_pair.at[g, pl.ds(TOK, TOK)], kv_own.at[core, g],
            pair_send.at[g], pair_recv.at[g], sibling,
        )
        for g in range(GROUPS)
    ]

    def turn_inputs():
        rows_copy.wait_recv()

        def turn(i, carry):
            at = pl.ds(pl.multiple_of(i * 128, 128), 128)
            rows = jnp.concatenate([rows_in[:, at], rows_sib[:, at]], axis=0)
            rows_turned[at, :] = jnp.transpose(rows)
            return carry

        lax.fori_loop(0, MODEL // 128, turn, 0)

    def near_arrived(g):
        halo[8 * g + 1].wait_recv()
        halo[8 * g + 3].start()
        halo[8 * g + 2].wait_recv()
        halo[8 * g + 4].start()
        halo[8 * g + 5].start()
        halo[8 * g + 6].start()

    def distant_arrived(g):
        halo[8 * g + 3].wait_recv()
        halo[8 * g + 4].wait_recv()
        halo[8 * g + 7].start()

    def send_whole(g):
        second_pass(far_whole, g, False)
        to_sibling(far_whole, g).start()
        for kind in range(2):
            far_out[core, g, kind] = own[far_whole, g, kind].astype(BF16)
            far_copy(core, g, kind).start()

    def send_half(g):
        to_sibling(far_half, g).wait_recv()
        for kind in range(2):
            far_out[1 - core, g, kind] = (
                own[far_half, g, kind] + sib_in[far_half, g, kind].astype(F32)
            ).astype(BF16)
            far_copy(1 - core, g, kind).start()

    def send_near(g):
        for i, j in enumerate((1, 3)):
            sib[j][g].wait_recv()
        for kind in range(2):
            for i, j in enumerate((1, 3)):
                far[i][g][kind].wait_recv()
                near_out[i, g, kind] = (
                    own[j, g, kind] + sib_in[j, g, kind].astype(F32)
                    + far_in[i, g, kind].astype(F32)
                ).astype(BF16)
                near[i][g][kind].start()

    def send_here(g):
        second_pass(HERE, g, False)
        here_out[g, 0] = own[HERE, g, 1 - core].astype(BF16)
        here_out[g, 1] = sib_out[HERE, g, 1 - core]
        here[g].start()

    halo[0].wait_recv()
    make_mask(HERE)
    first_pass(HERE, 0, True)
    halo[8].wait_recv()
    first_pass(HERE, 1, True)

    turn_inputs()
    near_arrived(0)
    halo[5].wait_recv()
    halo[6].wait_recv()
    both(make_mask, 1, 2)
    both(lambda j: first_pass(j, 0, False), 1, 2)
    near_arrived(1)
    halo[13].wait_recv()
    halo[14].wait_recv()
    both(lambda j: first_pass(j, 1, False), 1, 2)

    def distant(g):
        if not g:
            make_mask(far_half, False)
        first_pass(far_half, g, False, False)
        halo[8 * g + 7].wait_recv()
        if not g:
            make_mask(far_whole)
        first_pass(far_whole, g, False)
        merge(g)

    def second_and_send(j, g):
        second_pass(j, g, False)
        to_sibling(j, g).start()

    grad_query[...] = jnp.zeros_like(grad_query)
    distant_arrived(0)
    distant(0)
    distant_arrived(1)
    send_whole(0)
    second_pass(far_half, 0, False, False)
    send_half(0)
    distant(1)
    send_whole(1)
    second_pass(far_half, 1, False, False)
    send_half(1)
    second_and_send(1, 0)
    second_and_send(3, 0)
    second_and_send(1, 1)
    send_near(0)
    second_and_send(3, 1)
    send_here(0)
    send_near(1)
    send_here(1)

    row = [
        [
            remote(
                row_out.at[g, i], row_in.at[g, i],
                row_send.at[(n_x - 1) * g + i], row_recv.at[(n_x - 1) * g + i], row_peers[i],
            )
            for i in range(n_x - 1)
        ]
        for g in range(GROUPS)
    ]
    col = [
        [
            remote(
                col_out.at[g, col_at[i]], col_in.at[g, i],
                col_send.at[(n_outer - 1) * g + i], col_recv.at[(n_outer - 1) * g + i],
                col_peers[i],
            )
            for i in range(n_outer - 1)
        ]
        for g in range(GROUPS)
    ]

    def finish_kv(g):
        here[g].wait_recv()
        for i in range(2):
            for side in range(2):
                remote(
                    near_out.at[i, g, side], near_in.at[i, g, side],
                    near_send.at[4 * i + 2 * g + side], near_recv.at[4 * i + 2 * g + side], right,
                ).wait_recv()
        mine_kv = own[HERE, g, core] + sib_in[HERE, g, 1].astype(F32)
        sib_kv = sib_out[HERE, g, core].astype(F32) + sib_in[HERE, g, 0].astype(F32)
        for i in range(2):
            mine_kv = mine_kv + near_in[i, g, 0].astype(F32)
            sib_kv = sib_kv + near_in[i, g, 1].astype(F32)
        mine_kv = mine_kv.astype(BF16)
        kv_own[core, g] = mine_kv
        kv_pair[g, 0:TOK, :] = mine_kv
        kv_pair[g, TOK:PAIR, :] = sib_kv.astype(BF16)
        swap[g].start()

    def row_first(g):
        whole = product(rows_turned[...], kv_pair[g], 1, 0)
        part[g] = whole.reshape(n_outer, n_x, 16, HEAD)
        for i, s in enumerate(row_order):
            row_out[g, i] = part[g, :, lax.rem(x + s, n_x)].astype(BF16)
            row[g][i].start()

    def row_last(g):
        share = part[g, :, x]
        for i in range(n_x - 1):
            row[g][i].wait_recv()
            share = share + row_in[g, i].astype(F32)
        part[g, :, x] = share
        col_out[g] = share.astype(BF16)
        for copy in col[g]:
            copy.start()

    def col_last(g):
        share = part[g, outer, x]
        for s, copy in enumerate(col[g]):
            copy.wait_recv()
            share = share + col_in[g, s].astype(F32)
        mine[0, g] = share[:8]
        mine[1, g] = share[8:]

    finish_kv(0)
    row_first(0)
    finish_kv(1)
    row_first(1)
    row_last(0)
    row_last(1)

    for g in range(GROUPS):
        for b in range(2):
            rows = jnp.transpose(grad_query[g, b]) * FACTOR
            for m in range(2):
                h = g * PER_GROUP + 2 * b + m
                dq_out[:, h * HEAD : (h + 1) * HEAD] = rows[m * TOK : (m + 1) * TOK].astype(BF16)
    for g in range(GROUPS):
        swap[g].wait_recv()
    kv_rows = jnp.concatenate(
        [kv_own[kind, g] for kind in range(2) for g in range(GROUPS)], axis=1
    )
    dx_out[...] = product(kv_rows, weight[...], 1, 1).astype(BF16)
    others = [to_sibling(far_whole, g) for g in range(GROUPS)] + sib[1] + sib[3]
    by_kind = [copy for group in far + near for kinds in group for copy in kinds]
    for copy in halo + others + by_kind + here + swap + [rows_copy] + sum(row, []):
        copy.wait_send()
    col_last(0)
    col_last(1)

    last = []
    for i, (s, flip, peer) in enumerate(dp_peers):
        copy = remote(
            mine.at[1 - core if flip else core], dp_buf.at[dp, core],
            dp_send.at[i], dp_recv.at[i], peer,
        )
        copy.start()
        last.append(copy)
    dp_buf[dp, core] = mine[core]
    for copy in sum(col, []):
        copy.wait_send()
    for copy in last:
        copy.wait_recv()
    for kind in range(2):
        whole = dp_buf[0, kind]
        for r in range(1, n_dp):
            whole = whole + dp_buf[r, kind]
        for g in range(GROUPS):
            at = kind * GROUPS + g
            gw_ref[:, at * HEAD : (at + 1) * HEAD] = whole[g]
    for copy in last:
        copy.wait_send()


PARTS = 4


def place(*refs):
    count = len(refs) // 2
    sems = refs[-1]
    copies = []
    for source, target in zip(refs[:count], refs[count:-1]):
        rows = source.shape[0] // PARTS if source.shape[0] == TOK else source.shape[0]
        for start in range(0, source.shape[0], rows):
            at = pl.ds(start, rows)
            copies.append(
                pltpu.make_async_copy(source.at[at], target.at[at], sems.at[len(copies)])
            )
    for copy in copies:
        copy.start()
    for copy in copies:
        copy.wait()


def on_device(sizes, queries, inputs, kv_weight, grad_out, segment_ids):
    n_dp, n_outer, n_inner = sizes
    n_x = n_inner // 2
    vmem, dma = pltpu.VMEM, pltpu.SemaphoreType.DMA
    anywhere = pl.BlockSpec(memory_space=pl.ANY)
    inside = pl.BlockSpec(memory_space=pltpu.VMEM)
    tokens = jax.ShapeDtypeStruct((TOK, MODEL), BF16)
    shapes = (tokens, tokens, jax.ShapeDtypeStruct((8, WIDTH), F32))
    results = pl.pallas_call(
        functools.partial(kernel, *sizes),
        out_shape=tuple(pltpu.VMEM(leaf.shape, leaf.dtype) for leaf in shapes),
        in_specs=[anywhere] * 4 + [inside],
        out_specs=(inside,) * 3,
        scratch_shapes=[
            vmem((2, TOK, MODEL), BF16),
            vmem((TOK, MODEL), BF16),
            vmem((TOK, MODEL), BF16),
            vmem((MODEL, PAIR), BF16),
            vmem((MODEL, WIDTH), BF16),
            vmem((GROUPS, PER_GROUP * TOK, HEAD), BF16),
            vmem((GROUPS, PER_GROUP * TOK, HEAD), BF16),
            vmem((SPAN, 2, GROUPS, SENT, HALF), BF16),
            vmem((8, PAIR), F32),
            vmem((SPAN, PAIR, PAIR), F32),
            vmem((SPAN, GROUPS, 2, PAIR, PAIR), F32),
            vmem((SPAN, GROUPS, 2, PAIR, PAIR), F32),
            vmem((GROUPS, 2, 8, PAIR), F32),
            vmem((GROUPS, 2, 8, PAIR), F32),
            vmem((GROUPS, 2, 8, PAIR), F32),
            vmem((GROUPS, 2, HEAD, PAIR), F32),
            vmem((SPAN, GROUPS, 2, TOK, HEAD), F32),
            vmem((SPAN, GROUPS, 2, TOK, HEAD), BF16),
            vmem((SPAN, GROUPS, 2, TOK, HEAD), BF16),
            vmem((GROUPS, 2, TOK, HEAD), BF16),
            vmem((2, GROUPS, 2, TOK, HEAD), BF16),
            vmem((2, GROUPS, 2, TOK, HEAD), BF16),
            vmem((2, GROUPS, 2, TOK, HEAD), BF16),
            vmem((2, GROUPS, 2, TOK, HEAD), BF16),
            vmem((GROUPS, PAIR, HEAD), BF16),
            vmem((2, GROUPS, TOK, HEAD), BF16),
            vmem((GROUPS, n_outer, n_x, 16, HEAD), F32),
            vmem((GROUPS, n_x - 1, n_outer, 16, HEAD), BF16),
            vmem((GROUPS, n_x - 1, n_outer, 16, HEAD), BF16),
            vmem((GROUPS, n_outer, 16, HEAD), BF16),
            vmem((GROUPS, n_outer - 1, 16, HEAD), BF16),
            vmem((2, GROUPS, 8, HEAD), F32),
            vmem((n_dp, 2, GROUPS, 8, HEAD), F32),
            dma((7,)),
            dma((16,)), dma((16,)), dma, dma, dma((10,)), dma((10,)),
            dma((8,)), dma((8,)), dma((8,)), dma((8,)),
            dma((2,)), dma((2,)), dma((2 * (n_x - 1),)), dma((2 * (n_x - 1),)),
            dma((2 * (n_outer - 1),)), dma((2 * (n_outer - 1),)), dma((2 * n_dp - 1,)), dma((2 * n_dp - 1,)),
        ],
        compiler_params=pltpu.CompilerParams(
            collective_id=0, has_side_effects=True, vmem_limit_bytes=56 * 2**20
        ),
    )(queries[0], inputs[0], kv_weight, grad_out[0], segment_ids)
    grad_query, grad_input, grad_weight = pl.pallas_call(
        place,
        out_shape=shapes,
        in_specs=[inside] * 3,
        out_specs=(anywhere,) * 3,
        scratch_shapes=[dma((2 * PARTS + 1,))],
    )(*results)
    return grad_query[None], grad_input[None], grad_weight


def solution(mesh):
    spread = P("dp", ("outer", "inner"), None)
    sizes = (mesh.shape["dp"], mesh.shape["outer"], mesh.shape["inner"])
    return jax.shard_map(
        functools.partial(on_device, sizes),
        mesh=mesh,
        in_specs=(spread, spread, P(), spread, P("dp", ("outer", "inner"))),
        out_specs=(spread, spread, P(("outer", "inner"), None)),
        check_vma=False,
    )
```
